32 devices in a mesh: dp: 4 (over x, core), row: 4 (over z), col: 2 (over y).
Axes of the slice: x: 2, y: 2, z: 4, core: 2. Of those that a mesh axis runs over, the one named last changes fastest.
Arguments:
- tokens: bfloat16 [8, 4, 256, 1472], P(('dp', 'col'), 'row'), may hold values from -6 to 6
- lengths: int32 [8, 4], P(('dp', 'col'), 'row'), may hold values from 32 to 256, as said below
- attn_gain: float32 [1472], replicated, may hold values from 0.1 to 1.9
- ffn_gain: float32 [1472], replicated, may hold values from 0.1 to 1.9
- w_query: bfloat16 [1472, 384], P(None, ('row', 'col')), may hold values from -0.01953125 to 0.01953125
- w_key: bfloat16 [1472, 384], P(None, ('row', 'col')), may hold values from -0.15625 to 0.15625
- w_value: bfloat16 [1472, 384], P(None, ('row', 'col')), may hold values from -0.15625 to 0.15625
- w_attn_out: bfloat16 [384, 1472], P(('row', 'col')), may hold values from -2.5 to 2.5
- rel_bias: float32 [32, 6], replicated, may hold values from -3 to 3
- w_gate: bfloat16 [1472, 3584], P('row', 'col'), may hold values from -0.15625 to 0.15625
- w_up: bfloat16 [1472, 3584], P('row', 'col'), may hold values from -0.15625 to 0.15625
- w_down: bfloat16 [3584, 1472], P('col', 'row'), may hold values from -0.09375 to 0.09375
- out_grad: bfloat16 [8, 4, 256, 1472], P(('dp', 'col'), 'row'), may hold values from -6 to 6
Outputs:
- layer_out: bfloat16 [8, 4, 256, 1472], P(('dp', 'col'), 'row')
- tokens_grad: bfloat16 [8, 4, 256, 1472], P(('dp', 'col'), 'row')
- attn_gain_grad: float32 [1472], P(('row', 'col'))
- ffn_gain_grad: float32 [1472], P(('row', 'col'))
- w_query_grad: float32 [1472, 384], P(None, ('row', 'col'))
- w_key_grad: float32 [1472, 384], P(None, ('row', 'col'))
- w_value_grad: float32 [1472, 384], P(None, ('row', 'col'))
- w_attn_out_grad: float32 [384, 1472], P(('row', 'col'))
- rel_bias_grad: float32 [32, 6], P(('row', 'col'))
- w_gate_grad: float32 [1472, 3584], P('row', 'col')
- w_up_grad: float32 [1472, 3584], P('row', 'col')
- w_down_grad: float32 [3584, 1472], P('col', 'row')
The draws below stay inside these ranges and needn't reach their ends.
Inputs may be any that keep to these rules, and one draw needn't show every extreme that they name: `lengths`: each sequence's real tokens are its first entries; the rest of its 256 slots is padding; in every draw some sequence fills all 256 slots.
All inputs are finite; a program needn't handle non-finite values.
Results may differ from the reference program's by a relative error of at most 0.024.
Values may be sent and summed in bfloat16 or wider, within the bound.
No kernel may reach another device: no remote copies, remote signals or barrier semaphores. Data moves between devices by JAX's collectives and lax.ppermute only.
A program may use at most 192 MiB of HBM per device.

```python
import math
import jax
import jax.numpy as jnp
import numpy as np
from jax import lax

D = 1472
HEADS = 6
DKV = 64
FF = 3584
BUCKETS = 32
MAX_DIST = 128
SEQ = 256
INNER = 384
BATCH = 8
N_ROW = 4


def draw_lengths(key, part):
    lowest = max(1, SEQ // 8)
    drawn = jax.random.randint(key, (BATCH, N_ROW), lowest, SEQ + 1, dtype=jnp.int32)
    chosen = jax.random.randint(jax.random.fold_in(key, 7), (), 0, BATCH * N_ROW, dtype=jnp.int32)
    position = jnp.arange(BATCH * N_ROW, dtype=jnp.int32).reshape(BATCH, N_ROW)
    return jnp.where(position == chosen, SEQ, drawn).astype(jnp.int32)


def level_of(own_key, shape, cuts, smallest, high):
    loudness, own = 1.0, jax.random.fold_in(own_key, 6)
    for dim, parts in cuts:
        draws = jnp.exp(jax.random.uniform(jax.random.fold_in(own, dim), (parts,), jnp.float32, smallest / len(cuts), high / len(cuts)))
        loudness = loudness * jnp.repeat(draws, shape[dim] // parts).reshape([-1 if axis == dim else 1 for axis in range(len(shape))])
    return loudness


def normal_values(own_key, shape, width, bound, split=(), held_as=jnp.bfloat16):
    values = jax.random.normal(own_key, shape, jnp.float32) * width
    if len(split) > 0:
        values = level_of(own_key, shape, split, -0.22, 0.18) * values
    return jnp.clip(values, min=-bound, max=bound).astype(held_as)


def setup_inputs(seed: int = 0) -> dict:
    keys = jax.random.split(jax.random.key(seed), 14)
    tokens = normal_values(keys[0], (BATCH, N_ROW, SEQ, D), 1.0, 6.0, ((0, 8), (1, 4)))
    lengths = draw_lengths(jax.random.fold_in(keys[13], 71), 0)
    attn_gain = jnp.clip(1.0 + 0.18 * jax.random.normal(keys[2], (D,), jnp.float32), 0.1, 1.9)
    ffn_gain = jnp.clip(1.0 + 0.18 * jax.random.normal(keys[3], (D,), jnp.float32), 0.1, 1.9)
    w_query = normal_values(keys[4], (D, INNER), (D * DKV) ** -0.5, 0.01953125, ((1, 8),))
    w_key = normal_values(keys[5], (D, INNER), D ** -0.5, 0.15625, ((1, 8),))
    w_value = normal_values(keys[6], (D, INNER), D ** -0.5, 0.15625, ((1, 8),))
    w_attn_out = normal_values(keys[7], (INNER, D), (max(1, INNER * 4 // SEQ)) ** -0.5, 2.5, ((0, 8),))
    rel_bias = normal_values(keys[8], (BUCKETS, HEADS), 0.5, 3.0, (), jnp.float32)
    w_gate = normal_values(keys[9], (D, FF), D ** -0.5, 0.15625, ((0, 4), (1, 2)))
    w_up = normal_values(keys[10], (D, FF), D ** -0.5, 0.15625, ((0, 4), (1, 2)))
    w_down = normal_values(keys[11], (FF, D), FF ** -0.5, 0.09375, ((0, 2), (1, 4)))
    out_grad = normal_values(keys[12], (BATCH, N_ROW, SEQ, D), 1.0, 6.0, ((0, 8), (1, 4)))
    return {"tokens": tokens, "lengths": lengths, "attn_gain": attn_gain, "ffn_gain": ffn_gain, "w_query": w_query, "w_key": w_key, "w_value": w_value, "w_attn_out": w_attn_out, "rel_bias": rel_bias, "w_gate": w_gate, "w_up": w_up, "w_down": w_down, "out_grad": out_grad}


@jax.custom_vjp
def low(v):
    return lax.optimization_barrier(v.astype(jnp.bfloat16)).astype(jnp.float32)

@jax.custom_vjp
def low_back(v):
    return v

def low_keep(v):
    return (low(v), None)

def low_pass(kept, grad):
    return (grad,)

def back_keep(v):
    return (v, None)

def back_low(kept, grad):
    return (low(grad),)
low.defvjp(low_keep, low_pass)
low_back.defvjp(back_keep, back_low)
EPSILON = 1e-06
HIGHEST = lax.Precision.HIGHEST

def bucket_table(length):
    offsets = np.arange(-(length - 1), length)
    half_count = BUCKETS // 2
    exact_count = half_count // 2
    upper_half = (offsets > 0).astype(np.int64) * half_count
    distance = np.abs(offsets)
    safe_distance = np.maximum(distance, 1)
    spread = np.log(safe_distance / exact_count) / np.log(MAX_DIST / exact_count) * (half_count - exact_count)
    far_bucket = np.minimum(exact_count + np.floor(np.maximum(spread, 0.0)).astype(np.int64), half_count - 1)
    return (upper_half + np.where(distance < exact_count, distance, far_bucket)).astype(np.int32)

def position_bias(bias_table, length):
    buckets = jnp.asarray(bucket_table(length))
    onehot = (buckets[None, :] == jnp.arange(BUCKETS, dtype=jnp.int32)[:, None]).astype(bias_table.dtype)
    per_offset = jnp.dot(jnp.transpose(bias_table), onehot, precision=HIGHEST)
    offset_index = np.arange(length)[None, :] - np.arange(length)[:, None] + length - 1
    return jnp.take(per_offset, jnp.asarray(offset_index.astype(np.int32)), axis=1)

def attend(normed, length, w_query, w_key, w_value, w_out, position_terms):
    seq_len = normed.shape[0]

    def project(weight):
        product = low(low_back(jnp.dot(normed, weight, precision=HIGHEST)))
        return jnp.transpose(product.reshape(seq_len, HEADS, DKV), (1, 0, 2))
    query_heads = project(w_query)
    key_heads = project(w_key)
    value_heads = project(w_value)
    scores = jnp.einsum('hid,hjd->hij', query_heads, key_heads, precision=HIGHEST) + position_terms
    key_valid = jnp.arange(seq_len, dtype=jnp.int32) < length
    scores = low_back(jnp.where(key_valid[None, None, :], scores, -1e+30))
    row_max = lax.optimization_barrier(jnp.max(scores, axis=2, keepdims=True))
    weights_exp = jnp.exp(scores - row_max)
    probabilities = weights_exp / lax.optimization_barrier(jnp.sum(weights_exp, axis=2, keepdims=True))
    context = jnp.einsum('hij,hjd->hid', low(probabilities), value_heads, precision=HIGHEST)
    context = low(low_back(jnp.transpose(context, (1, 0, 2)).reshape(seq_len, HEADS * DKV)))
    return low_back(jnp.dot(context, w_out, precision=HIGHEST))

def layer(tokens, lengths, params):
    attn_gain, ffn_gain, w_query, w_key, w_value, w_out, bias_table, w_gate, w_up, w_down = params
    position_terms = position_bias(bias_table, tokens.shape[1])
    inverse_one = lax.rsqrt(lax.optimization_barrier(jnp.mean(tokens * tokens, axis=-1, keepdims=True)) + EPSILON)
    normed_one = low(tokens * inverse_one * attn_gain)

    def attend_one(seq_item):
        return attend(seq_item[0], seq_item[1], w_query, w_key, w_value, w_out, position_terms)
    residual = tokens + lax.map(jax.checkpoint(attend_one), (normed_one, lengths))
    inverse_two = lax.rsqrt(lax.optimization_barrier(jnp.mean(residual * residual, axis=-1, keepdims=True)) + EPSILON)
    normed_two = low(residual * inverse_two * ffn_gain)
    gate_pre = low_back(jnp.einsum('bld,df->blf', normed_two, w_gate, precision=HIGHEST))
    up_pre = low_back(jnp.einsum('bld,df->blf', normed_two, w_up, precision=HIGHEST))
    gated_hidden = low(jax.nn.gelu(gate_pre, approximate=True) * up_pre)
    branch = low_back(jnp.einsum('blf,fd->bld', gated_hidden, w_down, precision=HIGHEST))
    return residual + branch

def reference(tokens, lengths, attn_gain, ffn_gain, w_query, w_key, w_value, w_attn_out, rel_bias, w_gate, w_up, w_down, out_grad):
    params = tuple((weight.astype(jnp.float32) for weight in (attn_gain, ffn_gain, w_query, w_key, w_value, w_attn_out, rel_bias, w_gate, w_up, w_down)))
    seq_total = BATCH * N_ROW
    group_size = math.gcd(seq_total, max(1, 4096 // SEQ))
    blocks = seq_total // group_size
    inputs = tokens.astype(jnp.float32).reshape(blocks, group_size, SEQ, D)
    cotangents = out_grad.astype(jnp.float32).reshape(blocks, group_size, SEQ, D)
    block_lengths = lengths.reshape(blocks, group_size)

    def one_block(totals, block_item):
        block_tokens, block_lens, block_cot = block_item
        outputs, pullback = jax.vjp(lambda inner_tokens, inner_params: layer(inner_tokens, block_lens, inner_params), block_tokens, params)
        token_grads, param_grads = pullback(block_cot)
        totals = jax.tree.map(jnp.add, totals, param_grads)
        return (totals, (outputs.astype(jnp.bfloat16), token_grads.astype(jnp.bfloat16)))
    totals, (outputs, token_grads) = lax.scan(one_block, jax.tree.map(jnp.zeros_like, params), (inputs, block_lengths, cotangents))
    full_shape = (BATCH, N_ROW, SEQ, D)
    return (outputs.reshape(full_shape), token_grads.reshape(full_shape), totals[0], totals[1], totals[2], totals[3], totals[4], totals[5], totals[6], totals[7], totals[8], totals[9])
```

```python
import functools

import jax
import jax.numpy as jnp
import numpy as np
from jax import lax
from jax.experimental import pallas as pl
from jax.experimental.pallas import tpu as pltpu
from jax.sharding import PartitionSpec as P

HEADS = 6
DKV = 64
BUCKETS = 32
MAX_DIST = 128
EPSILON = 1e-06
HIGHEST = lax.Precision.HIGHEST
F32 = jnp.float32
BF16 = jnp.bfloat16
VMEM_LIMIT = 56 * 1024 * 1024


def bucket_table(length):
    offsets = np.arange(-(length - 1), length)
    half_count = BUCKETS // 2
    exact_count = half_count // 2
    upper_half = (offsets > 0).astype(np.int64) * half_count
    distance = np.abs(offsets)
    safe_distance = np.maximum(distance, 1)
    spread = (
        np.log(safe_distance / exact_count)
        / np.log(MAX_DIST / exact_count)
        * (half_count - exact_count)
    )
    far_bucket = np.minimum(
        exact_count + np.floor(np.maximum(spread, 0.0)).astype(np.int64), half_count - 1
    )
    return (upper_half + np.where(distance < exact_count, distance, far_bucket)).astype(np.int32)


def bucket_onehot(length):
    onehot = np.zeros((BUCKETS, 2 * length), np.float32)
    onehot[bucket_table(length), np.arange(2 * length - 1)] = 1.0
    return onehot


def dot(a, b, dims=((1,), (0,)), precision=None):
    return lax.dot_general(a, b, (dims, ((), ())), precision=precision, preferred_element_type=F32)


NN = ((1,), (0,))
NT = ((1,), (1,))
TN = ((0,), (0,))


def attention_forward_kernel(
    where_ref, x_ref, gain_one_ref, gain_two_ref, bias_ref, onehot_ref, *rest, n_row, shard
):
    units = rest[:8]
    (weights_ref, residual_ref, normed_one_ref, normed_two_ref, qkv_ref, context_ref, probs_ref, sems) = rest[8:]
    length, core, x_bit, y_bit, z_index = (where_ref[k] for k in range(5))
    inner = HEADS * DKV
    seq = x_ref.shape[0]
    copies = []
    for unit in range(8):
        far, one, two = unit >> 2, (unit >> 1) & 1, unit & 1
        own_core = core ^ far
        x_shift = jnp.where(own_core == 0, one, two)
        y_shift = jnp.where(own_core == 0, two, one)
        matrix = (x_bit ^ x_shift) * 2 + own_core
        side = y_bit ^ y_shift
        for k in range(n_row):
            z_from = lax.rem(z_index - k + n_row, n_row)
            start = pl.multiple_of(matrix * inner + (z_from * 2 + side) * shard, 16)
            copy = pltpu.make_async_copy(
                units[unit].at[pl.ds(k * shard, shard)],
                weights_ref.at[pl.ds(start, shard)],
                sems.at[unit, k],
            )
            copy.start()
            copies.append(copy)
    x = x_ref[...].astype(F32)
    inverse = lax.rsqrt(jnp.mean(x * x, axis=-1, keepdims=True) + EPSILON)
    normed = (x * inverse * gain_one_ref[...]).astype(BF16)
    normed_one_ref[...] = normed
    per_offset = dot(bias_ref[...], onehot_ref[...], NN, HIGHEST)
    key_valid = lax.broadcasted_iota(jnp.int32, (seq, seq), 1) < length
    for copy in copies:
        copy.wait()
    queries, keys, values = (
        dot(normed, weights_ref[m * inner : (m + 1) * inner, :], NT).astype(BF16) for m in range(3)
    )
    for m, part in enumerate((queries, keys, values)):
        qkv_ref[m] = part
    contexts = []
    for h in range(HEADS):
        cols = slice(h * DKV, (h + 1) * DKV)
        row = jnp.broadcast_to(per_offset[h : h + 1, :], (seq, 2 * seq))
        bias = pltpu.roll(row, seq + 1, 1, stride=1, stride_axis=0)[:, :seq]
        scores = jnp.where(key_valid, dot(queries[:, cols], keys[:, cols], NT) + bias, -1e30)
        weights = jnp.exp(scores - jnp.max(scores, axis=1, keepdims=True))
        probs = weights / jnp.sum(weights, axis=1, keepdims=True)
        probs_ref[h] = probs
        contexts.append(dot(probs.astype(BF16), values[:, cols], NN))
    context = jnp.concatenate(contexts, axis=1).astype(BF16)
    context_ref[...] = context
    residual = x + dot(context, weights_ref[3 * inner :, :], NN)
    residual_ref[...] = residual
    inverse_two = lax.rsqrt(jnp.mean(residual * residual, axis=-1, keepdims=True) + EPSILON)
    normed_two_ref[...] = (residual * inverse_two * gain_two_ref[...]).astype(BF16)


def attention_forward(where, x, gain_one, gain_two, bias, onehot, units, n_row):
    seq, width = x.shape
    inner = HEADS * DKV
    vmem = pl.BlockSpec(memory_space=pltpu.VMEM)
    return pl.pallas_call(
        functools.partial(attention_forward_kernel, n_row=n_row, shard=inner // (2 * n_row)),
        out_shape=(
            jax.ShapeDtypeStruct((4 * inner, width), BF16),
            jax.ShapeDtypeStruct((seq, width), F32),
            jax.ShapeDtypeStruct((seq, width), BF16),
            jax.ShapeDtypeStruct((seq, width), BF16),
            jax.ShapeDtypeStruct((3, seq, inner), BF16),
            jax.ShapeDtypeStruct((seq, inner), BF16),
            jax.ShapeDtypeStruct((HEADS, seq, seq), F32),
        ),
        in_specs=[pl.BlockSpec(memory_space=pltpu.SMEM)]
        + [vmem] * 5
        + [pl.BlockSpec(memory_space=pl.ANY)] * 8,
        out_specs=(vmem,) * 7,
        scratch_shapes=[pltpu.SemaphoreType.DMA((8, n_row))],
        compiler_params=pltpu.CompilerParams(vmem_limit_bytes=VMEM_LIMIT),
        cost_estimate=pl.CostEstimate(flops=2_000_000_000, bytes_accessed=16_000_000, transcendentals=400_000),
        name="attention_forward",
    )(where, x, gain_one, gain_two, bias, onehot, *units)


def attention_backward_kernel(
    where_ref,
    x_ref,
    gain_one_ref,
    gain_two_ref,
    onehot_ref,
    out_grad_ref,
    part_a_ref,
    part_b_ref,
    part_c_ref,
    weights_ref,
    residual_ref,
    normed_one_ref,
    qkv_ref,
    context_ref,
    probs_ref,
    near_ref,
    far_ref,
    tokens_grad_ref,
    gains_ref,
    table_ref,
    *,
    n_row,
    shard,
):
    _, core, x_bit, y_bit, z_index = (where_ref[k] for k in range(5))
    inner = HEADS * DKV
    seq = x_ref.shape[0]

    def store_weight_grad(matrix, grad):
        grad = grad.astype(BF16)
        target_core = matrix & 1
        x_shift = (matrix >> 1) ^ x_bit
        for side in range(2):
            y_shift = side ^ y_bit
            if target_core == 0:
                unit = x_shift * 2 + y_shift
            else:
                unit = y_shift * 2 + x_shift
            for z in range(n_row):
                slot = unit * n_row + lax.rem(z - z_index + n_row, n_row)
                start = (z * 2 + side) * shard
                block = grad[start : start + shard, :]

                @pl.when(core == target_core)
                def _():
                    near_ref[slot] = block

                @pl.when(core != target_core)
                def _():
                    far_ref[slot] = block

    residual = residual_ref[...]
    grad_normed = (
        part_a_ref[...].astype(F32) + part_b_ref[...].astype(F32) + part_c_ref[...].astype(F32)
    )
    inverse_two = lax.rsqrt(jnp.mean(residual * residual, axis=-1, keepdims=True) + EPSILON)
    gained = grad_normed * gain_two_ref[...]
    gains_ref[1:2, :] = jnp.sum(grad_normed * residual * inverse_two, axis=0, keepdims=True)
    grad_residual = (
        out_grad_ref[...].astype(F32)
        + inverse_two * gained
        - residual
        * (inverse_two * inverse_two * inverse_two * jnp.mean(gained * residual, axis=-1, keepdims=True))
    )
    grad_attended = grad_residual.astype(BF16)
    store_weight_grad(3, dot(context_ref[...], grad_attended, TN))
    grad_context = dot(grad_attended, weights_ref[3 * inner :, :], NT).astype(BF16)
    flip = (
        lax.broadcasted_iota(jnp.int32, (seq, seq), 0)
        + lax.broadcasted_iota(jnp.int32, (seq, seq), 1)
        == seq - 1
    ).astype(BF16)
    zero_half = jnp.zeros((seq, seq), F32)
    grads = ([], [], [])
    diagonals = []
    for h in range(HEADS):
        cols = slice(h * DKV, (h + 1) * DKV)
        probs = probs_ref[h]
        grad_head = grad_context[:, cols]
        grads[2].append(dot(probs.astype(BF16), grad_head, TN))
        grad_probs = dot(grad_head, qkv_ref[2, :, cols], NT)
        grad_scores = (
            probs * (grad_probs - jnp.sum(probs * grad_probs, axis=1, keepdims=True))
        ).astype(BF16)
        grads[0].append(dot(grad_scores, qkv_ref[1, :, cols], NN))
        grads[1].append(dot(grad_scores, qkv_ref[0, :, cols], TN))
        flipped = jnp.concatenate((dot(flip, grad_scores, NN), zero_half), axis=1)
        rolled = pltpu.roll(flipped, 0, 1, stride=1, stride_axis=0)
        diagonals.append(jnp.sum(rolled, axis=0, keepdims=True))
    diagonals.append(jnp.zeros((8 - HEADS, 2 * seq), F32))
    table_ref[...] = dot(jnp.concatenate(diagonals, axis=0), onehot_ref[...], NT, HIGHEST)
    grads = [jnp.concatenate(parts, axis=1).astype(BF16) for parts in grads]
    normed_one = normed_one_ref[...]
    grad_normed_one = None
    for m in range(3):
        store_weight_grad(m, dot(grads[m], normed_one, TN))
        part = dot(grads[m], weights_ref[m * inner : (m + 1) * inner, :], NN)
        grad_normed_one = part if grad_normed_one is None else grad_normed_one + part
    x = x_ref[...].astype(F32)
    inverse_one = lax.rsqrt(jnp.mean(x * x, axis=-1, keepdims=True) + EPSILON)
    gained_one = grad_normed_one * gain_one_ref[...]
    gains_ref[0:1, :] = jnp.sum(grad_normed_one * x * inverse_one, axis=0, keepdims=True)
    tokens_grad_ref[...] = (
        grad_residual
        + inverse_one * gained_one
        - x * (inverse_one * inverse_one * inverse_one * jnp.mean(gained_one * x, axis=-1, keepdims=True))
    ).astype(BF16)


def attention_backward(where, x, gain_one, gain_two, onehot, out_grad, parts, saved, n_row):
    seq, width = x.shape
    inner = HEADS * DKV
    shard = inner // (2 * n_row)
    vmem = pl.BlockSpec(memory_space=pltpu.VMEM)
    return pl.pallas_call(
        functools.partial(attention_backward_kernel, n_row=n_row, shard=shard),
        out_shape=(
            jax.ShapeDtypeStruct((4 * n_row, shard, width), BF16),
            jax.ShapeDtypeStruct((4 * n_row, shard, width), BF16),
            jax.ShapeDtypeStruct((seq, width), BF16),
            jax.ShapeDtypeStruct((2, width), F32),
            jax.ShapeDtypeStruct((8, BUCKETS), F32),
        ),
        in_specs=[pl.BlockSpec(memory_space=pltpu.SMEM)] + [vmem] * 14,
        out_specs=(vmem,) * 5,
        compiler_params=pltpu.CompilerParams(vmem_limit_bytes=VMEM_LIMIT),
        cost_estimate=pl.CostEstimate(flops=4_000_000_000, bytes_accessed=20_000_000, transcendentals=1000),
        name="attention_backward",
    )(where, x, gain_one, gain_two, onehot, out_grad, *parts, *saved)


GELU_SCALE = float(np.sqrt(2.0 / np.pi))


def feed_forward_kernel(*refs, count):
    normed_refs, grad_refs = refs[:count], refs[count : 2 * count]
    weights_ref = refs[2 * count]
    outs = refs[2 * count + 1 :]
    gated_refs, hidden_refs, back_refs = outs[:count], outs[count : 2 * count], outs[2 * count :]
    hidden = weights_ref.shape[2]
    for b in range(count):
        normed = normed_refs[b][...]
        gate = dot(normed, weights_ref[0], NN)
        up = dot(normed, weights_ref[1], NN)
        grad_gated = dot(grad_refs[b][...], weights_ref[2], NN)
        square = gate * gate
        tanh = jnp.tanh(GELU_SCALE * gate * (1.0 + 0.044715 * square))
        half = 0.5 * (1.0 + tanh)
        gelu = gate * half
        slope = half + (0.5 * GELU_SCALE) * gate * (1.0 - tanh * tanh) * (1.0 + 3 * 0.044715 * square)
        gated_refs[b][...] = (gelu * up).astype(BF16)
        grad_gate = (grad_gated * up * slope).astype(BF16)
        grad_up = (grad_gated * gelu).astype(BF16)
        hidden_refs[b][:, :hidden] = grad_gate
        hidden_refs[b][:, hidden:] = grad_up
        back_refs[b][...] = (
            dot(grad_gate, weights_ref[0], NT) + dot(grad_up, weights_ref[1], NT)
        ).astype(BF16)


def feed_forward(normed, grads, weights):
    count = len(normed)
    rows, width = normed[0].shape
    hidden = weights.shape[2]
    vmem = pl.BlockSpec(memory_space=pltpu.VMEM)
    outs = pl.pallas_call(
        functools.partial(feed_forward_kernel, count=count),
        out_shape=[jax.ShapeDtypeStruct((rows, hidden), BF16)] * count
        + [jax.ShapeDtypeStruct((rows, 2 * hidden), BF16)] * count
        + [jax.ShapeDtypeStruct((rows, width), BF16)] * count,
        in_specs=[vmem] * (2 * count + 1),
        out_specs=[vmem] * (3 * count),
        compiler_params=pltpu.CompilerParams(vmem_limit_bytes=VMEM_LIMIT),
        cost_estimate=pl.CostEstimate(
            flops=10 * count * rows * width * hidden,
            bytes_accessed=2 * (3 * width * hidden + count * rows * (3 * width + 3 * hidden)),
            transcendentals=count * rows * hidden,
        ),
        name="feed_forward",
    )(*normed, *grads, weights)
    return outs[:count], outs[count : 2 * count], outs[2 * count :]


def local(
    sizes,
    tokens,
    lengths,
    attn_gain,
    ffn_gain,
    w_query,
    w_key,
    w_value,
    w_attn_out,
    rel_bias,
    w_gate,
    w_up,
    w_down,
    out_grad,
):
    n_dp, n_row, n_col = sizes
    lo = n_col // 2
    seq, width = tokens.shape[2], tokens.shape[3]
    inner = HEADS * DKV
    dp, row, col = lax.axis_index("dp"), lax.axis_index("row"), lax.axis_index("col")
    core, x_bit, y_bit, quarter = dp % 2, (dp // 2) % 2, col // lo, dp % 4

    first, second = [], []
    for d in range(n_dp):
        for c in range(n_col):
            here, over_x, over_y = d * n_col + c, (d ^ 2) * n_col + c, d * n_col + (c + lo) % n_col
            first.append((here, over_x if d % 2 == 0 else over_y))
            second.append((here, over_y if d % 2 == 0 else over_x))
    swap = [(d, d ^ 1) for d in range(n_dp)]

    def send_first(a):
        return lax.ppermute(a, ("dp", "col"), first)

    def send_second(a):
        return lax.ppermute(a, ("dp", "col"), second)

    def send_core(a):
        return lax.ppermute(a, "dp", swap)

    def after(a, *others):
        return lax.optimization_barrier((a, *others))[0]

    def spread(block):
        one = send_first(block)
        two = send_second(block)
        three = send_second(one)
        near = [block, two, one, three]
        return near + [send_core(a) for a in near]

    def add(a, b):
        return (a.astype(F32) + b.astype(F32)).astype(BF16)

    def collect(blocks):
        near = {p: add(blocks[p], send_core(blocks[4 + p])) for p in (3, 1, 2, 0)}
        from_three = send_second(near[3])
        from_one = send_second(near[1])
        from_two = send_first(add(near[2], from_three))
        return near[0], from_one, from_two

    def whole_cols(a, axis):
        return lax.all_gather(a, "col", axis=axis, tiled=True) if lo > 1 else a

    x = tokens.reshape(seq, width)
    grad = out_grad.reshape(seq, width)
    onehot = jnp.asarray(bucket_onehot(seq))
    where = jnp.stack(
        (lengths.reshape(()), core, x_bit, y_bit, row, quarter, quarter, quarter)
    ).astype(jnp.int32)
    gain_one, gain_two = attn_gain.reshape(1, width), ffn_gain.reshape(1, width)
    bias = jnp.pad(jnp.transpose(rel_bias), ((0, 8 - HEADS), (0, 0)))

    shard = inner // (2 * n_row)
    proj = jnp.where(quarter == 0, w_query, jnp.where(quarter == 1, w_key, w_value))
    own = jnp.where(quarter == 3, w_attn_out, jnp.transpose(proj))
    if lo > 1:
        own = lax.dynamic_slice_in_dim(whole_cols(own, 0), y_bit * shard, shard, 0)
    unit = jnp.concatenate(
        [own]
        + [lax.ppermute(own, "row", [(i, (i + k) % n_row) for i in range(n_row)]) for k in range(1, n_row)],
        axis=0,
    )
    units = spread(unit)

    hidden = w_gate.shape[1] * lo // 4
    start = quarter * hidden + (y_bit * 4 * hidden if lo > 1 else 0)
    ffn_own = jnp.stack(
        (
            lax.dynamic_slice_in_dim(whole_cols(w_gate, 1), start, hidden, 1),
            lax.dynamic_slice_in_dim(whole_cols(w_up, 1), start, hidden, 1),
            jnp.transpose(lax.dynamic_slice_in_dim(whole_cols(w_down, 0), start, hidden, 0)),
        )
    )
    ffn_own = after(ffn_own, unit)
    ffn_weights = lax.all_gather(ffn_own, "row", axis=1, tiled=True)

    grads = spread(grad)
    weights, residual, normed_one, normed_two, qkv, context, probs = attention_forward(
        where, x, gain_one, gain_two, bias, onehot, units, n_row
    )
    normed = spread(normed_two)

    gated, hidden_grads, back = [None] * 8, [None] * 8, [None] * 8
    for near in (0, 2, 1, 3):
        pair = (near, near + 4)
        got = feed_forward([normed[p] for p in pair], [grads[p] for p in pair], ffn_weights)
        for i, p in enumerate(pair):
            gated[p], hidden_grads[p], back[p] = got[0][i], got[1][i], got[2][i]
    back_parts = collect(back)

    branch = [dot(g, ffn_weights[2], NT).astype(BF16) for g in gated]
    branch_parts = collect(branch)
    layer_out = (
        (residual + sum(p.astype(F32) for p in branch_parts)).astype(BF16).reshape(tokens.shape)
    )

    all_normed, all_grads = jnp.concatenate(normed, 0), jnp.concatenate(grads, 0)
    all_gated, all_hidden = jnp.concatenate(gated, 0), jnp.concatenate(hidden_grads, 0)
    down_grad = dot(all_grads, all_gated, TN).astype(BF16)
    in_grad = dot(all_normed, all_hidden, TN).astype(BF16)
    ffn_grads = jnp.stack((in_grad[:, :hidden], in_grad[:, hidden:], down_grad))
    ffn_grads = lax.psum_scatter(ffn_grads, "row", scatter_dimension=1, tiled=True)

    near_grads, far_grads, tokens_grad, gain_grads, table_grad = attention_backward(
        where,
        x,
        gain_one,
        gain_two,
        onehot,
        grad,
        back_parts,
        (weights, residual, normed_one, qkv, context, probs),
        n_row,
    )
    summed = add(near_grads, send_core(far_grads))
    quad = [summed[p * n_row : (p + 1) * n_row] for p in range(4)]
    from_three = send_second(quad[3])
    from_one = send_second(quad[1])
    from_two = send_first(add(quad[2], from_three))
    mine = (
        quad[0].astype(F32) + from_one.astype(F32) + from_two.astype(F32)
    ).astype(BF16)
    attn_grad = mine[0].astype(F32)
    for k in range(1, n_row):
        attn_grad = attn_grad + lax.ppermute(
            mine[k], "row", [(i, (i + k) % n_row) for i in range(n_row)]
        ).astype(F32)
    attn_grad = attn_grad.astype(BF16)

    def gather_quarters(a):
        if n_dp == 4:
            return lax.all_gather(a, "dp", axis=0)
        placed = lax.dynamic_update_index_in_dim(jnp.zeros((4, *a.shape), a.dtype), a, quarter, 0)
        return lax.psum(placed, "dp")

    def own_cols(a):
        placed = jnp.zeros((n_col, *a.shape[1:]), a.dtype)
        placed = lax.dynamic_update_slice_in_dim(placed, a, y_bit * lo, 0)
        return lax.psum_scatter(placed, "col", scatter_dimension=0, tiled=False)

    attn_grads = gather_quarters(attn_grad)
    ffn_grads = gather_quarters(ffn_grads)
    ffn_grads = jnp.transpose(ffn_grads, (1, 2, 0, 3)).reshape(3, width // n_row, 4 * hidden)
    if lo > 1:
        piece = shard // lo
        attn_grads = own_cols(jnp.transpose(attn_grads.reshape(4, lo, piece, width), (1, 0, 2, 3)))
        piece = 4 * hidden // lo
        ffn_grads = own_cols(
            jnp.transpose(ffn_grads.reshape(3, width // n_row, lo, piece), (2, 0, 1, 3))
        )
    attn_grads = attn_grads.astype(F32)
    ffn_grads = ffn_grads.astype(F32)

    small = jnp.concatenate(
        (gain_grads, jnp.pad(table_grad.reshape(1, 8 * BUCKETS), ((0, 0), (0, width - 8 * BUCKETS)))), 0
    )
    small = lax.psum(small, ("dp", "row", "col"))
    place = row * n_col + col
    gain_cols, table_rows = width // (n_row * n_col), BUCKETS // (n_row * n_col)
    gain_grads = lax.dynamic_slice_in_dim(small[:2], place * gain_cols, gain_cols, 1)
    table_grad = jnp.transpose(small[2, : 8 * BUCKETS].reshape(8, BUCKETS)[:HEADS])
    table_grad = lax.dynamic_slice_in_dim(table_grad, place * table_rows, table_rows, 0)
    return (
        layer_out,
        tokens_grad.reshape(tokens.shape),
        gain_grads[0],
        gain_grads[1],
        jnp.transpose(attn_grads[0]),
        jnp.transpose(attn_grads[1]),
        jnp.transpose(attn_grads[2]),
        attn_grads[3],
        table_grad,
        ffn_grads[0],
        ffn_grads[1],
        jnp.transpose(ffn_grads[2]),
    )


def solution(mesh):
    sizes = tuple(mesh.shape[name] for name in ("dp", "row", "col"))
    placed = (
        P(("dp", "col"), "row", None, None),
        P(("dp", "col"), "row"),
        P(),
        P(),
        P(None, ("row", "col")),
        P(None, ("row", "col")),
        P(None, ("row", "col")),
        P(("row", "col"), None),
        P(),
        P("row", "col"),
        P("row", "col"),
        P("col", "row"),
        P(("dp", "col"), "row", None, None),
    )
    return jax.shard_map(
        functools.partial(local, sizes),
        mesh=mesh,
        in_specs=placed,
        out_specs=(
            P(("dp", "col"), "row", None, None),
            P(("dp", "col"), "row", None, None),
            P(("row", "col")),
            P(("row", "col")),
            P(None, ("row", "col")),
            P(None, ("row", "col")),
            P(None, ("row", "col")),
            P(("row", "col"), None),
            P(("row", "col"), None),
            P("row", "col"),
            P("row", "col"),
            P("col", "row"),
        ),
        check_vma=False,
    )
```

```python
import functools

import jax
import jax.numpy as jnp
import numpy as np
from jax import lax
from jax.experimental import pallas as pl
from jax.experimental.pallas import tpu as pltpu
from jax.sharding import PartitionSpec as P

HEADS = 6
DKV = 64
BUCKETS = 32
MAX_DIST = 128
EPSILON = 1e-06
HIGHEST = lax.Precision.HIGHEST
F32 = jnp.float32
BF16 = jnp.bfloat16
VMEM_LIMIT = 56 * 1024 * 1024


def bucket_table(length):
    offsets = np.arange(-(length - 1), length)
    half_count = BUCKETS // 2
    exact_count = half_count // 2
    upper_half = (offsets > 0).astype(np.int64) * half_count
    distance = np.abs(offsets)
    safe_distance = np.maximum(distance, 1)
    spread = (
        np.log(safe_distance / exact_count)
        / np.log(MAX_DIST / exact_count)
        * (half_count - exact_count)
    )
    far_bucket = np.minimum(
        exact_count + np.floor(np.maximum(spread, 0.0)).astype(np.int64), half_count - 1
    )
    return (upper_half + np.where(distance < exact_count, distance, far_bucket)).astype(np.int32)


def bucket_onehot(length):
    onehot = np.zeros((BUCKETS, 2 * length), np.float32)
    offsets = np.arange(-(length - 1), length)
    onehot[bucket_table(length), (-offsets) % (2 * length)] = 1.0
    return onehot


def dot(a, b, dims, precision=None):
    return lax.dot_general(a, b, (dims, ((), ())), precision=precision, preferred_element_type=F32)


NN = ((1,), (0,))
NT = ((1,), (1,))
TN = ((0,), (0,))


def vmem_spec():
    return pl.BlockSpec(memory_space=pltpu.VMEM)


def any_spec():
    return pl.BlockSpec(memory_space=pl.ANY)


def wide(column, width):
    return jnp.concatenate([column] * (width // column.shape[1]), axis=1)


def attention_forward_kernel(
    where_ref, x_ref, gain_one_ref, gain_two_ref, bias_ref, onehot_ref, *rest, n_row, shard
):
    units = rest[:8]
    (weights_ref, residual_ref, normed_one_ref, normed_two_ref, qkv_ref, context_ref, probs_ref, sems) = rest[8:]
    length, core, x_bit, y_bit, z_index = (where_ref[k] for k in range(5))
    inner = HEADS * DKV
    seq = x_ref.shape[1]
    copies = []
    for unit in range(8):
        far, one, two = unit >> 2, (unit >> 1) & 1, unit & 1
        own_core = core ^ far
        x_shift = jnp.where(own_core == 0, one, two)
        y_shift = jnp.where(own_core == 0, two, one)
        matrix = (x_bit ^ x_shift) * 2 + own_core
        side = y_bit ^ y_shift
        for k in range(n_row):
            z_from = lax.rem(z_index - k + n_row, n_row)
            start = pl.multiple_of(matrix * inner + (z_from * 2 + side) * shard, 16)
            copy = pltpu.make_async_copy(
                units[unit].at[pl.ds(k * shard, shard)],
                weights_ref.at[pl.ds(start, shard)],
                sems.at[unit, k],
            )
            copy.start()
            copies.append(copy)
    x = x_ref[...].astype(F32)
    inverse = lax.rsqrt(jnp.mean(x * x, axis=0, keepdims=True) + EPSILON)
    normed = (x * inverse * wide(gain_one_ref[...], seq)).astype(BF16)
    normed_one_ref[...] = normed
    per_offset = dot(bias_ref[...], onehot_ref[...], NN, HIGHEST)
    key_valid = lax.broadcasted_iota(jnp.int32, (seq, seq), 0) < length
    for copy in copies:
        copy.wait()
    for m in range(3):
        qkv_ref[m] = dot(weights_ref[m * inner : (m + 1) * inner, :], normed, NN).astype(BF16)
    for h in range(HEADS):
        rows = slice(h * DKV, (h + 1) * DKV)
        row = jnp.broadcast_to(per_offset[h : h + 1, :], (seq, 2 * seq))
        bias = pltpu.roll(row, 0, 1, stride=1, stride_axis=0)[:, :seq]
        scores = dot(qkv_ref[1, rows, :], qkv_ref[0, rows, :], TN) + bias
        scores = jnp.where(key_valid, scores, -1e30)
        weights = jnp.exp(scores - jnp.max(scores, axis=0, keepdims=True))
        probs = weights / jnp.sum(weights, axis=0, keepdims=True)
        probs_ref[h] = probs
        context_ref[rows, :] = dot(qkv_ref[2, rows, :], probs.astype(BF16), NN).astype(BF16)
    residual = x + dot(weights_ref[3 * inner :, :], context_ref[...], TN)
    residual_ref[...] = residual
    inverse_two = lax.rsqrt(jnp.mean(residual * residual, axis=0, keepdims=True) + EPSILON)
    normed_two_ref[...] = (residual * inverse_two * wide(gain_two_ref[...], seq)).astype(BF16)


def attention_forward(where, x, gain_one, gain_two, bias, onehot, units, n_row):
    width, seq = x.shape
    inner = HEADS * DKV
    return pl.pallas_call(
        functools.partial(attention_forward_kernel, n_row=n_row, shard=inner // (2 * n_row)),
        out_shape=(
            jax.ShapeDtypeStruct((4 * inner, width), BF16),
            jax.ShapeDtypeStruct((width, seq), F32),
            jax.ShapeDtypeStruct((width, seq), BF16),
            jax.ShapeDtypeStruct((width, seq), BF16),
            jax.ShapeDtypeStruct((3, inner, seq), BF16),
            jax.ShapeDtypeStruct((inner, seq), BF16),
            jax.ShapeDtypeStruct((HEADS, seq, seq), F32),
        ),
        in_specs=[pl.BlockSpec(memory_space=pltpu.SMEM)] + [vmem_spec()] * 5 + [any_spec()] * 8,
        out_specs=(vmem_spec(),) * 7,
        scratch_shapes=[pltpu.SemaphoreType.DMA((8, n_row))],
        compiler_params=pltpu.CompilerParams(vmem_limit_bytes=VMEM_LIMIT),
        cost_estimate=pl.CostEstimate(flops=8_000_000_000, bytes_accessed=16_000_000, transcendentals=400_000),
        name="attention_forward",
    )(where, x, gain_one, gain_two, bias, onehot, *units)


def attention_backward_kernel(
    where_ref,
    x_ref,
    gain_one_ref,
    gain_two_ref,
    onehot_ref,
    out_grad_ref,
    part_a_ref,
    part_b_ref,
    part_c_ref,
    weights_ref,
    residual_ref,
    normed_one_ref,
    qkv_ref,
    context_ref,
    probs_ref,
    near_ref,
    far_ref,
    tokens_grad_ref,
    small_ref,
    grads_ref,
    *,
    n_row,
    shard,
):
    _, core, x_bit, y_bit, z_index = (where_ref[k] for k in range(5))
    inner = HEADS * DKV
    seq = x_ref.shape[1]
    width = x_ref.shape[0]
    ones = jnp.ones((8, seq), F32)

    def store_weight_grad(matrix, grad):
        grad = grad.astype(BF16)
        target_core = matrix & 1
        x_shift = (matrix >> 1) ^ x_bit
        for side in range(2):
            y_shift = side ^ y_bit
            if target_core == 0:
                unit = x_shift * 2 + y_shift
            else:
                unit = y_shift * 2 + x_shift
            for z in range(n_row):
                slot = unit * n_row + lax.rem(z - z_index + n_row, n_row)
                start = (z * 2 + side) * shard
                block = grad[start : start + shard, :]

                @pl.when(core == target_core)
                def _():
                    near_ref[slot] = block

                @pl.when(core != target_core)
                def _():
                    far_ref[slot] = block

    residual = residual_ref[...]
    grad_normed = (
        part_a_ref[...].astype(F32) + part_b_ref[...].astype(F32) + part_c_ref[...].astype(F32)
    )
    inverse_two = lax.rsqrt(jnp.mean(residual * residual, axis=0, keepdims=True) + EPSILON)
    gained = grad_normed * wide(gain_two_ref[...], seq)
    ffn_gain_grad = dot(ones, grad_normed * residual * inverse_two, NT, HIGHEST)
    grad_residual = (
        out_grad_ref[...].astype(F32)
        + inverse_two * gained
        - residual
        * (inverse_two * inverse_two * inverse_two * jnp.mean(gained * residual, axis=0, keepdims=True))
    )
    grad_attended = grad_residual.astype(BF16)
    store_weight_grad(3, dot(context_ref[...], grad_attended, NT))
    grad_context = dot(weights_ref[3 * inner :, :], grad_attended, NN).astype(BF16)
    flip = (
        lax.broadcasted_iota(jnp.int32, (seq, seq), 0)
        + lax.broadcasted_iota(jnp.int32, (seq, seq), 1)
        == seq - 1
    ).astype(BF16)
    zero_half = jnp.zeros((seq, seq), F32)
    diagonals = []
    for h in range(HEADS):
        rows = slice(h * DKV, (h + 1) * DKV)
        probs = probs_ref[h]
        grad_head = grad_context[rows, :]
        grads_ref[2, rows, :] = dot(grad_head, probs.astype(BF16), NT).astype(BF16)
        grad_probs = dot(qkv_ref[2, rows, :], grad_head, TN)
        grad_scores = (
            probs * (grad_probs - jnp.sum(probs * grad_probs, axis=0, keepdims=True))
        ).astype(BF16)
        grads_ref[0, rows, :] = dot(qkv_ref[1, rows, :], grad_scores, NN).astype(BF16)
        grads_ref[1, rows, :] = dot(qkv_ref[0, rows, :], grad_scores, NT).astype(BF16)
        flipped = jnp.concatenate((dot(flip, grad_scores, NN), zero_half), axis=1)
        rolled = pltpu.roll(flipped, seq + 1, 1, stride=1, stride_axis=0)
        diagonals.append(jnp.sum(rolled, axis=0, keepdims=True))
    diagonals.append(jnp.zeros((8 - HEADS, 2 * seq), F32))
    table = dot(jnp.concatenate(diagonals, axis=0), onehot_ref[...], NT, HIGHEST)
    normed_one = normed_one_ref[...]
    grad_normed_one = None
    for m in range(3):
        store_weight_grad(m, dot(grads_ref[m], normed_one, NT))
        part = dot(weights_ref[m * inner : (m + 1) * inner, :], grads_ref[m], TN)
        grad_normed_one = part if grad_normed_one is None else grad_normed_one + part
    x = x_ref[...].astype(F32)
    inverse_one = lax.rsqrt(jnp.mean(x * x, axis=0, keepdims=True) + EPSILON)
    gained_one = grad_normed_one * wide(gain_one_ref[...], seq)
    attn_gain_grad = dot(ones, grad_normed_one * x * inverse_one, NT, HIGHEST)
    tokens_grad_ref[...] = (
        grad_residual
        + inverse_one * gained_one
        - x * (inverse_one * inverse_one * inverse_one * jnp.mean(gained_one * x, axis=0, keepdims=True))
    ).astype(BF16)
    small_ref[0:8, :] = jnp.where(
        lax.broadcasted_iota(jnp.int32, (8, width), 0) == 0, attn_gain_grad, ffn_gain_grad
    )
    small_ref[8:16, :] = jnp.concatenate((table, jnp.zeros((8, width - BUCKETS), F32)), axis=1)


def attention_backward(where, x, gain_one, gain_two, onehot, out_grad, parts, saved, n_row):
    width, seq = x.shape
    inner = HEADS * DKV
    shard = inner // (2 * n_row)
    return pl.pallas_call(
        functools.partial(attention_backward_kernel, n_row=n_row, shard=shard),
        out_shape=(
            jax.ShapeDtypeStruct((4 * n_row, shard, width), BF16),
            jax.ShapeDtypeStruct((4 * n_row, shard, width), BF16),
            jax.ShapeDtypeStruct((width, seq), BF16),
            jax.ShapeDtypeStruct((16, width), F32),
        ),
        in_specs=[pl.BlockSpec(memory_space=pltpu.SMEM)] + [vmem_spec()] * 14,
        out_specs=(vmem_spec(),) * 4,
        scratch_shapes=[pltpu.VMEM((3, inner, seq), BF16)],
        compiler_params=pltpu.CompilerParams(vmem_limit_bytes=VMEM_LIMIT),
        cost_estimate=pl.CostEstimate(flops=12_000_000_000, bytes_accessed=20_000_000, transcendentals=1000),
        name="attention_backward",
    )(where, x, gain_one, gain_two, onehot, out_grad, *parts, *saved)


GELU_SCALE = float(np.sqrt(2.0 / np.pi))


def feed_forward_kernel(*refs, count):
    normed_refs, grad_refs = refs[:count], refs[count : 2 * count]
    weights_ref = refs[2 * count]
    outs = refs[2 * count + 1 :]
    gated_refs, hidden_refs, back_refs = outs[:count], outs[count : 2 * count], outs[2 * count :]
    hidden = weights_ref.shape[2]
    for b in range(count):
        normed = normed_refs[b][...]
        gate = dot(weights_ref[0], normed, TN)
        up = dot(weights_ref[1], normed, TN)
        grad_gated = dot(weights_ref[2], grad_refs[b][...], TN)
        square = gate * gate
        tanh = jnp.tanh(GELU_SCALE * gate * (1.0 + 0.044715 * square))
        half = 0.5 * (1.0 + tanh)
        gelu = gate * half
        slope = half + (0.5 * GELU_SCALE) * gate * (1.0 - tanh * tanh) * (1.0 + 3 * 0.044715 * square)
        gated_refs[b][...] = (gelu * up).astype(BF16)
        grad_gate = (grad_gated * up * slope).astype(BF16)
        grad_up = (grad_gated * gelu).astype(BF16)
        hidden_refs[b][:hidden, :] = grad_gate
        hidden_refs[b][hidden:, :] = grad_up
        back_refs[b][...] = (
            dot(weights_ref[0], grad_gate, NN) + dot(weights_ref[1], grad_up, NN)
        ).astype(BF16)


def feed_forward(normed, grads, weights):
    count = len(normed)
    width, rows = normed[0].shape
    hidden = weights.shape[2]
    outs = pl.pallas_call(
        functools.partial(feed_forward_kernel, count=count),
        out_shape=[jax.ShapeDtypeStruct((hidden, rows), BF16)] * count
        + [jax.ShapeDtypeStruct((2 * hidden, rows), BF16)] * count
        + [jax.ShapeDtypeStruct((width, rows), BF16)] * count,
        in_specs=[vmem_spec()] * (2 * count + 1),
        out_specs=[vmem_spec()] * (3 * count),
        compiler_params=pltpu.CompilerParams(vmem_limit_bytes=VMEM_LIMIT),
        cost_estimate=pl.CostEstimate(
            flops=16 * count * rows * width * hidden,
            bytes_accessed=2 * (3 * width * hidden + count * rows * (3 * width + 3 * hidden)),
            transcendentals=count * rows * hidden,
        ),
        name="feed_forward",
    )(*normed, *grads, weights)
    return outs[:count], outs[count : 2 * count], outs[2 * count :]


def weight_grads_kernel(*refs, count, tile):
    normed, grads, gated, hidden_grads = (refs[k * count : (k + 1) * count] for k in range(4))
    weights_ref, out_ref = refs[4 * count : 4 * count + 2]
    branch = refs[4 * count + 2 : 5 * count + 2]
    grads_all, gated_all, normed_all, hidden_all, sems = refs[5 * count + 2 :]
    rows = gated[0].shape[1]
    hidden = gated[0].shape[0]
    width = grads_all.shape[0]
    copies = []
    for k, (sources, target) in enumerate(
        ((gated, gated_all), (grads, grads_all), (hidden_grads, hidden_all), (normed, normed_all))
    ):
        group = []
        for b in range(count):
            copy = pltpu.make_async_copy(
                sources[b], target.at[:, pl.ds(b * rows, rows)], sems.at[k, b]
            )
            copy.start()
            group.append(copy)
        copies.append(group)
    for copy in copies[0]:
        copy.wait()
    for b in range(count):
        branch[b][...] = dot(
            weights_ref[2], gated_all[:, b * rows : (b + 1) * rows], NN
        ).astype(BF16)
    for copy in copies[1]:
        copy.wait()

    @pl.loop(0, width // tile)
    def _(t):
        at = pl.ds(pl.multiple_of(t * tile, 16), tile)
        out_ref[2, at, :] = dot(grads_all[at, :], gated_all[...], NT).astype(BF16)

    for copy in copies[2] + copies[3]:
        copy.wait()

    @pl.loop(0, width // tile)
    def _(t):
        at = pl.ds(pl.multiple_of(t * tile, 16), tile)
        piece = normed_all[at, :]
        out_ref[0, at, :] = dot(piece, hidden_all[:hidden, :], NT).astype(BF16)
        out_ref[1, at, :] = dot(piece, hidden_all[hidden:, :], NT).astype(BF16)


def weight_grads(normed, grads, gated, hidden_grads, weights):
    count = len(normed)
    width, rows = normed[0].shape
    hidden = weights.shape[2]
    tokens = count * rows
    outs = pl.pallas_call(
        functools.partial(weight_grads_kernel, count=count, tile=width // 4),
        out_shape=[jax.ShapeDtypeStruct((3, width, hidden), BF16)]
        + [jax.ShapeDtypeStruct((width, rows), BF16)] * count,
        in_specs=[any_spec()] * (4 * count) + [vmem_spec()],
        out_specs=[vmem_spec()] * (count + 1),
        scratch_shapes=[
            pltpu.VMEM((width, tokens), BF16),
            pltpu.VMEM((hidden, tokens), BF16),
            pltpu.VMEM((width, tokens), BF16),
            pltpu.VMEM((2 * hidden, tokens), BF16),
            pltpu.SemaphoreType.DMA((4, count)),
        ],
        compiler_params=pltpu.CompilerParams(vmem_limit_bytes=VMEM_LIMIT),
        cost_estimate=pl.CostEstimate(
            flops=14 * tokens * width * hidden,
            bytes_accessed=2 * (6 * width * hidden + 3 * tokens * (width + hidden)),
            transcendentals=0,
        ),
        name="weight_grads",
    )(*normed, *grads, *gated, *hidden_grads, weights)
    return outs[0], outs[1:]


def join_quarters_kernel(parts_ref, gate_ref, up_ref, down_ref, held, joined, in_sems, out_sems):
    loads = [
        pltpu.make_async_copy(parts_ref.at[:, m], held.at[m], in_sems.at[m]) for m in range(3)
    ]
    for load in loads:
        load.start()
    stores = []
    for m, ref in enumerate((gate_ref, up_ref, down_ref)):
        loads[m].wait()
        joined[m] = jnp.concatenate([held[m, q] for q in range(4)], axis=1).astype(F32)
        store = pltpu.make_async_copy(joined.at[m], ref, out_sems.at[m])
        store.start()
        stores.append(store)
    for store in stores:
        store.wait()


def join_quarters(parts):
    _, _, rows, cols = parts.shape
    return pl.pallas_call(
        join_quarters_kernel,
        out_shape=[jax.ShapeDtypeStruct((rows, 4 * cols), F32)] * 3,
        in_specs=[any_spec()],
        out_specs=[any_spec()] * 3,
        scratch_shapes=[
            pltpu.VMEM((3, 4, rows, cols), BF16),
            pltpu.VMEM((3, rows, 4 * cols), F32),
            pltpu.SemaphoreType.DMA((3,)),
            pltpu.SemaphoreType.DMA((3,)),
        ],
        compiler_params=pltpu.CompilerParams(vmem_limit_bytes=VMEM_LIMIT),
        cost_estimate=pl.CostEstimate(flops=0, bytes_accessed=12 * rows * cols * 6, transcendentals=0),
        name="join_quarters",
    )(parts)


def local(
    sizes,
    tokens,
    lengths,
    attn_gain,
    ffn_gain,
    w_query,
    w_key,
    w_value,
    w_attn_out,
    rel_bias,
    w_gate,
    w_up,
    w_down,
    out_grad,
):
    n_dp, n_row, n_col = sizes
    lo = n_col // 2
    one_group = n_dp == 4 and n_col == 2
    seq, width = tokens.shape[2], tokens.shape[3]
    inner = HEADS * DKV
    dp, row, col = lax.axis_index("dp"), lax.axis_index("row"), lax.axis_index("col")
    core, x_bit, y_bit, quarter = dp % 2, (dp // 2) % 2, col // lo, dp % 4

    first, second = [], []
    for d in range(n_dp):
        for c in range(n_col):
            here, over_x, over_y = d * n_col + c, (d ^ 2) * n_col + c, d * n_col + (c + lo) % n_col
            first.append((here, over_x if d % 2 == 0 else over_y))
            second.append((here, over_y if d % 2 == 0 else over_x))
    swap = [(d, d ^ 1) for d in range(n_dp)]

    def send_first(a):
        return lax.ppermute(a, ("dp", "col"), first)

    def send_second(a):
        return lax.ppermute(a, ("dp", "col"), second)

    def send_core(a):
        return lax.ppermute(a, "dp", swap)

    def send_row(a, k):
        return lax.ppermute(a, "row", [(i, (i + k) % n_row) for i in range(n_row)])

    def after(a, *others):
        return lax.optimization_barrier((a, *others))[0]

    def add(a, b):
        return (a.astype(F32) + b.astype(F32)).astype(BF16)

    def whole_cols(a, axis):
        return lax.all_gather(a, "col", axis=axis, tiled=True) if lo > 1 else a

    x = jnp.transpose(tokens.reshape(seq, width))
    grad = jnp.transpose(out_grad.reshape(seq, width))
    onehot = jnp.asarray(bucket_onehot(seq))
    where = jnp.stack((lengths.reshape(()), core, x_bit, y_bit, row)).astype(jnp.int32)
    gain_one = jnp.broadcast_to(attn_gain.reshape(width, 1), (width, 128))
    gain_two = jnp.broadcast_to(ffn_gain.reshape(width, 1), (width, 128))
    bias = jnp.pad(jnp.transpose(rel_bias), ((0, 8 - HEADS), (0, 0)))

    shard = inner // (2 * n_row)
    proj = jnp.where(quarter == 0, w_query, jnp.where(quarter == 1, w_key, w_value))
    own = jnp.where(quarter == 3, w_attn_out, jnp.transpose(proj))
    if lo > 1:
        own = lax.dynamic_slice_in_dim(whole_cols(own, 0), y_bit * shard, shard, 0)
    unit = jnp.concatenate([own] + [send_row(own, k) for k in range(1, n_row)], axis=0)
    grad_two, grad_one = send_first(grad), send_second(grad)
    unit = after(unit, grad_two, grad_one)
    unit_two, unit_one = send_first(unit), send_second(unit)
    unit_three = send_second(unit_two)
    near_units = [unit, unit_one, unit_two, unit_three]
    units = near_units + [send_core(u) for u in near_units]
    grad_three = send_second(after(grad_two, unit_two))
    near_grads = [grad, grad_one, grad_two, grad_three]
    grads = near_grads + [send_core(g) for g in near_grads]

    hidden = w_gate.shape[1] * lo // 4
    start = quarter * hidden + (y_bit * 4 * hidden if lo > 1 else 0)
    ffn_own = jnp.stack(
        (
            lax.dynamic_slice_in_dim(whole_cols(w_gate, 1), start, hidden, 1),
            lax.dynamic_slice_in_dim(whole_cols(w_up, 1), start, hidden, 1),
            jnp.transpose(lax.dynamic_slice_in_dim(whole_cols(w_down, 0), start, hidden, 0)),
        )
    )
    ffn_weights = lax.all_gather(ffn_own, "row", axis=1, tiled=True)

    weights, residual, normed_one, normed_two, qkv, context, probs = attention_forward(
        where, x, gain_one, gain_two, bias, onehot, units, n_row
    )
    two, one = send_first(normed_two), send_second(normed_two)
    near_normed = [normed_two, one, two, send_second(two)]
    normed = near_normed + [send_core(a) for a in near_normed]

    gated, hidden_grads, back = [None] * 8, [None] * 8, [None] * 8
    for near in (0, 2, 1, 3):
        pair = (near, near + 4)
        got = feed_forward([normed[p] for p in pair], [grads[p] for p in pair], ffn_weights)
        for i, p in enumerate(pair):
            gated[p], hidden_grads[p], back[p] = got[0][i], got[1][i], got[2][i]

    def collect(blocks, *ready):
        near = {p: add(blocks[p], send_core(blocks[4 + p])) for p in (1, 3, 2, 0)}
        if ready:
            near[1], near[3] = after(near[1], *ready), after(near[3], *ready)
        from_one, from_three = send_second(near[1]), send_second(near[3])
        from_two = send_first(add(near[2], from_three))
        return (near[0], from_one, from_two), near[3]

    back_parts, sent = collect(back)

    ffn_grads, branch = weight_grads(normed, grads, gated, hidden_grads, after(ffn_weights, sent))
    ffn_grads = lax.psum_scatter(ffn_grads, "row", scatter_dimension=1, tiled=True)
    branch_parts, _ = collect(branch, *back_parts)
    layer_out = (residual + sum(p.astype(F32) for p in branch_parts)).astype(BF16)

    near_grads, far_grads, tokens_grad, small = attention_backward(
        where,
        x,
        gain_one,
        gain_two,
        onehot,
        grad,
        back_parts,
        (weights, residual, normed_one, qkv, context, probs),
        n_row,
    )
    summed = add(near_grads, send_core(far_grads))
    quad = [summed[p * n_row : (p + 1) * n_row] for p in range(4)]
    from_one, from_three = send_second(quad[1]), send_second(quad[3])
    from_two = send_first(add(quad[2], from_three))
    mine = (quad[0].astype(F32) + from_one.astype(F32) + from_two.astype(F32)).astype(BF16)
    attn_grad = mine[0].astype(F32)
    for k in range(1, n_row):
        attn_grad = attn_grad + send_row(mine[k], k).astype(F32)
    attn_grad = attn_grad.astype(BF16)

    if one_group:
        small = small + send_core(small)
        small = small + send_first(small)
        small = small + send_second(small)
        small = small + sum(send_row(small, k) for k in range(1, n_row))
    else:
        small = lax.psum(small, ("dp", "row", "col"))

    def gather_quarters(a):
        if n_dp == 4:
            return lax.all_gather(a, "dp", axis=0)
        placed = lax.dynamic_update_index_in_dim(jnp.zeros((4, *a.shape), a.dtype), a, quarter, 0)
        return lax.psum(placed, "dp")

    def own_cols(a):
        placed = jnp.zeros((n_col, *a.shape[1:]), a.dtype)
        placed = lax.dynamic_update_slice_in_dim(placed, a, y_bit * lo, 0)
        return lax.psum_scatter(placed, "col", scatter_dimension=0, tiled=False)

    attn_grads = gather_quarters(attn_grad)
    ffn_grads = gather_quarters(ffn_grads)
    if lo > 1:
        piece = shard // lo
        attn_grads = own_cols(jnp.transpose(attn_grads.reshape(4, lo, piece, width), (1, 0, 2, 3)))
        piece = 4 * hidden // lo
        ffn_grads = jnp.transpose(ffn_grads, (1, 2, 0, 3)).reshape(3, width // n_row, lo, piece)
        ffn_grads = own_cols(jnp.transpose(ffn_grads, (2, 0, 1, 3))).astype(F32)
        gate_grad, up_grad, down_grad = ffn_grads[0], ffn_grads[1], ffn_grads[2]
    else:
        gate_grad, up_grad, down_grad = join_quarters(ffn_grads)
    attn_grads = attn_grads.astype(F32)

    place = row * n_col + col
    gain_cols, table_rows = width // (n_row * n_col), BUCKETS // (n_row * n_col)
    gain_grads = lax.dynamic_slice_in_dim(small[:2], place * gain_cols, gain_cols, 1)
    table_grad = jnp.transpose(small[8 : 8 + HEADS, :BUCKETS])
    table_grad = lax.dynamic_slice_in_dim(table_grad, place * table_rows, table_rows, 0)
    return (
        jnp.transpose(layer_out).reshape(tokens.shape),
        jnp.transpose(tokens_grad).reshape(tokens.shape),
        gain_grads[0],
        gain_grads[1],
        jnp.transpose(attn_grads[0]),
        jnp.transpose(attn_grads[1]),
        jnp.transpose(attn_grads[2]),
        attn_grads[3],
        table_grad,
        gate_grad,
        up_grad,
        jnp.transpose(down_grad),
    )


def solution(mesh):
    sizes = tuple(mesh.shape[name] for name in ("dp", "row", "col"))
    placed = (
        P(("dp", "col"), "row", None, None),
        P(("dp", "col"), "row"),
        P(),
        P(),
        P(None, ("row", "col")),
        P(None, ("row", "col")),
        P(None, ("row", "col")),
        P(("row", "col"), None),
        P(),
        P("row", "col"),
        P("row", "col"),
        P("col", "row"),
        P(("dp", "col"), "row", None, None),
    )
    return jax.shard_map(
        functools.partial(local, sizes),
        mesh=mesh,
        in_specs=placed,
        out_specs=(
            P(("dp", "col"), "row", None, None),
            P(("dp", "col"), "row", None, None),
            P(("row", "col")),
            P(("row", "col")),
            P(None, ("row", "col")),
            P(None, ("row", "col")),
            P(None, ("row", "col")),
            P(("row", "col"), None),
            P(("row", "col"), None),
            P("row", "col"),
            P("row", "col"),
            P("col", "row"),
        ),
        check_vma=False,
    )
```

```python
import functools

import jax
import jax.numpy as jnp
import numpy as np
from jax import lax
from jax.experimental import pallas as pl
from jax.experimental.pallas import tpu as pltpu
from jax.sharding import PartitionSpec as P

HEADS = 6
DKV = 64
BUCKETS = 32
MAX_DIST = 128
EPSILON = 1e-06
HIGHEST = lax.Precision.HIGHEST
F32 = jnp.float32
BF16 = jnp.bfloat16
VMEM_LIMIT = 56 * 1024 * 1024


def bucket_table(length):
    offsets = np.arange(-(length - 1), length)
    half_count = BUCKETS // 2
    exact_count = half_count // 2
    upper_half = (offsets > 0).astype(np.int64) * half_count
    distance = np.abs(offsets)
    safe_distance = np.maximum(distance, 1)
    spread = (
        np.log(safe_distance / exact_count)
        / np.log(MAX_DIST / exact_count)
        * (half_count - exact_count)
    )
    far_bucket = np.minimum(
        exact_count + np.floor(np.maximum(spread, 0.0)).astype(np.int64), half_count - 1
    )
    return (upper_half + np.where(distance < exact_count, distance, far_bucket)).astype(np.int32)


def bucket_onehot(length):
    onehot = np.zeros((BUCKETS, 2 * length), np.float32)
    offsets = np.arange(-(length - 1), length)
    onehot[bucket_table(length), (-offsets) % (2 * length)] = 1.0
    return onehot


def dot(a, b, dims, precision=None):
    return lax.dot_general(a, b, (dims, ((), ())), precision=precision, preferred_element_type=F32)


NN = ((1,), (0,))
NT = ((1,), (1,))
TN = ((0,), (0,))


def vmem_spec():
    return pl.BlockSpec(memory_space=pltpu.VMEM)


def any_spec():
    return pl.BlockSpec(memory_space=pl.ANY)


def wide(column, width):
    return jnp.concatenate([column] * (width // column.shape[1]), axis=1)


def attention_forward_kernel(
    where_ref, x_ref, gain_one_ref, gain_two_ref, bias_ref, onehot_ref, *rest, n_row, shard
):
    units = rest[:8]
    (weights_ref, residual_ref, normed_one_ref, normed_two_ref, qkv_ref, context_ref, probs_ref, sems) = rest[8:]
    length, core, x_bit, y_bit, z_index = (where_ref[k] for k in range(5))
    inner = HEADS * DKV
    seq = x_ref.shape[1]
    copies = []
    for unit in range(8):
        far, one, two = unit >> 2, (unit >> 1) & 1, unit & 1
        own_core = core ^ far
        x_shift = jnp.where(own_core == 0, one, two)
        y_shift = jnp.where(own_core == 0, two, one)
        matrix = (x_bit ^ x_shift) * 2 + own_core
        side = y_bit ^ y_shift
        for k in range(n_row):
            z_from = lax.rem(z_index - k + n_row, n_row)
            start = pl.multiple_of(matrix * inner + (z_from * 2 + side) * shard, 16)
            copy = pltpu.make_async_copy(
                units[unit].at[pl.ds(k * shard, shard)],
                weights_ref.at[pl.ds(start, shard)],
                sems.at[unit, k],
            )
            copy.start()
            copies.append(copy)
    x = x_ref[...].astype(F32)
    inverse = lax.rsqrt(jnp.mean(x * x, axis=0, keepdims=True) + EPSILON)
    normed = (x * inverse * wide(gain_one_ref[...], seq)).astype(BF16)
    normed_one_ref[...] = normed
    per_offset = dot(bias_ref[...], onehot_ref[...], NN, HIGHEST)
    key_valid = lax.broadcasted_iota(jnp.int32, (seq, seq), 0) < length
    for copy in copies:
        copy.wait()
    for m in range(3):
        qkv_ref[m] = dot(weights_ref[m * inner : (m + 1) * inner, :], normed, NN).astype(BF16)
    for h in range(HEADS):
        rows = slice(h * DKV, (h + 1) * DKV)
        row = jnp.broadcast_to(per_offset[h : h + 1, :], (seq, 2 * seq))
        bias = pltpu.roll(row, 0, 1, stride=1, stride_axis=0)[:, :seq]
        scores = dot(qkv_ref[1, rows, :], qkv_ref[0, rows, :], TN) + bias
        scores = jnp.where(key_valid, scores, -1e30)
        weights = jnp.exp(scores - jnp.max(scores, axis=0, keepdims=True))
        probs = weights / jnp.sum(weights, axis=0, keepdims=True)
        probs_ref[h] = probs
        context_ref[rows, :] = dot(qkv_ref[2, rows, :], probs.astype(BF16), NN).astype(BF16)
    residual = x + dot(weights_ref[3 * inner :, :], context_ref[...], TN)
    residual_ref[...] = residual
    inverse_two = lax.rsqrt(jnp.mean(residual * residual, axis=0, keepdims=True) + EPSILON)
    normed_two_ref[...] = (residual * inverse_two * wide(gain_two_ref[...], seq)).astype(BF16)


def attention_forward(where, x, gain_one, gain_two, bias, onehot, units, n_row):
    width, seq = x.shape
    inner = HEADS * DKV
    return pl.pallas_call(
        functools.partial(attention_forward_kernel, n_row=n_row, shard=inner // (2 * n_row)),
        out_shape=(
            jax.ShapeDtypeStruct((4 * inner, width), BF16),
            jax.ShapeDtypeStruct((width, seq), F32),
            jax.ShapeDtypeStruct((width, seq), BF16),
            jax.ShapeDtypeStruct((width, seq), BF16),
            jax.ShapeDtypeStruct((3, inner, seq), BF16),
            jax.ShapeDtypeStruct((inner, seq), BF16),
            jax.ShapeDtypeStruct((HEADS, seq, seq), F32),
        ),
        in_specs=[pl.BlockSpec(memory_space=pltpu.SMEM)] + [vmem_spec()] * 5 + [any_spec()] * 8,
        out_specs=(vmem_spec(),) * 7,
        scratch_shapes=[pltpu.SemaphoreType.DMA((8, n_row))],
        compiler_params=pltpu.CompilerParams(vmem_limit_bytes=VMEM_LIMIT),
        cost_estimate=pl.CostEstimate(flops=8_000_000_000, bytes_accessed=16_000_000, transcendentals=400_000),
        name="attention_forward",
    )(where, x, gain_one, gain_two, bias, onehot, *units)


def attention_backward_kernel(
    where_ref,
    x_ref,
    gain_one_ref,
    gain_two_ref,
    onehot_ref,
    out_grad_ref,
    part_a_ref,
    part_b_ref,
    part_c_ref,
    weights_ref,
    residual_ref,
    normed_one_ref,
    qkv_ref,
    context_ref,
    probs_ref,
    near_ref,
    far_ref,
    tokens_grad_ref,
    small_ref,
    grads_ref,
    *,
    n_row,
    shard,
):
    _, core, x_bit, y_bit, z_index = (where_ref[k] for k in range(5))
    inner = HEADS * DKV
    seq = x_ref.shape[1]
    width = x_ref.shape[0]
    ones = jnp.ones((8, seq), F32)

    def store_weight_grad(matrix, grad):
        grad = grad.astype(BF16)
        target_core = matrix & 1
        x_shift = (matrix >> 1) ^ x_bit
        for side in range(2):
            y_shift = side ^ y_bit
            if target_core == 0:
                unit = x_shift * 2 + y_shift
            else:
                unit = y_shift * 2 + x_shift
            for z in range(n_row):
                slot = unit * n_row + lax.rem(z - z_index + n_row, n_row)
                start = (z * 2 + side) * shard
                block = grad[start : start + shard, :]

                @pl.when(core == target_core)
                def _():
                    near_ref[slot] = block

                @pl.when(core != target_core)
                def _():
                    far_ref[slot] = block

    residual = residual_ref[...]
    grad_normed = (
        part_a_ref[...].astype(F32) + part_b_ref[...].astype(F32) + part_c_ref[...].astype(F32)
    )
    inverse_two = lax.rsqrt(jnp.mean(residual * residual, axis=0, keepdims=True) + EPSILON)
    gained = grad_normed * wide(gain_two_ref[...], seq)
    ffn_gain_grad = dot(ones, grad_normed * residual * inverse_two, NT, HIGHEST)
    grad_residual = (
        out_grad_ref[...].astype(F32)
        + inverse_two * gained
        - residual
        * (inverse_two * inverse_two * inverse_two * jnp.mean(gained * residual, axis=0, keepdims=True))
    )
    grad_attended = grad_residual.astype(BF16)
    store_weight_grad(3, dot(context_ref[...], grad_attended, NT))
    grad_context = dot(weights_ref[3 * inner :, :], grad_attended, NN).astype(BF16)
    flip = (
        lax.broadcasted_iota(jnp.int32, (seq, seq), 0)
        + lax.broadcasted_iota(jnp.int32, (seq, seq), 1)
        == seq - 1
    ).astype(BF16)
    zero_half = jnp.zeros((seq, seq), F32)
    diagonals = []
    for h in range(HEADS):
        rows = slice(h * DKV, (h + 1) * DKV)
        probs = probs_ref[h]
        grad_head = grad_context[rows, :]
        grads_ref[2, rows, :] = dot(grad_head, probs.astype(BF16), NT).astype(BF16)
        grad_probs = dot(qkv_ref[2, rows, :], grad_head, TN)
        grad_scores = (
            probs * (grad_probs - jnp.sum(probs * grad_probs, axis=0, keepdims=True))
        ).astype(BF16)
        grads_ref[0, rows, :] = dot(qkv_ref[1, rows, :], grad_scores, NN).astype(BF16)
        grads_ref[1, rows, :] = dot(qkv_ref[0, rows, :], grad_scores, NT).astype(BF16)
        flipped = jnp.concatenate((dot(flip, grad_scores, NN), zero_half), axis=1)
        rolled = pltpu.roll(flipped, seq + 1, 1, stride=1, stride_axis=0)
        diagonals.append(jnp.sum(rolled, axis=0, keepdims=True))
    diagonals.append(jnp.zeros((8 - HEADS, 2 * seq), F32))
    table = dot(jnp.concatenate(diagonals, axis=0), onehot_ref[...], NT, HIGHEST)
    normed_one = normed_one_ref[...]
    grad_normed_one = None
    for m in range(3):
        store_weight_grad(m, dot(grads_ref[m], normed_one, NT))
        part = dot(weights_ref[m * inner : (m + 1) * inner, :], grads_ref[m], TN)
        grad_normed_one = part if grad_normed_one is None else grad_normed_one + part
    x = x_ref[...].astype(F32)
    inverse_one = lax.rsqrt(jnp.mean(x * x, axis=0, keepdims=True) + EPSILON)
    gained_one = grad_normed_one * wide(gain_one_ref[...], seq)
    attn_gain_grad = dot(ones, grad_normed_one * x * inverse_one, NT, HIGHEST)
    tokens_grad_ref[...] = (
        grad_residual
        + inverse_one * gained_one
        - x * (inverse_one * inverse_one * inverse_one * jnp.mean(gained_one * x, axis=0, keepdims=True))
    ).astype(BF16)
    small_ref[0:8, :] = jnp.where(
        lax.broadcasted_iota(jnp.int32, (8, width), 0) == 0, attn_gain_grad, ffn_gain_grad
    )
    small_ref[8:16, :] = jnp.concatenate((table, jnp.zeros((8, width - BUCKETS), F32)), axis=1)


def attention_backward(where, x, gain_one, gain_two, onehot, out_grad, parts, saved, n_row):
    width, seq = x.shape
    inner = HEADS * DKV
    shard = inner // (2 * n_row)
    return pl.pallas_call(
        functools.partial(attention_backward_kernel, n_row=n_row, shard=shard),
        out_shape=(
            jax.ShapeDtypeStruct((4 * n_row, shard, width), BF16),
            jax.ShapeDtypeStruct((4 * n_row, shard, width), BF16),
            jax.ShapeDtypeStruct((width, seq), BF16),
            jax.ShapeDtypeStruct((16, width), F32),
        ),
        in_specs=[pl.BlockSpec(memory_space=pltpu.SMEM)] + [vmem_spec()] * 14,
        out_specs=(vmem_spec(),) * 4,
        scratch_shapes=[pltpu.VMEM((3, inner, seq), BF16)],
        compiler_params=pltpu.CompilerParams(vmem_limit_bytes=VMEM_LIMIT),
        cost_estimate=pl.CostEstimate(flops=12_000_000_000, bytes_accessed=20_000_000, transcendentals=1000),
        name="attention_backward",
    )(where, x, gain_one, gain_two, onehot, out_grad, *parts, *saved)


GELU_SCALE = float(np.sqrt(2.0 / np.pi))


def feed_forward_kernel(*refs, count):
    normed_refs, grad_refs = refs[:count], refs[count : 2 * count]
    weights_ref = refs[2 * count]
    outs = refs[2 * count + 1 :]
    gated_refs, hidden_refs, back_refs = (outs[k * count : (k + 1) * count] for k in range(3))
    turned, normed, grads, grads_in = outs[3 * count :]
    hidden, rows = gated_refs[0].shape
    turned[...] = weights_ref[...].T
    halves = (slice(0, rows), slice(rows, 2 * rows))
    for b in range(0, count, 2):
        for i, at in enumerate(halves):
            normed[:, at] = normed_refs[b + i][...]
            grads[:, at] = grad_refs[b + i][...]
        both = dot(turned[: 2 * hidden], normed[...], NN)
        gate, up = both[:hidden], both[hidden:]
        grad_gated = dot(turned[2 * hidden : 3 * hidden], grads[...], NN)
        square = gate * gate
        tanh = jnp.tanh(GELU_SCALE * gate * (1.0 + 0.044715 * square))
        half = 0.5 * (1.0 + tanh)
        gelu = gate * half
        slope = half + (0.5 * GELU_SCALE) * gate * (1.0 - tanh * tanh) * (1.0 + 3 * 0.044715 * square)
        gated = (gelu * up).astype(BF16)
        grad_gate = (grad_gated * up * slope).astype(BF16)
        grad_up = (grad_gated * gelu).astype(BF16)
        grads_in[:hidden] = grad_gate
        grads_in[hidden:] = grad_up
        back = dot(weights_ref[:, : 2 * hidden], grads_in[...], NN).astype(BF16)
        for i, at in enumerate(halves):
            gated_refs[b + i][...] = gated[:, at]
            hidden_refs[b + i][:hidden, :] = grad_gate[:, at]
            hidden_refs[b + i][hidden:, :] = grad_up[:, at]
            back_refs[b + i][...] = back[:, at]


def feed_forward(normed, grads, weights, hidden):
    count = len(normed)
    width, rows = normed[0].shape
    outs = pl.pallas_call(
        functools.partial(feed_forward_kernel, count=count),
        out_shape=[jax.ShapeDtypeStruct((hidden, rows), BF16)] * count
        + [jax.ShapeDtypeStruct((2 * hidden, rows), BF16)] * count
        + [jax.ShapeDtypeStruct((width, rows), BF16)] * count,
        in_specs=[vmem_spec()] * (2 * count + 1),
        out_specs=[vmem_spec()] * (3 * count),
        scratch_shapes=[
            pltpu.VMEM((weights.shape[1], width), BF16),
            pltpu.VMEM((width, 2 * rows), BF16),
            pltpu.VMEM((width, 2 * rows), BF16),
            pltpu.VMEM((2 * hidden, 2 * rows), BF16),
        ],
        compiler_params=pltpu.CompilerParams(vmem_limit_bytes=VMEM_LIMIT),
        cost_estimate=pl.CostEstimate(
            flops=16 * count * rows * width * hidden,
            bytes_accessed=2 * (3 * width * hidden + count * rows * (3 * width + 3 * hidden)),
            transcendentals=count * rows * hidden,
        ),
        name="feed_forward",
    )(*normed, *grads, weights)
    return outs[:count], outs[count : 2 * count], outs[2 * count :]


def weight_grads_kernel(*refs, count):
    normed, grads, gated, hidden_grads = (refs[k * count : (k + 1) * count] for k in range(4))
    weights_ref, out_ref = refs[4 * count : 4 * count + 2]
    branch = refs[4 * count + 2 : 5 * count + 2]
    normed_all, grads_all, gated_all, hidden_all, weights, sums, sent = refs[5 * count + 2 : 5 * count + 9]
    in_sems, weight_sem, sum_sems, sent_sems = refs[5 * count + 9 :]
    rows = gated[0].shape[1]
    hidden = gated[0].shape[0]
    tail = out_ref.shape[1] - 2 * hidden

    def load(k, sources, target):
        copies = [
            pltpu.make_async_copy(sources[b], target.at[:, pl.ds(b * rows, rows)], in_sems.at[k, b])
            for b in range(count)
        ]
        for copy in copies:
            copy.start()
        return copies

    def wait(copies):
        for copy in copies:
            copy.wait()

    stores = []

    def store(source, target, sem):
        copy = pltpu.make_async_copy(source, target, sem)
        copy.start()
        stores.append(copy)

    wait(load(0, hidden_grads, hidden_all) + load(1, normed, normed_all))
    later = load(2, gated, gated_all) + load(3, grads, grads_all)
    later.append(pltpu.make_async_copy(weights_ref.at[:, pl.ds(2 * hidden, tail)], weights, weight_sem))
    later[-1].start()
    sums[:, : 2 * hidden] = dot(normed_all[...], hidden_all[...], NT).astype(BF16)
    store(sums.at[:, pl.ds(0, 2 * hidden)], out_ref.at[:, pl.ds(0, 2 * hidden)], sum_sems.at[0])
    wait(later)
    sums[:, 2 * hidden : 3 * hidden] = dot(grads_all[...], gated_all[...], NT).astype(BF16)
    sums[:, 3 * hidden :] = jnp.zeros((sums.shape[0], tail - hidden), BF16)
    store(sums.at[:, pl.ds(2 * hidden, tail)], out_ref.at[:, pl.ds(2 * hidden, tail)], sum_sems.at[1])
    for b in range(count):
        sent[b] = dot(weights[:, :hidden], gated_all[:, b * rows : (b + 1) * rows], NN).astype(BF16)
        store(sent.at[b], branch[b], sent_sems.at[b])
    wait(stores)


def weight_grads(normed, grads, gated, hidden_grads, weights):
    count = len(grads)
    width, rows = grads[0].shape
    hidden = gated[0].shape[0]
    lanes = weights.shape[1]
    tokens = count * rows
    outs = pl.pallas_call(
        functools.partial(weight_grads_kernel, count=count),
        out_shape=[jax.ShapeDtypeStruct((width, lanes), BF16)]
        + [jax.ShapeDtypeStruct((width, rows), BF16)] * count,
        in_specs=[any_spec()] * (4 * count + 1),
        out_specs=[any_spec()] * (count + 1),
        scratch_shapes=[
            pltpu.VMEM((width, tokens), BF16),
            pltpu.VMEM((width, tokens), BF16),
            pltpu.VMEM((hidden, tokens), BF16),
            pltpu.VMEM((2 * hidden, tokens), BF16),
            pltpu.VMEM((width, lanes - 2 * hidden), BF16),
            pltpu.VMEM((width, lanes), BF16),
            pltpu.VMEM((count, width, rows), BF16),
            pltpu.SemaphoreType.DMA((4, count)),
            pltpu.SemaphoreType.DMA(()),
            pltpu.SemaphoreType.DMA((2,)),
            pltpu.SemaphoreType.DMA((count,)),
        ],
        compiler_params=pltpu.CompilerParams(vmem_limit_bytes=VMEM_LIMIT),
        cost_estimate=pl.CostEstimate(
            flops=14 * tokens * width * hidden,
            bytes_accessed=2 * (6 * width * hidden + 3 * tokens * (width + hidden)),
            transcendentals=0,
        ),
        name="weight_grads",
    )(*normed, *grads, *gated, *hidden_grads, weights)
    return outs[0], outs[1:]


def join_quarters_kernel(where_ref, *refs):
    parts, outs = refs[:4], refs[4:7]
    held, joined, in_sems, out_sems = refs[7:]
    quarter = where_ref[2] * 2 + where_ref[1]
    cols = outs[0].shape[1] // 4
    loads = []
    for r in range(4):
        load = pltpu.make_async_copy(parts[r], held.at[quarter ^ r], in_sems.at[r])
        load.start()
        loads.append(load)
    for load in loads:
        load.wait()
    stores = []
    for m in range(3):
        joined[m] = jnp.concatenate(
            [held[q, :, m * cols : (m + 1) * cols] for q in range(4)], axis=1
        ).astype(F32)
        store = pltpu.make_async_copy(joined.at[m], outs[m], out_sems.at[m])
        store.start()
        stores.append(store)
    for store in stores:
        store.wait()


def join_quarters(where, parts, cols):
    rows, lanes = parts[0].shape
    return pl.pallas_call(
        join_quarters_kernel,
        out_shape=[jax.ShapeDtypeStruct((rows, 4 * cols), F32)] * 3,
        in_specs=[pl.BlockSpec(memory_space=pltpu.SMEM)] + [any_spec()] * 4,
        out_specs=[any_spec()] * 3,
        scratch_shapes=[
            pltpu.VMEM((4, rows, lanes), BF16),
            pltpu.VMEM((3, rows, 4 * cols), F32),
            pltpu.SemaphoreType.DMA((4,)),
            pltpu.SemaphoreType.DMA((3,)),
        ],
        compiler_params=pltpu.CompilerParams(vmem_limit_bytes=VMEM_LIMIT),
        cost_estimate=pl.CostEstimate(flops=0, bytes_accessed=12 * rows * cols * 6, transcendentals=0),
        name="join_quarters",
    )(where, *parts)


def local(
    sizes,
    tokens,
    lengths,
    attn_gain,
    ffn_gain,
    w_query,
    w_key,
    w_value,
    w_attn_out,
    rel_bias,
    w_gate,
    w_up,
    w_down,
    out_grad,
):
    n_dp, n_row, n_col = sizes
    lo = n_col // 2
    one_group = n_dp == 4 and n_col == 2
    seq, width = tokens.shape[2], tokens.shape[3]
    inner = HEADS * DKV
    dp, row, col = lax.axis_index("dp"), lax.axis_index("row"), lax.axis_index("col")
    core, x_bit, y_bit, quarter = dp % 2, (dp // 2) % 2, col // lo, dp % 4

    first, second = [], []
    for d in range(n_dp):
        for c in range(n_col):
            here, over_x, over_y = d * n_col + c, (d ^ 2) * n_col + c, d * n_col + (c + lo) % n_col
            first.append((here, over_x if d % 2 == 0 else over_y))
            second.append((here, over_y if d % 2 == 0 else over_x))
    swap = [(d, d ^ 1) for d in range(n_dp)]

    def send_first(a):
        return lax.ppermute(a, ("dp", "col"), first)

    def send_second(a):
        return lax.ppermute(a, ("dp", "col"), second)

    def send_core(a):
        return lax.ppermute(a, "dp", swap)

    def send_row(a, k):
        return lax.ppermute(a, "row", [(i, (i + k) % n_row) for i in range(n_row)])

    def after(a, *others):
        return lax.optimization_barrier((a, *others))[0]

    def add(a, b):
        return (a.astype(F32) + b.astype(F32)).astype(BF16)

    def whole_cols(a, axis):
        return lax.all_gather(a, "col", axis=axis, tiled=True) if lo > 1 else a

    x = jnp.transpose(tokens.reshape(seq, width))
    grad = jnp.transpose(out_grad.reshape(seq, width))
    onehot = jnp.asarray(bucket_onehot(seq))
    where = jnp.stack((lengths.reshape(()), core, x_bit, y_bit, row)).astype(jnp.int32)
    gain_one = jnp.broadcast_to(attn_gain.reshape(width, 1), (width, 128))
    gain_two = jnp.broadcast_to(ffn_gain.reshape(width, 1), (width, 128))
    bias = jnp.pad(jnp.transpose(rel_bias), ((0, 8 - HEADS), (0, 0)))

    shard = inner // (2 * n_row)
    proj = jnp.where(quarter == 0, w_query, jnp.where(quarter == 1, w_key, w_value))
    own = jnp.where(quarter == 3, w_attn_out, jnp.transpose(proj))
    if lo > 1:
        own = lax.dynamic_slice_in_dim(whole_cols(own, 0), y_bit * shard, shard, 0)
    unit = jnp.concatenate([own] + [send_row(own, k) for k in range(1, n_row)], axis=0)
    grad_two, grad_one = send_first(grad), send_second(grad)
    unit = after(unit, grad_two, grad_one, gain_one, gain_two)
    unit_two, unit_one = send_first(unit), send_second(unit)
    unit_three = send_second(unit_two)
    near_units = [unit, unit_one, unit_two, unit_three]
    units = near_units + [send_core(u) for u in near_units]
    grad_three = send_second(after(grad_two, unit_three))
    near_grads = [grad, grad_one, grad_two, grad_three]
    grads = near_grads + [send_core(g) for g in near_grads]

    hidden = w_gate.shape[1] * lo // 4
    start = quarter * hidden + (y_bit * 4 * hidden if lo > 1 else 0)
    ffn_own = jnp.concatenate(
        (
            lax.dynamic_slice_in_dim(whole_cols(w_gate, 1), start, hidden, 1),
            lax.dynamic_slice_in_dim(whole_cols(w_up, 1), start, hidden, 1),
            jnp.transpose(lax.dynamic_slice_in_dim(whole_cols(w_down, 0), start, hidden, 0)),
            jnp.zeros((w_gate.shape[0], -3 * hidden % 128), BF16),
        ),
        axis=1,
    )
    ffn_weights = lax.all_gather(after(ffn_own, unit), "row", axis=0, tiled=True)

    weights, residual, normed_one, normed_two, qkv, context, probs = attention_forward(
        where, x, gain_one, gain_two, bias, onehot, units, n_row
    )
    normed_two = after(normed_two, grad_three)
    two, one = send_first(normed_two), send_second(normed_two)
    three = send_second(after(two, one))
    near_normed = [normed_two, one, two, three]
    normed = near_normed + [send_core(a) for a in near_normed]

    gated, hidden_grads, back = feed_forward(normed, grads, ffn_weights, hidden)

    near = {p: add(back[p], send_core(back[4 + p])) for p in (3, 1, 2, 0)}
    from_three, from_one = send_second(near[3]), send_second(near[1])
    ffn_grads, branch = weight_grads(
        normed, grads, gated, hidden_grads, after(ffn_weights, near[3], near[1])
    )
    near[2] = add(after(near[2], branch[0], from_one), from_three)
    from_two = send_first(near[2])
    back_parts = near[0], from_one, from_two
    ffn_grads = lax.psum_scatter(ffn_grads, "row", scatter_dimension=0, tiled=True)

    near = {p: add(branch[p], send_core(branch[4 + p])) for p in (1, 3, 2, 0)}
    branch_one = send_second(after(near[1], *back_parts))
    branch_three = send_second(after(near[3], *back_parts))

    near_grads, far_grads, tokens_grad, small = attention_backward(
        where,
        x,
        gain_one,
        gain_two,
        onehot,
        grad,
        back_parts,
        (weights, residual, normed_one, qkv, context, probs),
        n_row,
    )
    summed = add(near_grads, send_core(after(far_grads, branch_one, branch_three)))
    quad = [summed[p * n_row : (p + 1) * n_row] for p in range(4)]
    from_one = send_second(quad[1])
    from_three = send_second(quad[3])
    from_two = send_first(add(quad[2], from_three))
    mine = (quad[0].astype(F32) + from_one.astype(F32) + from_two.astype(F32)).astype(BF16)
    branch_two = send_first(after(add(near[2], branch_three), mine))
    if one_group:
        small = small + send_core(small)
        small = small + send_first(small)
        small = small + send_second(small)
        extra = small.astype(BF16)
    else:
        small = lax.psum(small, ("dp", "row", "col"))
        extra = jnp.zeros(small.shape, BF16)
    got = [
        send_row(jnp.concatenate((mine[k], extra), axis=0), k).astype(F32) for k in range(1, n_row)
    ]
    attn_grad = mine[0].astype(F32) + sum(a[:shard] for a in got)
    attn_grad = after(attn_grad.astype(BF16), branch_two)
    small = small + sum(a[shard:] for a in got)
    layer_out = (
        residual + near[0].astype(F32) + branch_one.astype(F32) + branch_two.astype(F32)
    ).astype(BF16)

    def quarters(a):
        two = lax.ppermute(a, "dp", [(d, d ^ 2) for d in range(n_dp)])
        return [a, send_core(a), two, send_core(two)]

    def gather_quarters(a):
        placed = lax.dynamic_update_index_in_dim(jnp.zeros((4, *a.shape), a.dtype), a, quarter, 0)
        return lax.psum(placed, "dp")

    def own_cols(a):
        placed = jnp.zeros((n_col, *a.shape[1:]), a.dtype)
        placed = lax.dynamic_update_slice_in_dim(placed, a, y_bit * lo, 0)
        return lax.psum_scatter(placed, "col", scatter_dimension=0, tiled=False)

    if one_group:
        ffn_grads = after(ffn_grads, attn_grad)
        gate_grad, up_grad, down_grads = join_quarters(where, quarters(ffn_grads), hidden)
        parts = quarters(attn_grad)
        attn_grads = []
        for m in range(4):
            picked = parts[3]
            for r in range(3):
                picked = jnp.where(quarter == m ^ r, parts[r], picked)
            attn_grads.append(picked)
    else:
        ffn_grads = gather_quarters(ffn_grads)[:, :, : 3 * hidden].reshape(4, width // n_row, 3, hidden)
        ffn_grads = jnp.transpose(ffn_grads, (2, 1, 0, 3)).reshape(3, width // n_row, lo, 4 * hidden // lo)
        ffn_grads = own_cols(jnp.transpose(ffn_grads, (2, 0, 1, 3))).astype(F32)
        gate_grad, up_grad, down_grads = ffn_grads[0], ffn_grads[1], ffn_grads[2]
        attn_grads = gather_quarters(attn_grad).reshape(4, lo, shard // lo, width)
        attn_grads = own_cols(jnp.transpose(attn_grads, (1, 0, 2, 3)))
    attn_grads = [attn_grads[m].astype(F32) for m in range(4)]

    place = row * n_col + col
    gain_cols, table_rows = width // (n_row * n_col), BUCKETS // (n_row * n_col)
    gain_grads = lax.dynamic_slice_in_dim(small[:2], place * gain_cols, gain_cols, 1)
    table_grad = jnp.transpose(small[8 : 8 + HEADS, :BUCKETS])
    table_grad = lax.dynamic_slice_in_dim(table_grad, place * table_rows, table_rows, 0)
    return (
        jnp.transpose(layer_out).reshape(tokens.shape),
        jnp.transpose(tokens_grad).reshape(tokens.shape),
        gain_grads[0],
        gain_grads[1],
        jnp.transpose(attn_grads[0]),
        jnp.transpose(attn_grads[1]),
        jnp.transpose(attn_grads[2]),
        attn_grads[3],
        table_grad,
        gate_grad,
        up_grad,
        jnp.transpose(down_grads),
    )


def solution(mesh):
    sizes = tuple(mesh.shape[name] for name in ("dp", "row", "col"))
    placed = (
        P(("dp", "col"), "row", None, None),
        P(("dp", "col"), "row"),
        P(),
        P(),
        P(None, ("row", "col")),
        P(None, ("row", "col")),
        P(None, ("row", "col")),
        P(("row", "col"), None),
        P(),
        P("row", "col"),
        P("row", "col"),
        P("col", "row"),
        P(("dp", "col"), "row", None, None),
    )
    return jax.shard_map(
        functools.partial(local, sizes),
        mesh=mesh,
        in_specs=placed,
        out_specs=(
            P(("dp", "col"), "row", None, None),
            P(("dp", "col"), "row", None, None),
            P(("row", "col")),
            P(("row", "col")),
            P(None, ("row", "col")),
            P(None, ("row", "col")),
            P(None, ("row", "col")),
            P(("row", "col"), None),
            P(("row", "col"), None),
            P("row", "col"),
            P("row", "col"),
            P("col", "row"),
        ),
        check_vma=False,
    )
```

```python
import functools

import jax
import jax.numpy as jnp
import numpy as np
from jax import lax
from jax.experimental import pallas as pl
from jax.experimental.pallas import tpu as pltpu
from jax.sharding import PartitionSpec as P

HEADS = 6
DKV = 64
BUCKETS = 32
MAX_DIST = 128
EPSILON = 1e-06
HIGHEST = lax.Precision.HIGHEST
F32 = jnp.float32
BF16 = jnp.bfloat16
VMEM_LIMIT = 56 * 1024 * 1024


def bucket_table(length):
    offsets = np.arange(-(length - 1), length)
    half_count = BUCKETS // 2
    exact_count = half_count // 2
    upper_half = (offsets > 0).astype(np.int64) * half_count
    distance = np.abs(offsets)
    safe_distance = np.maximum(distance, 1)
    spread = (
        np.log(safe_distance / exact_count)
        / np.log(MAX_DIST / exact_count)
        * (half_count - exact_count)
    )
    far_bucket = np.minimum(
        exact_count + np.floor(np.maximum(spread, 0.0)).astype(np.int64), half_count - 1
    )
    return (upper_half + np.where(distance < exact_count, distance, far_bucket)).astype(np.int32)


def bucket_onehot(length):
    onehot = np.zeros((BUCKETS, 2 * length), np.float32)
    offsets = np.arange(-(length - 1), length)
    onehot[bucket_table(length), (-offsets) % (2 * length)] = 1.0
    return onehot


def dot(a, b, dims, precision=None):
    return lax.dot_general(a, b, (dims, ((), ())), precision=precision, preferred_element_type=F32)


NN = ((1,), (0,))
NT = ((1,), (1,))
TN = ((0,), (0,))


def vmem_spec():
    return pl.BlockSpec(memory_space=pltpu.VMEM)


def any_spec():
    return pl.BlockSpec(memory_space=pl.ANY)


def wide(column, width):
    return jnp.concatenate([column] * (width // column.shape[1]), axis=1)


def attention_forward_kernel(
    where_ref, x_ref, gain_one_ref, gain_two_ref, bias_ref, onehot_ref, *rest, n_row, shard
):
    units = rest[:8]
    (weights_ref, residual_ref, normed_one_ref, normed_two_ref, qkv_ref, context_ref, probs_ref, sems) = rest[8:]
    length, core, x_bit, y_bit, z_index = (where_ref[k] for k in range(5))
    inner = HEADS * DKV
    seq = x_ref.shape[1]
    copies = []
    for unit in range(8):
        far, one, two = unit >> 2, (unit >> 1) & 1, unit & 1
        own_core = core ^ far
        x_shift = jnp.where(own_core == 0, one, two)
        y_shift = jnp.where(own_core == 0, two, one)
        matrix = (x_bit ^ x_shift) * 2 + own_core
        side = y_bit ^ y_shift
        for k in range(n_row):
            z_from = lax.rem(z_index - k + n_row, n_row)
            start = pl.multiple_of(matrix * inner + (z_from * 2 + side) * shard, 16)
            copy = pltpu.make_async_copy(
                units[unit].at[pl.ds(k * shard, shard)],
                weights_ref.at[pl.ds(start, shard)],
                sems.at[unit, k],
            )
            copy.start()
            copies.append(copy)
    x = x_ref[...].astype(F32)
    inverse = lax.rsqrt(jnp.mean(x * x, axis=0, keepdims=True) + EPSILON)
    normed = (x * inverse * wide(gain_one_ref[...], seq)).astype(BF16)
    normed_one_ref[...] = normed
    per_offset = dot(bias_ref[...], onehot_ref[...], NN, HIGHEST)
    key_valid = lax.broadcasted_iota(jnp.int32, (seq, seq), 0) < length
    for copy in copies:
        copy.wait()
    for m in range(3):
        qkv_ref[m] = dot(weights_ref[m * inner : (m + 1) * inner, :], normed, NN).astype(BF16)
    for h in range(HEADS):
        rows = slice(h * DKV, (h + 1) * DKV)
        row = jnp.broadcast_to(per_offset[h : h + 1, :], (seq, 2 * seq))
        bias = pltpu.roll(row, 0, 1, stride=1, stride_axis=0)[:, :seq]
        scores = dot(qkv_ref[1, rows, :], qkv_ref[0, rows, :], TN) + bias
        scores = jnp.where(key_valid, scores, -1e30)
        weights = jnp.exp(scores - jnp.max(scores, axis=0, keepdims=True))
        probs = weights / jnp.sum(weights, axis=0, keepdims=True)
        probs_ref[h] = probs
        context_ref[rows, :] = dot(qkv_ref[2, rows, :], probs.astype(BF16), NN).astype(BF16)
    residual = x + dot(weights_ref[3 * inner :, :], context_ref[...], TN)
    residual_ref[...] = residual
    inverse_two = lax.rsqrt(jnp.mean(residual * residual, axis=0, keepdims=True) + EPSILON)
    normed_two_ref[...] = (residual * inverse_two * wide(gain_two_ref[...], seq)).astype(BF16)


def attention_forward(where, x, gain_one, gain_two, bias, onehot, units, n_row):
    width, seq = x.shape
    inner = HEADS * DKV
    return pl.pallas_call(
        functools.partial(attention_forward_kernel, n_row=n_row, shard=inner // (2 * n_row)),
        out_shape=(
            jax.ShapeDtypeStruct((4 * inner, width), BF16),
            jax.ShapeDtypeStruct((width, seq), F32),
            jax.ShapeDtypeStruct((width, seq), BF16),
            jax.ShapeDtypeStruct((width, seq), BF16),
            jax.ShapeDtypeStruct((3, inner, seq), BF16),
            jax.ShapeDtypeStruct((inner, seq), BF16),
            jax.ShapeDtypeStruct((HEADS, seq, seq), F32),
        ),
        in_specs=[pl.BlockSpec(memory_space=pltpu.SMEM)] + [vmem_spec()] * 5 + [any_spec()] * 8,
        out_specs=(vmem_spec(),) * 7,
        scratch_shapes=[pltpu.SemaphoreType.DMA((8, n_row))],
        compiler_params=pltpu.CompilerParams(vmem_limit_bytes=VMEM_LIMIT),
        cost_estimate=pl.CostEstimate(flops=8_000_000_000, bytes_accessed=16_000_000, transcendentals=400_000),
        name="attention_forward",
    )(where, x, gain_one, gain_two, bias, onehot, *units)


def attention_backward_kernel(
    where_ref,
    x_ref,
    gain_one_ref,
    gain_two_ref,
    onehot_ref,
    out_grad_ref,
    part_a_ref,
    part_b_ref,
    part_c_ref,
    weights_ref,
    residual_ref,
    normed_one_ref,
    qkv_ref,
    context_ref,
    probs_ref,
    near_ref,
    far_ref,
    tokens_grad_ref,
    small_ref,
    grads_ref,
    *,
    n_row,
    shard,
):
    _, core, x_bit, y_bit, z_index = (where_ref[k] for k in range(5))
    inner = HEADS * DKV
    seq = x_ref.shape[1]
    width = x_ref.shape[0]
    ones = jnp.ones((8, seq), F32)

    def store_weight_grad(matrix, grad):
        grad = grad.astype(BF16)
        target_core = matrix & 1
        x_shift = (matrix >> 1) ^ x_bit
        for side in range(2):
            y_shift = side ^ y_bit
            if target_core == 0:
                unit = x_shift * 2 + y_shift
            else:
                unit = y_shift * 2 + x_shift
            for z in range(n_row):
                slot = unit * n_row + lax.rem(z - z_index + n_row, n_row)
                start = (z * 2 + side) * shard
                block = grad[start : start + shard, :]

                @pl.when(core == target_core)
                def _():
                    near_ref[slot] = block

                @pl.when(core != target_core)
                def _():
                    far_ref[slot] = block

    residual = residual_ref[...]
    grad_normed = (
        part_a_ref[...].astype(F32) + part_b_ref[...].astype(F32) + part_c_ref[...].astype(F32)
    )
    inverse_two = lax.rsqrt(jnp.mean(residual * residual, axis=0, keepdims=True) + EPSILON)
    gained = grad_normed * wide(gain_two_ref[...], seq)
    ffn_gain_grad = dot(ones, grad_normed * residual * inverse_two, NT, HIGHEST)
    grad_residual = (
        out_grad_ref[...].astype(F32)
        + inverse_two * gained
        - residual
        * (inverse_two * inverse_two * inverse_two * jnp.mean(gained * residual, axis=0, keepdims=True))
    )
    grad_attended = grad_residual.astype(BF16)
    store_weight_grad(3, dot(context_ref[...], grad_attended, NT))
    grad_context = dot(weights_ref[3 * inner :, :], grad_attended, NN).astype(BF16)
    flip = (
        lax.broadcasted_iota(jnp.int32, (seq, seq), 0)
        + lax.broadcasted_iota(jnp.int32, (seq, seq), 1)
        == seq - 1
    ).astype(BF16)
    zero_half = jnp.zeros((seq, seq), F32)
    diagonals = []
    for h in range(HEADS):
        rows = slice(h * DKV, (h + 1) * DKV)
        probs = probs_ref[h]
        grad_head = grad_context[rows, :]
        grads_ref[2, rows, :] = dot(grad_head, probs.astype(BF16), NT).astype(BF16)
        grad_probs = dot(qkv_ref[2, rows, :], grad_head, TN)
        grad_scores = (
            probs * (grad_probs - jnp.sum(probs * grad_probs, axis=0, keepdims=True))
        ).astype(BF16)
        grads_ref[0, rows, :] = dot(qkv_ref[1, rows, :], grad_scores, NN).astype(BF16)
        grads_ref[1, rows, :] = dot(qkv_ref[0, rows, :], grad_scores, NT).astype(BF16)
        flipped = jnp.concatenate((dot(flip, grad_scores, NN), zero_half), axis=1)
        rolled = pltpu.roll(flipped, seq + 1, 1, stride=1, stride_axis=0)
        diagonals.append(jnp.sum(rolled, axis=0, keepdims=True))
    diagonals.append(jnp.zeros((8 - HEADS, 2 * seq), F32))
    table = dot(jnp.concatenate(diagonals, axis=0), onehot_ref[...], NT, HIGHEST)
    normed_one = normed_one_ref[...]
    grad_normed_one = None
    for m in range(3):
        store_weight_grad(m, dot(grads_ref[m], normed_one, NT))
        part = dot(weights_ref[m * inner : (m + 1) * inner, :], grads_ref[m], TN)
        grad_normed_one = part if grad_normed_one is None else grad_normed_one + part
    x = x_ref[...].astype(F32)
    inverse_one = lax.rsqrt(jnp.mean(x * x, axis=0, keepdims=True) + EPSILON)
    gained_one = grad_normed_one * wide(gain_one_ref[...], seq)
    attn_gain_grad = dot(ones, grad_normed_one * x * inverse_one, NT, HIGHEST)
    tokens_grad_ref[...] = (
        grad_residual
        + inverse_one * gained_one
        - x * (inverse_one * inverse_one * inverse_one * jnp.mean(gained_one * x, axis=0, keepdims=True))
    ).astype(BF16)
    small_ref[0:8, :] = jnp.where(
        lax.broadcasted_iota(jnp.int32, (8, width), 0) == 0, attn_gain_grad, ffn_gain_grad
    )
    small_ref[8:16, :] = jnp.concatenate((table, jnp.zeros((8, width - BUCKETS), F32)), axis=1)


def attention_backward(where, x, gain_one, gain_two, onehot, out_grad, parts, saved, n_row):
    width, seq = x.shape
    inner = HEADS * DKV
    shard = inner // (2 * n_row)
    return pl.pallas_call(
        functools.partial(attention_backward_kernel, n_row=n_row, shard=shard),
        out_shape=(
            jax.ShapeDtypeStruct((4 * n_row, shard, width), BF16),
            jax.ShapeDtypeStruct((4 * n_row, shard, width), BF16),
            jax.ShapeDtypeStruct((width, seq), BF16),
            jax.ShapeDtypeStruct((16, width), F32),
        ),
        in_specs=[pl.BlockSpec(memory_space=pltpu.SMEM)] + [vmem_spec()] * 14,
        out_specs=(vmem_spec(),) * 4,
        scratch_shapes=[pltpu.VMEM((3, inner, seq), BF16)],
        compiler_params=pltpu.CompilerParams(vmem_limit_bytes=VMEM_LIMIT),
        cost_estimate=pl.CostEstimate(flops=12_000_000_000, bytes_accessed=20_000_000, transcendentals=1000),
        name="attention_backward",
    )(where, x, gain_one, gain_two, onehot, out_grad, *parts, *saved)


GELU_SCALE = float(np.sqrt(2.0 / np.pi))


def feed_forward_kernel(*refs, count):
    normed_refs, grad_refs = refs[:count], refs[count : 2 * count]
    weights_ref = refs[2 * count]
    outs = refs[2 * count + 1 :]
    gated_refs, hidden_refs, back_refs = (outs[k * count : (k + 1) * count] for k in range(3))
    turned, normed, grads, grads_in = outs[3 * count :]
    hidden, rows = gated_refs[0].shape
    turned[...] = weights_ref[...].T
    halves = (slice(0, rows), slice(rows, 2 * rows))
    for b in range(0, count, 2):
        for i, at in enumerate(halves):
            normed[:, at] = normed_refs[b + i][...]
            grads[:, at] = grad_refs[b + i][...]
        both = dot(turned[: 2 * hidden], normed[...], NN)
        gate, up = both[:hidden], both[hidden:]
        grad_gated = dot(turned[2 * hidden : 3 * hidden], grads[...], NN)
        square = gate * gate
        tanh = jnp.tanh(GELU_SCALE * gate * (1.0 + 0.044715 * square))
        half = 0.5 * (1.0 + tanh)
        gelu = gate * half
        slope = half + (0.5 * GELU_SCALE) * gate * (1.0 - tanh * tanh) * (1.0 + 3 * 0.044715 * square)
        gated = (gelu * up).astype(BF16)
        grad_gate = (grad_gated * up * slope).astype(BF16)
        grad_up = (grad_gated * gelu).astype(BF16)
        grads_in[:hidden] = grad_gate
        grads_in[hidden:] = grad_up
        back = dot(weights_ref[:, : 2 * hidden], grads_in[...], NN).astype(BF16)
        for i, at in enumerate(halves):
            gated_refs[b + i][...] = gated[:, at]
            hidden_refs[b + i][:hidden, :] = grad_gate[:, at]
            hidden_refs[b + i][hidden:, :] = grad_up[:, at]
            back_refs[b + i][...] = back[:, at]


def feed_forward(normed, grads, weights, hidden):
    count = len(normed)
    width, rows = normed[0].shape
    outs = pl.pallas_call(
        functools.partial(feed_forward_kernel, count=count),
        out_shape=[jax.ShapeDtypeStruct((hidden, rows), BF16)] * count
        + [jax.ShapeDtypeStruct((2 * hidden, rows), BF16)] * count
        + [jax.ShapeDtypeStruct((width, rows), BF16)] * count,
        in_specs=[vmem_spec()] * (2 * count + 1),
        out_specs=[vmem_spec()] * (3 * count),
        scratch_shapes=[
            pltpu.VMEM((weights.shape[1], width), BF16),
            pltpu.VMEM((width, 2 * rows), BF16),
            pltpu.VMEM((width, 2 * rows), BF16),
            pltpu.VMEM((2 * hidden, 2 * rows), BF16),
        ],
        compiler_params=pltpu.CompilerParams(vmem_limit_bytes=VMEM_LIMIT),
        cost_estimate=pl.CostEstimate(
            flops=16 * count * rows * width * hidden,
            bytes_accessed=2 * (3 * width * hidden + count * rows * (3 * width + 3 * hidden)),
            transcendentals=count * rows * hidden,
        ),
        name="feed_forward",
    )(*normed, *grads, weights)
    return outs[:count], outs[count : 2 * count], outs[2 * count :]


def weight_grads_kernel(*refs, count):
    normed, grads, gated, hidden_grads = (refs[k * count : (k + 1) * count] for k in range(4))
    weights_ref, out_ref = refs[4 * count : 4 * count + 2]
    branch = refs[4 * count + 2 : 5 * count + 2]
    normed_all, grads_all, gated_all, hidden_all, weights, sums, sent = refs[5 * count + 2 : 5 * count + 9]
    in_sems, weight_sem, sum_sems, sent_sems = refs[5 * count + 9 :]
    rows = gated[0].shape[1]
    hidden = gated[0].shape[0]
    tail = out_ref.shape[1] - 2 * hidden

    def load(k, sources, target):
        copies = [
            pltpu.make_async_copy(sources[b], target.at[:, pl.ds(b * rows, rows)], in_sems.at[k, b])
            for b in range(count)
        ]
        for copy in copies:
            copy.start()
        return copies

    def wait(copies):
        for copy in copies:
            copy.wait()

    stores = []

    def store(source, target, sem):
        copy = pltpu.make_async_copy(source, target, sem)
        copy.start()
        stores.append(copy)

    wait(load(0, hidden_grads, hidden_all) + load(1, normed, normed_all))
    later = load(2, gated, gated_all) + load(3, grads, grads_all)
    later.append(pltpu.make_async_copy(weights_ref.at[:, pl.ds(2 * hidden, tail)], weights, weight_sem))
    later[-1].start()
    sums[:, : 2 * hidden] = dot(normed_all[...], hidden_all[...], NT).astype(BF16)
    store(sums.at[:, pl.ds(0, 2 * hidden)], out_ref.at[:, pl.ds(0, 2 * hidden)], sum_sems.at[0])
    wait(later)
    sums[:, 2 * hidden : 3 * hidden] = dot(grads_all[...], gated_all[...], NT).astype(BF16)
    sums[:, 3 * hidden :] = jnp.zeros((sums.shape[0], tail - hidden), BF16)
    store(sums.at[:, pl.ds(2 * hidden, tail)], out_ref.at[:, pl.ds(2 * hidden, tail)], sum_sems.at[1])
    for b in range(count):
        sent[b] = dot(weights[:, :hidden], gated_all[:, b * rows : (b + 1) * rows], NN).astype(BF16)
        store(sent.at[b], branch[b], sent_sems.at[b])
    wait(stores)


def weight_grads(normed, grads, gated, hidden_grads, weights):
    count = len(grads)
    width, rows = grads[0].shape
    hidden = gated[0].shape[0]
    lanes = weights.shape[1]
    tokens = count * rows
    outs = pl.pallas_call(
        functools.partial(weight_grads_kernel, count=count),
        out_shape=[jax.ShapeDtypeStruct((width, lanes), BF16)]
        + [jax.ShapeDtypeStruct((width, rows), BF16)] * count,
        in_specs=[any_spec()] * (4 * count + 1),
        out_specs=[any_spec()] * (count + 1),
        scratch_shapes=[
            pltpu.VMEM((width, tokens), BF16),
            pltpu.VMEM((width, tokens), BF16),
            pltpu.VMEM((hidden, tokens), BF16),
            pltpu.VMEM((2 * hidden, tokens), BF16),
            pltpu.VMEM((width, lanes - 2 * hidden), BF16),
            pltpu.VMEM((width, lanes), BF16),
            pltpu.VMEM((count, width, rows), BF16),
            pltpu.SemaphoreType.DMA((4, count)),
            pltpu.SemaphoreType.DMA(()),
            pltpu.SemaphoreType.DMA((2,)),
            pltpu.SemaphoreType.DMA((count,)),
        ],
        compiler_params=pltpu.CompilerParams(vmem_limit_bytes=VMEM_LIMIT),
        cost_estimate=pl.CostEstimate(
            flops=14 * tokens * width * hidden,
            bytes_accessed=2 * (6 * width * hidden + 3 * tokens * (width + hidden)),
            transcendentals=0,
        ),
        name="weight_grads",
    )(*normed, *grads, *gated, *hidden_grads, weights)
    return outs[0], outs[1:]


def join_pair_kernel(where_ref, near_ref, far_ref, *refs, other):
    outs, joined, sems = refs[-5:-2], refs[-2], refs[-1]
    own_first = where_ref[1] == 0
    half = where_ref[2] if not other else 1 - where_ref[2]
    cols = outs[0].shape[1] // 4
    at = pl.ds(pl.multiple_of(half * (2 * cols), 128), 2 * cols)
    stores = []
    for m in range(3):
        lanes = slice(m * cols, (m + 1) * cols)
        near, far = near_ref[:, lanes].astype(F32), far_ref[:, lanes].astype(F32)
        joined[m] = jnp.concatenate(
            (jnp.where(own_first, near, far), jnp.where(own_first, far, near)), axis=1
        )
        store = pltpu.make_async_copy(joined.at[m], outs[m].at[:, at], sems.at[m])
        store.start()
        stores.append(store)
    for store in stores:
        store.wait()


def join_pair(where, near, far, cols, held=None):
    rows = near.shape[0]
    held = () if held is None else tuple(held)
    return pl.pallas_call(
        functools.partial(join_pair_kernel, other=len(held) > 0),
        out_shape=[jax.ShapeDtypeStruct((rows, 4 * cols), F32)] * 3,
        in_specs=[pl.BlockSpec(memory_space=pltpu.SMEM)] + [vmem_spec()] * 2 + [any_spec()] * len(held),
        out_specs=[any_spec()] * 3,
        scratch_shapes=[pltpu.VMEM((3, rows, 2 * cols), F32), pltpu.SemaphoreType.DMA((3,))],
        input_output_aliases={3 + m: m for m in range(len(held))},
        compiler_params=pltpu.CompilerParams(vmem_limit_bytes=VMEM_LIMIT),
        cost_estimate=pl.CostEstimate(flops=0, bytes_accessed=6 * rows * cols * 6, transcendentals=0),
        name="join_pair",
    )(where, near, far, *held)


def local(
    sizes,
    tokens,
    lengths,
    attn_gain,
    ffn_gain,
    w_query,
    w_key,
    w_value,
    w_attn_out,
    rel_bias,
    w_gate,
    w_up,
    w_down,
    out_grad,
):
    n_dp, n_row, n_col = sizes
    lo = n_col // 2
    one_group = n_dp == 4 and n_col == 2
    seq, width = tokens.shape[2], tokens.shape[3]
    inner = HEADS * DKV
    dp, row, col = lax.axis_index("dp"), lax.axis_index("row"), lax.axis_index("col")
    core, x_bit, y_bit, quarter = dp % 2, (dp // 2) % 2, col // lo, dp % 4

    first, second = [], []
    for d in range(n_dp):
        for c in range(n_col):
            here, over_x, over_y = d * n_col + c, (d ^ 2) * n_col + c, d * n_col + (c + lo) % n_col
            first.append((here, over_x if d % 2 == 0 else over_y))
            second.append((here, over_y if d % 2 == 0 else over_x))
    swap = [(d, d ^ 1) for d in range(n_dp)]

    def send_first(a):
        return lax.ppermute(a, ("dp", "col"), first)

    def send_second(a):
        return lax.ppermute(a, ("dp", "col"), second)

    def send_core(a):
        return lax.ppermute(a, "dp", swap)

    def send_row(a, k):
        return lax.ppermute(a, "row", [(i, (i + k) % n_row) for i in range(n_row)])

    def after(a, *others):
        return lax.optimization_barrier((a, *others))[0]

    def add(a, b):
        return (a.astype(F32) + b.astype(F32)).astype(BF16)

    def whole_cols(a, axis):
        return lax.all_gather(a, "col", axis=axis, tiled=True) if lo > 1 else a

    x = jnp.transpose(tokens.reshape(seq, width))
    grad = jnp.transpose(out_grad.reshape(seq, width))
    onehot = jnp.asarray(bucket_onehot(seq))
    where = jnp.stack((lengths.reshape(()), core, x_bit, y_bit, row)).astype(jnp.int32)
    gain_one = jnp.broadcast_to(attn_gain.reshape(width, 1), (width, 128))
    gain_two = jnp.broadcast_to(ffn_gain.reshape(width, 1), (width, 128))
    bias = jnp.pad(jnp.transpose(rel_bias), ((0, 8 - HEADS), (0, 0)))

    shard = inner // (2 * n_row)
    proj = jnp.where(quarter == 0, w_query, jnp.where(quarter == 1, w_key, w_value))
    own = jnp.where(quarter == 3, w_attn_out, jnp.transpose(proj))
    if lo > 1:
        own = lax.dynamic_slice_in_dim(whole_cols(own, 0), y_bit * shard, shard, 0)
    others = [send_row(own, k) for k in range(1, n_row)]
    unit = jnp.concatenate([own] + others, axis=0)
    grad_two, grad_one = send_first(grad), send_second(grad)
    unit = after(unit, grad_two, grad_one)
    unit_two, unit_one = send_first(unit), send_second(unit)
    unit_three = send_second(after(unit_two, gain_one, gain_two))
    near_units = [unit, unit_one, unit_two, unit_three]
    units = near_units + [send_core(u) for u in near_units]
    grad_three = send_second(after(grad_two, unit_three))
    near_grads = [grad, grad_one, grad_two, grad_three]
    grads = near_grads + [send_core(g) for g in near_grads]

    hidden = w_gate.shape[1] * lo // 4
    start = quarter * hidden + (y_bit * 4 * hidden if lo > 1 else 0)
    ffn_own = jnp.concatenate(
        (
            lax.dynamic_slice_in_dim(whole_cols(w_gate, 1), start, hidden, 1),
            lax.dynamic_slice_in_dim(whole_cols(w_up, 1), start, hidden, 1),
            jnp.transpose(lax.dynamic_slice_in_dim(whole_cols(w_down, 0), start, hidden, 0)),
            jnp.zeros((w_gate.shape[0], -3 * hidden % 128), BF16),
        ),
        axis=1,
    )
    ffn_weights = lax.all_gather(after(ffn_own, unit), "row", axis=0, tiled=True)

    weights, residual, normed_one, normed_two, qkv, context, probs = attention_forward(
        where, x, gain_one, gain_two, bias, onehot, units, n_row
    )
    normed_two = after(normed_two, grad_three)
    two, one = send_first(normed_two), send_second(normed_two)
    three = send_second(after(two, one))
    near_normed = [normed_two, one, two, three]
    normed = near_normed + [send_core(a) for a in near_normed]

    gated, hidden_grads, back = feed_forward(normed, grads, ffn_weights, hidden)

    near = {p: add(back[p], send_core(back[4 + p])) for p in (3, 1, 2, 0)}
    from_three, from_one = send_second(near[3]), send_second(near[1])
    ffn_grads, branch = weight_grads(
        normed, grads, gated, hidden_grads, after(ffn_weights, near[3], near[1])
    )
    near[2] = add(after(near[2], branch[0], from_one), from_three)
    from_two = send_first(near[2])
    back_parts = near[0], from_one, from_two
    ffn_grads = lax.psum_scatter(ffn_grads, "row", scatter_dimension=0, tiled=True)

    near = {p: add(branch[p], send_core(branch[4 + p])) for p in (3, 1, 2, 0)}
    branch_one = send_second(after(near[1], *back_parts))
    branch_three = send_second(after(near[3], near[2], near[0], *back_parts))

    near_grads, far_grads, tokens_grad, small = attention_backward(
        where,
        x,
        gain_one,
        gain_two,
        onehot,
        grad,
        back_parts,
        (weights, residual, normed_one, qkv, context, probs),
        n_row,
    )
    summed = add(near_grads, send_core(after(far_grads, branch_one, branch_three)))
    quad = [summed[p * n_row : (p + 1) * n_row] for p in range(4)]
    from_one = send_second(quad[1])
    from_three = send_second(quad[3])
    branch_two = send_first(add(near[2], branch_three))
    from_two = send_first(add(after(quad[2], branch_two), from_three))
    mine = (quad[0].astype(F32) + from_one.astype(F32) + from_two.astype(F32)).astype(BF16)
    ffn_grads = after(ffn_grads, mine)
    mine = after(mine, ffn_grads)
    layer_out = (
        residual + near[0].astype(F32) + branch_one.astype(F32) + branch_two.astype(F32)
    ).astype(BF16)
    if one_group:
        small = small + send_core(small)
        small = small + send_first(small)
        small = small + send_second(small)
        extra = small.astype(BF16)
    else:
        small = lax.psum(small, ("dp", "row", "col"))
        extra = jnp.zeros(small.shape, BF16)
    got = [
        send_row(jnp.concatenate((mine[k], extra), axis=0), k).astype(F32) for k in range(1, n_row)
    ]
    attn_grad = mine[0].astype(F32) + sum(a[:shard] for a in got)
    attn_grad = after(attn_grad.astype(BF16), layer_out)
    small = small + sum(a[shard:] for a in got)
    def quarters(a):
        two = lax.ppermute(a, "dp", [(d, d ^ 2) for d in range(n_dp)])
        return [a, send_core(a), two, send_core(two)]

    def gather_quarters(a):
        placed = lax.dynamic_update_index_in_dim(jnp.zeros((4, *a.shape), a.dtype), a, quarter, 0)
        return lax.psum(placed, "dp")

    def own_cols(a):
        placed = jnp.zeros((n_col, *a.shape[1:]), a.dtype)
        placed = lax.dynamic_update_slice_in_dim(placed, a, y_bit * lo, 0)
        return lax.psum_scatter(placed, "col", scatter_dimension=0, tiled=False)

    if one_group:
        two = lax.ppermute(ffn_grads, "dp", [(d, d ^ 2) for d in range(n_dp)])
        half = join_pair(where, ffn_grads, send_core(ffn_grads), hidden)
        two = after(two, *half)
        gate_grad, up_grad, down_grads = join_pair(where, two, send_core(two), hidden, half)
        parts = quarters(attn_grad)
        attn_grads = []
        for m in range(4):
            picked = parts[3]
            for r in range(3):
                picked = jnp.where(quarter == m ^ r, parts[r], picked)
            attn_grads.append(picked.astype(F32))
    else:
        ffn_grads = gather_quarters(ffn_grads)[:, :, : 3 * hidden].reshape(4, width // n_row, 3, hidden)
        ffn_grads = jnp.transpose(ffn_grads, (2, 1, 0, 3)).reshape(3, width // n_row, lo, 4 * hidden // lo)
        ffn_grads = own_cols(jnp.transpose(ffn_grads, (2, 0, 1, 3))).astype(F32)
        gate_grad, up_grad, down_grads = ffn_grads[0], ffn_grads[1], ffn_grads[2]
        attn_grads = gather_quarters(attn_grad).reshape(4, lo, shard // lo, width)
        attn_grads = own_cols(jnp.transpose(attn_grads, (1, 0, 2, 3)))
    attn_grads = [attn_grads[m].astype(F32) for m in range(4)]

    place = row * n_col + col
    gain_cols, table_rows = width // (n_row * n_col), BUCKETS // (n_row * n_col)
    gain_grads = lax.dynamic_slice_in_dim(small[:2], place * gain_cols, gain_cols, 1)
    table_grad = jnp.transpose(small[8 : 8 + HEADS, :BUCKETS])
    table_grad = lax.dynamic_slice_in_dim(table_grad, place * table_rows, table_rows, 0)
    return (
        jnp.transpose(layer_out).reshape(tokens.shape),
        jnp.transpose(tokens_grad).reshape(tokens.shape),
        gain_grads[0],
        gain_grads[1],
        jnp.transpose(attn_grads[0]),
        jnp.transpose(attn_grads[1]),
        jnp.transpose(attn_grads[2]),
        attn_grads[3],
        table_grad,
        gate_grad,
        up_grad,
        jnp.transpose(down_grads),
    )


def solution(mesh):
    sizes = tuple(mesh.shape[name] for name in ("dp", "row", "col"))
    placed = (
        P(("dp", "col"), "row", None, None),
        P(("dp", "col"), "row"),
        P(),
        P(),
        P(None, ("row", "col")),
        P(None, ("row", "col")),
        P(None, ("row", "col")),
        P(("row", "col"), None),
        P(),
        P("row", "col"),
        P("row", "col"),
        P("col", "row"),
        P(("dp", "col"), "row", None, None),
    )
    return jax.shard_map(
        functools.partial(local, sizes),
        mesh=mesh,
        in_specs=placed,
        out_specs=(
            P(("dp", "col"), "row", None, None),
            P(("dp", "col"), "row", None, None),
            P(("row", "col")),
            P(("row", "col")),
            P(None, ("row", "col")),
            P(None, ("row", "col")),
            P(None, ("row", "col")),
            P(("row", "col"), None),
            P(("row", "col"), None),
            P("row", "col"),
            P("row", "col"),
            P("col", "row"),
        ),
        check_vma=False,
    )
```

```python
import functools

import jax
import jax.numpy as jnp
import numpy as np
from jax import lax
from jax.experimental import pallas as pl
from jax.experimental.pallas import tpu as pltpu
from jax.sharding import PartitionSpec as P

HEADS = 6
DKV = 64
BUCKETS = 32
MAX_DIST = 128
EPSILON = 1e-06
HIGHEST = lax.Precision.HIGHEST
F32 = jnp.float32
BF16 = jnp.bfloat16
VMEM_LIMIT = 56 * 1024 * 1024


def bucket_table(length):
    offsets = np.arange(-(length - 1), length)
    half_count = BUCKETS // 2
    exact_count = half_count // 2
    upper_half = (offsets > 0).astype(np.int64) * half_count
    distance = np.abs(offsets)
    safe_distance = np.maximum(distance, 1)
    spread = (
        np.log(safe_distance / exact_count)
        / np.log(MAX_DIST / exact_count)
        * (half_count - exact_count)
    )
    far_bucket = np.minimum(
        exact_count + np.floor(np.maximum(spread, 0.0)).astype(np.int64), half_count - 1
    )
    return (upper_half + np.where(distance < exact_count, distance, far_bucket)).astype(np.int32)


def bucket_onehot(length):
    onehot = np.zeros((BUCKETS, 2 * length), np.float32)
    offsets = np.arange(-(length - 1), length)
    onehot[bucket_table(length), (-offsets) % (2 * length)] = 1.0
    return onehot


def dot(a, b, dims, precision=None):
    return lax.dot_general(a, b, (dims, ((), ())), precision=precision, preferred_element_type=F32)


NN = ((1,), (0,))
NT = ((1,), (1,))
TN = ((0,), (0,))


def vmem_spec():
    return pl.BlockSpec(memory_space=pltpu.VMEM)


def any_spec():
    return pl.BlockSpec(memory_space=pl.ANY)


def wide(column, width):
    return jnp.concatenate([column] * (width // column.shape[1]), axis=1)


def attention_forward_kernel(
    where_ref, x_ref, gain_one_ref, gain_two_ref, bias_ref, onehot_ref, *rest, n_row, shard
):
    units = rest[:8]
    (weights_ref, residual_ref, normed_one_ref, normed_two_ref, qkv_ref, context_ref, probs_ref, sems) = rest[8:]
    length, core, x_bit, y_bit, z_index = (where_ref[k] for k in range(5))
    inner = HEADS * DKV
    seq = x_ref.shape[1]
    copies = []
    for unit in range(8):
        far, one, two = unit >> 2, (unit >> 1) & 1, unit & 1
        own_core = core ^ far
        x_shift = jnp.where(own_core == 0, one, two)
        y_shift = jnp.where(own_core == 0, two, one)
        matrix = (x_bit ^ x_shift) * 2 + own_core
        side = y_bit ^ y_shift
        for k in range(n_row):
            z_from = lax.rem(z_index - k + n_row, n_row)
            start = pl.multiple_of(matrix * inner + (z_from * 2 + side) * shard, 16)
            copy = pltpu.make_async_copy(
                units[unit].at[pl.ds(k * shard, shard)],
                weights_ref.at[pl.ds(start, shard)],
                sems.at[unit, k],
            )
            copy.start()
            copies.append(copy)
    x = x_ref[...].astype(F32)
    inverse = lax.rsqrt(jnp.mean(x * x, axis=0, keepdims=True) + EPSILON)
    normed = (x * inverse * wide(gain_one_ref[...], seq)).astype(BF16)
    normed_one_ref[...] = normed
    per_offset = dot(bias_ref[...], onehot_ref[...], NN, HIGHEST)
    key_valid = lax.broadcasted_iota(jnp.int32, (seq, seq), 0) < length
    for copy in copies:
        copy.wait()
    for m in range(3):
        qkv_ref[m] = dot(weights_ref[m * inner : (m + 1) * inner, :], normed, NN).astype(BF16)
    for h in range(HEADS):
        rows = slice(h * DKV, (h + 1) * DKV)
        row = jnp.broadcast_to(per_offset[h : h + 1, :], (seq, 2 * seq))
        bias = pltpu.roll(row, 0, 1, stride=1, stride_axis=0)[:, :seq]
        scores = dot(qkv_ref[1, rows, :], qkv_ref[0, rows, :], TN) + bias
        scores = jnp.where(key_valid, scores, -1e30)
        weights = jnp.exp(scores - jnp.max(scores, axis=0, keepdims=True))
        probs = weights / jnp.sum(weights, axis=0, keepdims=True)
        probs_ref[h] = probs
        context_ref[rows, :] = dot(qkv_ref[2, rows, :], probs.astype(BF16), NN).astype(BF16)
    residual = x + dot(weights_ref[3 * inner :, :], context_ref[...], TN)
    residual_ref[...] = residual
    inverse_two = lax.rsqrt(jnp.mean(residual * residual, axis=0, keepdims=True) + EPSILON)
    normed_two_ref[...] = (residual * inverse_two * wide(gain_two_ref[...], seq)).astype(BF16)


def attention_forward(where, x, gain_one, gain_two, bias, onehot, units, n_row):
    width, seq = x.shape
    inner = HEADS * DKV
    return pl.pallas_call(
        functools.partial(attention_forward_kernel, n_row=n_row, shard=inner // (2 * n_row)),
        out_shape=(
            jax.ShapeDtypeStruct((4 * inner, width), BF16),
            jax.ShapeDtypeStruct((width, seq), F32),
            jax.ShapeDtypeStruct((width, seq), BF16),
            jax.ShapeDtypeStruct((width, seq), BF16),
            jax.ShapeDtypeStruct((3, inner, seq), BF16),
            jax.ShapeDtypeStruct((inner, seq), BF16),
            jax.ShapeDtypeStruct((HEADS, seq, seq), F32),
        ),
        in_specs=[pl.BlockSpec(memory_space=pltpu.SMEM)] + [vmem_spec()] * 5 + [any_spec()] * 8,
        out_specs=(vmem_spec(),) * 7,
        scratch_shapes=[pltpu.SemaphoreType.DMA((8, n_row))],
        compiler_params=pltpu.CompilerParams(vmem_limit_bytes=VMEM_LIMIT),
        cost_estimate=pl.CostEstimate(flops=8_000_000_000, bytes_accessed=16_000_000, transcendentals=400_000),
        name="attention_forward",
    )(where, x, gain_one, gain_two, bias, onehot, *units)


def attention_backward_kernel(
    where_ref,
    x_ref,
    gain_one_ref,
    gain_two_ref,
    onehot_ref,
    out_grad_ref,
    part_a_ref,
    part_b_ref,
    part_c_ref,
    weights_ref,
    residual_ref,
    normed_one_ref,
    qkv_ref,
    context_ref,
    probs_ref,
    near_ref,
    far_ref,
    tokens_grad_ref,
    small_ref,
    grads_ref,
    *,
    n_row,
    shard,
):
    _, core, x_bit, y_bit, z_index = (where_ref[k] for k in range(5))
    inner = HEADS * DKV
    seq = x_ref.shape[1]
    width = x_ref.shape[0]
    ones = jnp.ones((8, seq), F32)

    def store_weight_grad(matrix, grad):
        grad = grad.astype(BF16)
        target_core = matrix & 1
        x_shift = (matrix >> 1) ^ x_bit
        for side in range(2):
            y_shift = side ^ y_bit
            if target_core == 0:
                unit = x_shift * 2 + y_shift
            else:
                unit = y_shift * 2 + x_shift
            for z in range(n_row):
                slot = unit * n_row + lax.rem(z - z_index + n_row, n_row)
                start = (z * 2 + side) * shard
                block = grad[start : start + shard, :]

                @pl.when(core == target_core)
                def _():
                    near_ref[slot] = block

                @pl.when(core != target_core)
                def _():
                    far_ref[slot] = block

    residual = residual_ref[...]
    grad_normed = (
        part_a_ref[...].astype(F32) + part_b_ref[...].astype(F32) + part_c_ref[...].astype(F32)
    )
    inverse_two = lax.rsqrt(jnp.mean(residual * residual, axis=0, keepdims=True) + EPSILON)
    gained = grad_normed * wide(gain_two_ref[...], seq)
    ffn_gain_grad = dot(ones, grad_normed * residual * inverse_two, NT, HIGHEST)
    grad_residual = (
        out_grad_ref[...].astype(F32)
        + inverse_two * gained
        - residual
        * (inverse_two * inverse_two * inverse_two * jnp.mean(gained * residual, axis=0, keepdims=True))
    )
    grad_attended = grad_residual.astype(BF16)
    store_weight_grad(3, dot(context_ref[...], grad_attended, NT))
    grad_context = dot(weights_ref[3 * inner :, :], grad_attended, NN).astype(BF16)
    flip = (
        lax.broadcasted_iota(jnp.int32, (seq, seq), 0)
        + lax.broadcasted_iota(jnp.int32, (seq, seq), 1)
        == seq - 1
    ).astype(BF16)
    zero_half = jnp.zeros((seq, seq), F32)
    diagonals = []
    for h in range(HEADS):
        rows = slice(h * DKV, (h + 1) * DKV)
        probs = probs_ref[h]
        grad_head = grad_context[rows, :]
        grads_ref[2, rows, :] = dot(grad_head, probs.astype(BF16), NT).astype(BF16)
        grad_probs = dot(qkv_ref[2, rows, :], grad_head, TN)
        grad_scores = (
            probs * (grad_probs - jnp.sum(probs * grad_probs, axis=0, keepdims=True))
        ).astype(BF16)
        grads_ref[0, rows, :] = dot(qkv_ref[1, rows, :], grad_scores, NN).astype(BF16)
        grads_ref[1, rows, :] = dot(qkv_ref[0, rows, :], grad_scores, NT).astype(BF16)
        flipped = jnp.concatenate((dot(flip, grad_scores, NN), zero_half), axis=1)
        rolled = pltpu.roll(flipped, seq + 1, 1, stride=1, stride_axis=0)
        diagonals.append(jnp.sum(rolled, axis=0, keepdims=True))
    diagonals.append(jnp.zeros((8 - HEADS, 2 * seq), F32))
    table = dot(jnp.concatenate(diagonals, axis=0), onehot_ref[...], NT, HIGHEST)
    normed_one = normed_one_ref[...]
    grad_normed_one = None
    for m in range(3):
        store_weight_grad(m, dot(grads_ref[m], normed_one, NT))
        part = dot(weights_ref[m * inner : (m + 1) * inner, :], grads_ref[m], TN)
        grad_normed_one = part if grad_normed_one is None else grad_normed_one + part
    x = x_ref[...].astype(F32)
    inverse_one = lax.rsqrt(jnp.mean(x * x, axis=0, keepdims=True) + EPSILON)
    gained_one = grad_normed_one * wide(gain_one_ref[...], seq)
    attn_gain_grad = dot(ones, grad_normed_one * x * inverse_one, NT, HIGHEST)
    tokens_grad_ref[...] = (
        grad_residual
        + inverse_one * gained_one
        - x * (inverse_one * inverse_one * inverse_one * jnp.mean(gained_one * x, axis=0, keepdims=True))
    ).astype(BF16)
    small_ref[0:8, :] = jnp.where(
        lax.broadcasted_iota(jnp.int32, (8, width), 0) == 0, attn_gain_grad, ffn_gain_grad
    )
    small_ref[8:16, :] = jnp.concatenate((table, jnp.zeros((8, width - BUCKETS), F32)), axis=1)


def attention_backward(where, x, gain_one, gain_two, onehot, out_grad, parts, saved, n_row):
    width, seq = x.shape
    inner = HEADS * DKV
    shard = inner // (2 * n_row)
    return pl.pallas_call(
        functools.partial(attention_backward_kernel, n_row=n_row, shard=shard),
        out_shape=(
            jax.ShapeDtypeStruct((4 * n_row, shard, width), BF16),
            jax.ShapeDtypeStruct((4 * n_row, shard, width), BF16),
            jax.ShapeDtypeStruct((width, seq), BF16),
            jax.ShapeDtypeStruct((16, width), F32),
        ),
        in_specs=[pl.BlockSpec(memory_space=pltpu.SMEM)] + [vmem_spec()] * 14,
        out_specs=(vmem_spec(),) * 4,
        scratch_shapes=[pltpu.VMEM((3, inner, seq), BF16)],
        compiler_params=pltpu.CompilerParams(vmem_limit_bytes=VMEM_LIMIT),
        cost_estimate=pl.CostEstimate(flops=12_000_000_000, bytes_accessed=20_000_000, transcendentals=1000),
        name="attention_backward",
    )(where, x, gain_one, gain_two, onehot, out_grad, *parts, *saved)


GELU_SCALE = float(np.sqrt(2.0 / np.pi))


def feed_forward_kernel(*refs, count, hidden):
    normed_refs, grad_refs = refs[:count], refs[count : 2 * count]
    weights_ref, gated_ref, hidden_ref = refs[2 * count : 2 * count + 3]
    back_refs = refs[2 * count + 3 : 3 * count + 3]
    weights, turned, normed, grads, gated, grads_in, back, weight_sem, in_sems, out_sems, back_sems = refs[
        3 * count + 3 :
    ]
    rows = normed_refs[0].shape[1]
    pairs = count // 2

    def fetch(pair):
        slot = pair % 2
        copies = []
        for k, (sources, target) in enumerate(((normed_refs, normed), (grad_refs, grads))):
            for i in range(2):
                copy = pltpu.make_async_copy(
                    sources[2 * pair + i],
                    target.at[slot, :, pl.ds(i * rows, rows)],
                    in_sems.at[k, 2 * pair + i],
                )
                copy.start()
                copies.append(copy)
        return copies

    load = pltpu.make_async_copy(weights_ref, weights, weight_sem)
    load.start()
    load.wait()
    coming = fetch(0)
    turned[...] = weights[...].T
    stores = []
    for pair in range(pairs):
        slot = pair % 2
        for copy in coming:
            copy.wait()
        if pair + 1 < pairs:
            coming = fetch(pair + 1)
        both = dot(turned[: 2 * hidden], normed[slot], NN)
        gate, up = both[:hidden], both[hidden:]
        grad_gated = dot(turned[2 * hidden : 3 * hidden], grads[slot], NN)
        square = gate * gate
        tanh = jnp.tanh(GELU_SCALE * gate * (1.0 + 0.044715 * square))
        half = 0.5 * (1.0 + tanh)
        gelu = gate * half
        slope = half + (0.5 * GELU_SCALE) * gate * (1.0 - tanh * tanh) * (1.0 + 3 * 0.044715 * square)
        gated[pair] = (gelu * up).astype(BF16)
        grads_in[pair, :hidden] = (grad_gated * up * slope).astype(BF16)
        grads_in[pair, hidden:] = (grad_gated * gelu).astype(BF16)
        back[pair] = dot(weights[:, : 2 * hidden], grads_in[pair], NN).astype(BF16)
        tokens = pl.ds(pair * 2 * rows, 2 * rows)
        made = [
            pltpu.make_async_copy(gated.at[pair], gated_ref.at[:, tokens], out_sems.at[0, pair]),
            pltpu.make_async_copy(grads_in.at[pair], hidden_ref.at[:, tokens], out_sems.at[1, pair]),
        ]
        for i in range(2):
            made.append(
                pltpu.make_async_copy(
                    back.at[pair, :, pl.ds(i * rows, rows)],
                    back_refs[2 * pair + i],
                    back_sems.at[2 * pair + i],
                )
            )
        for copy in made:
            copy.start()
        stores += made
    for copy in stores:
        copy.wait()


def feed_forward(normed, grads, weights, hidden):
    count = len(normed)
    width, rows = normed[0].shape
    tokens, pairs, lanes = count * rows, count // 2, weights.shape[1]
    outs = pl.pallas_call(
        functools.partial(feed_forward_kernel, count=count, hidden=hidden),
        out_shape=[
            jax.ShapeDtypeStruct((hidden, tokens), BF16),
            jax.ShapeDtypeStruct((2 * hidden, tokens), BF16),
        ]
        + [jax.ShapeDtypeStruct((width, rows), BF16)] * count,
        in_specs=[any_spec()] * (2 * count + 1),
        out_specs=[any_spec()] * (count + 2),
        scratch_shapes=[
            pltpu.VMEM((width, lanes), BF16),
            pltpu.VMEM((lanes, width), BF16),
            pltpu.VMEM((2, width, 2 * rows), BF16),
            pltpu.VMEM((2, width, 2 * rows), BF16),
            pltpu.VMEM((pairs, hidden, 2 * rows), BF16),
            pltpu.VMEM((pairs, 2 * hidden, 2 * rows), BF16),
            pltpu.VMEM((pairs, width, 2 * rows), BF16),
            pltpu.SemaphoreType.DMA(()),
            pltpu.SemaphoreType.DMA((2, count)),
            pltpu.SemaphoreType.DMA((2, pairs)),
            pltpu.SemaphoreType.DMA((count,)),
        ],
        compiler_params=pltpu.CompilerParams(vmem_limit_bytes=VMEM_LIMIT),
        cost_estimate=pl.CostEstimate(
            flops=16 * tokens * width * hidden,
            bytes_accessed=2 * (3 * width * hidden + tokens * (3 * width + 3 * hidden)),
            transcendentals=tokens * hidden,
        ),
        name="feed_forward",
    )(*normed, *grads, weights)
    return outs[0], outs[1], outs[2:]


def weight_grads_kernel(*refs, count):
    normed, grads = refs[:count], refs[count : 2 * count]
    gated_ref, hidden_ref, weights_ref, out_ref = refs[2 * count : 2 * count + 4]
    branch = refs[2 * count + 4 : 3 * count + 4]
    normed_all, grads_all, gated_all, hidden_all, weights, sums, sent = refs[3 * count + 4 : 3 * count + 11]
    in_sems, whole_sems, sum_sems, sent_sems = refs[3 * count + 11 :]
    rows = normed[0].shape[1]
    hidden = gated_ref.shape[0]
    tail = out_ref.shape[1] - 2 * hidden

    def start(source, target, sem):
        copy = pltpu.make_async_copy(source, target, sem)
        copy.start()
        return copy

    def load(k, sources, target):
        return [
            start(sources[b], target.at[:, pl.ds(b * rows, rows)], in_sems.at[k, b])
            for b in range(count)
        ]

    def wait(copies):
        for copy in copies:
            copy.wait()

    wait(
        [
            start(gated_ref, gated_all, whole_sems.at[1]),
            start(weights_ref.at[:, pl.ds(2 * hidden, tail)], weights, whole_sems.at[2]),
        ]
    )
    first = [start(hidden_ref, hidden_all, whole_sems.at[0])] + load(0, normed, normed_all)
    for pair in range(count // 2):
        at = slice(2 * pair * rows, 2 * (pair + 1) * rows)
        sent[pair] = dot(weights[:, :hidden], gated_all[:, at], NN).astype(BF16)
    wait(first)
    later = load(1, grads, grads_all)
    stores = [
        start(sent.at[b // 2, :, pl.ds(b % 2 * rows, rows)], branch[b], sent_sems.at[b])
        for b in range(count)
    ]
    sums[:, : 2 * hidden] = dot(normed_all[...], hidden_all[...], NT).astype(BF16)
    stores.append(
        start(sums.at[:, pl.ds(0, 2 * hidden)], out_ref.at[:, pl.ds(0, 2 * hidden)], sum_sems.at[0])
    )
    wait(later)
    sums[:, 2 * hidden : 3 * hidden] = dot(grads_all[...], gated_all[...], NT).astype(BF16)
    sums[:, 3 * hidden :] = jnp.zeros((sums.shape[0], tail - hidden), BF16)
    stores.append(
        start(sums.at[:, pl.ds(2 * hidden, tail)], out_ref.at[:, pl.ds(2 * hidden, tail)], sum_sems.at[1])
    )
    wait(stores)


def weight_grads(normed, grads, gated, hidden_grads, weights):
    count = len(grads)
    width, rows = grads[0].shape
    hidden, tokens = gated.shape
    lanes = weights.shape[1]
    outs = pl.pallas_call(
        functools.partial(weight_grads_kernel, count=count),
        out_shape=[jax.ShapeDtypeStruct((width, lanes), BF16)]
        + [jax.ShapeDtypeStruct((width, rows), BF16)] * count,
        in_specs=[any_spec()] * (2 * count + 3),
        out_specs=[any_spec()] * (count + 1),
        scratch_shapes=[
            pltpu.VMEM((width, tokens), BF16),
            pltpu.VMEM((width, tokens), BF16),
            pltpu.VMEM((hidden, tokens), BF16),
            pltpu.VMEM((2 * hidden, tokens), BF16),
            pltpu.VMEM((width, lanes - 2 * hidden), BF16),
            pltpu.VMEM((width, lanes), BF16),
            pltpu.VMEM((count // 2, width, 2 * rows), BF16),
            pltpu.SemaphoreType.DMA((2, count)),
            pltpu.SemaphoreType.DMA((3,)),
            pltpu.SemaphoreType.DMA((2,)),
            pltpu.SemaphoreType.DMA((count,)),
        ],
        compiler_params=pltpu.CompilerParams(vmem_limit_bytes=VMEM_LIMIT),
        cost_estimate=pl.CostEstimate(
            flops=14 * tokens * width * hidden,
            bytes_accessed=2 * (6 * width * hidden + 3 * tokens * (width + hidden)),
            transcendentals=0,
        ),
        name="weight_grads",
    )(*normed, *grads, gated, hidden_grads, weights)
    return outs[0], outs[1:]


def join_pair_kernel(where_ref, near_ref, far_ref, *refs, other):
    outs, joined, sems = refs[-5:-2], refs[-2], refs[-1]
    own_first = where_ref[1] == 0
    half = where_ref[2] if not other else 1 - where_ref[2]
    cols = outs[0].shape[1] // 4
    at = pl.ds(pl.multiple_of(half * (2 * cols), 128), 2 * cols)
    stores = []
    for m in range(3):
        lanes = slice(m * cols, (m + 1) * cols)
        near, far = near_ref[:, lanes].astype(F32), far_ref[:, lanes].astype(F32)
        joined[m] = jnp.concatenate(
            (jnp.where(own_first, near, far), jnp.where(own_first, far, near)), axis=1
        )
        store = pltpu.make_async_copy(joined.at[m], outs[m].at[:, at], sems.at[m])
        store.start()
        stores.append(store)
    for store in stores:
        store.wait()


def join_pair(where, near, far, cols, held=None):
    rows = near.shape[0]
    held = () if held is None else tuple(held)
    return pl.pallas_call(
        functools.partial(join_pair_kernel, other=len(held) > 0),
        out_shape=[jax.ShapeDtypeStruct((rows, 4 * cols), F32)] * 3,
        in_specs=[pl.BlockSpec(memory_space=pltpu.SMEM)] + [vmem_spec()] * 2 + [any_spec()] * len(held),
        out_specs=[any_spec()] * 3,
        scratch_shapes=[pltpu.VMEM((3, rows, 2 * cols), F32), pltpu.SemaphoreType.DMA((3,))],
        input_output_aliases={3 + m: m for m in range(len(held))},
        compiler_params=pltpu.CompilerParams(vmem_limit_bytes=VMEM_LIMIT),
        cost_estimate=pl.CostEstimate(flops=0, bytes_accessed=6 * rows * cols * 6, transcendentals=0),
        name="join_pair",
    )(where, near, far, *held)


def local(
    sizes,
    tokens,
    lengths,
    attn_gain,
    ffn_gain,
    w_query,
    w_key,
    w_value,
    w_attn_out,
    rel_bias,
    w_gate,
    w_up,
    w_down,
    out_grad,
):
    n_dp, n_row, n_col = sizes
    lo = n_col // 2
    one_group = n_dp == 4 and n_col == 2
    seq, width = tokens.shape[2], tokens.shape[3]
    inner = HEADS * DKV
    dp, row, col = lax.axis_index("dp"), lax.axis_index("row"), lax.axis_index("col")
    core, x_bit, y_bit, quarter = dp % 2, (dp // 2) % 2, col // lo, dp % 4

    first, second = [], []
    for d in range(n_dp):
        for c in range(n_col):
            here, over_x, over_y = d * n_col + c, (d ^ 2) * n_col + c, d * n_col + (c + lo) % n_col
            first.append((here, over_x if d % 2 == 0 else over_y))
            second.append((here, over_y if d % 2 == 0 else over_x))
    swap = [(d, d ^ 1) for d in range(n_dp)]

    def send_first(a):
        return lax.ppermute(a, ("dp", "col"), first)

    def send_second(a):
        return lax.ppermute(a, ("dp", "col"), second)

    def send_core(a):
        return lax.ppermute(a, "dp", swap)

    def send_row(a, k):
        return lax.ppermute(a, "row", [(i, (i + k) % n_row) for i in range(n_row)])

    def after(a, *others):
        return lax.optimization_barrier((a, *others))[0]

    def add(a, b):
        return (a.astype(F32) + b.astype(F32)).astype(BF16)

    def whole_cols(a, axis):
        return lax.all_gather(a, "col", axis=axis, tiled=True) if lo > 1 else a

    x = jnp.transpose(tokens.reshape(seq, width))
    grad = jnp.transpose(out_grad.reshape(seq, width))
    onehot = jnp.asarray(bucket_onehot(seq))
    where = jnp.stack((lengths.reshape(()), core, x_bit, y_bit, row)).astype(jnp.int32)
    gain_one = jnp.broadcast_to(attn_gain.reshape(width, 1), (width, 128))
    gain_two = jnp.broadcast_to(ffn_gain.reshape(width, 1), (width, 128))
    bias = jnp.pad(jnp.transpose(rel_bias), ((0, 8 - HEADS), (0, 0)))

    shard = inner // (2 * n_row)
    proj = jnp.where(quarter == 0, w_query, jnp.where(quarter == 1, w_key, w_value))
    own = jnp.where(quarter == 3, w_attn_out, jnp.transpose(proj))
    if lo > 1:
        own = lax.dynamic_slice_in_dim(whole_cols(own, 0), y_bit * shard, shard, 0)
    others = [send_row(own, k) for k in range(1, n_row)]
    unit = jnp.concatenate([own] + others, axis=0)
    grad_two, grad_one = send_first(grad), send_second(grad)
    unit = after(unit, grad_two, grad_one)
    unit_two, unit_one = send_first(unit), send_second(unit)
    unit_three = send_second(after(unit_two, gain_one, gain_two))
    near_units = [unit, unit_one, unit_two, unit_three]
    units = near_units + [send_core(u) for u in near_units]
    grad_three = send_second(after(grad_two, unit_three))
    near_grads = [grad, grad_one, grad_two, grad_three]
    grads = near_grads + [send_core(g) for g in near_grads]

    hidden = w_gate.shape[1] * lo // 4
    start = quarter * hidden + (y_bit * 4 * hidden if lo > 1 else 0)
    ffn_own = jnp.concatenate(
        (
            lax.dynamic_slice_in_dim(whole_cols(w_gate, 1), start, hidden, 1),
            lax.dynamic_slice_in_dim(whole_cols(w_up, 1), start, hidden, 1),
            jnp.transpose(lax.dynamic_slice_in_dim(whole_cols(w_down, 0), start, hidden, 0)),
            jnp.zeros((w_gate.shape[0], -3 * hidden % 128), BF16),
        ),
        axis=1,
    )
    ffn_weights = lax.all_gather(after(ffn_own, unit), "row", axis=0, tiled=True)

    weights, residual, normed_one, normed_two, qkv, context, probs = attention_forward(
        where, x, gain_one, gain_two, bias, onehot, units, n_row
    )
    normed_two = after(normed_two, grad_three)
    two, one = send_first(normed_two), send_second(normed_two)
    three = send_second(after(two, one))
    near_normed = [normed_two, one, two, three]
    normed = near_normed + [send_core(a) for a in near_normed]

    gated, hidden_grads, back = feed_forward(normed, grads, ffn_weights, hidden)

    near = {p: add(back[p], send_core(back[4 + p])) for p in (3, 1, 2, 0)}
    from_three, from_one = send_second(near[3]), send_second(near[1])
    ffn_grads, branch = weight_grads(
        normed, grads, gated, hidden_grads, after(ffn_weights, near[3], near[1])
    )
    near[2] = add(after(near[2], branch[0], from_one), from_three)
    from_two = send_first(near[2])
    back_parts = near[0], from_one, from_two
    ffn_grads = lax.psum_scatter(ffn_grads, "row", scatter_dimension=0, tiled=True)

    near = {p: add(branch[p], send_core(branch[4 + p])) for p in (3, 1, 2, 0)}
    branch_one = send_second(after(near[1], *back_parts))
    branch_three = send_second(after(near[3], near[2], near[0], *back_parts))

    near_grads, far_grads, tokens_grad, small = attention_backward(
        where,
        x,
        gain_one,
        gain_two,
        onehot,
        grad,
        back_parts,
        (weights, residual, normed_one, qkv, context, probs),
        n_row,
    )
    summed = add(near_grads, send_core(after(far_grads, branch_one, branch_three)))
    quad = [summed[p * n_row : (p + 1) * n_row] for p in range(4)]
    from_one = send_second(quad[1])
    from_three = send_second(quad[3])
    branch_two = send_first(add(near[2], branch_three))
    from_two = send_first(add(after(quad[2], branch_two), from_three))
    mine = (quad[0].astype(F32) + from_one.astype(F32) + from_two.astype(F32)).astype(BF16)
    ffn_grads = after(ffn_grads, mine)
    mine = after(mine, ffn_grads)
    layer_out = (
        residual + near[0].astype(F32) + branch_one.astype(F32) + branch_two.astype(F32)
    ).astype(BF16)
    if one_group:
        small = small + send_core(small)
        small = small + send_first(small)
        small = small + send_second(small)
        extra = small.astype(BF16)
    else:
        small = lax.psum(small, ("dp", "row", "col"))
        extra = jnp.zeros(small.shape, BF16)
    got = [
        send_row(jnp.concatenate((mine[k], extra), axis=0), k).astype(F32) for k in range(1, n_row)
    ]
    attn_grad = mine[0].astype(F32) + sum(a[:shard] for a in got)
    attn_grad = after(attn_grad.astype(BF16), layer_out)
    small = small + sum(a[shard:] for a in got)
    def quarters(a):
        two = lax.ppermute(a, "dp", [(d, d ^ 2) for d in range(n_dp)])
        return [a, send_core(a), two, send_core(two)]

    def gather_quarters(a):
        placed = lax.dynamic_update_index_in_dim(jnp.zeros((4, *a.shape), a.dtype), a, quarter, 0)
        return lax.psum(placed, "dp")

    def own_cols(a):
        placed = jnp.zeros((n_col, *a.shape[1:]), a.dtype)
        placed = lax.dynamic_update_slice_in_dim(placed, a, y_bit * lo, 0)
        return lax.psum_scatter(placed, "col", scatter_dimension=0, tiled=False)

    if one_group:
        two = lax.ppermute(ffn_grads, "dp", [(d, d ^ 2) for d in range(n_dp)])
        half = join_pair(where, ffn_grads, send_core(ffn_grads), hidden)
        two = after(two, *half)
        gate_grad, up_grad, down_grads = join_pair(where, two, send_core(two), hidden, half)
        parts = quarters(attn_grad)
        attn_grads = []
        for m in range(4):
            picked = parts[3]
            for r in range(3):
                picked = jnp.where(quarter == m ^ r, parts[r], picked)
            attn_grads.append(picked.astype(F32))
    else:
        ffn_grads = gather_quarters(ffn_grads)[:, :, : 3 * hidden].reshape(4, width // n_row, 3, hidden)
        ffn_grads = jnp.transpose(ffn_grads, (2, 1, 0, 3)).reshape(3, width // n_row, lo, 4 * hidden // lo)
        ffn_grads = own_cols(jnp.transpose(ffn_grads, (2, 0, 1, 3))).astype(F32)
        gate_grad, up_grad, down_grads = ffn_grads[0], ffn_grads[1], ffn_grads[2]
        attn_grads = gather_quarters(attn_grad).reshape(4, lo, shard // lo, width)
        attn_grads = own_cols(jnp.transpose(attn_grads, (1, 0, 2, 3)))
    attn_grads = [attn_grads[m].astype(F32) for m in range(4)]

    place = row * n_col + col
    gain_cols, table_rows = width // (n_row * n_col), BUCKETS // (n_row * n_col)
    gain_grads = lax.dynamic_slice_in_dim(small[:2], place * gain_cols, gain_cols, 1)
    table_grad = jnp.transpose(small[8 : 8 + HEADS, :BUCKETS])
    table_grad = lax.dynamic_slice_in_dim(table_grad, place * table_rows, table_rows, 0)
    return (
        jnp.transpose(layer_out).reshape(tokens.shape),
        jnp.transpose(tokens_grad).reshape(tokens.shape),
        gain_grads[0],
        gain_grads[1],
        jnp.transpose(attn_grads[0]),
        jnp.transpose(attn_grads[1]),
        jnp.transpose(attn_grads[2]),
        attn_grads[3],
        table_grad,
        gate_grad,
        up_grad,
        jnp.transpose(down_grads),
    )


def solution(mesh):
    sizes = tuple(mesh.shape[name] for name in ("dp", "row", "col"))
    placed = (
        P(("dp", "col"), "row", None, None),
        P(("dp", "col"), "row"),
        P(),
        P(),
        P(None, ("row", "col")),
        P(None, ("row", "col")),
        P(None, ("row", "col")),
        P(("row", "col"), None),
        P(),
        P("row", "col"),
        P("row", "col"),
        P("col", "row"),
        P(("dp", "col"), "row", None, None),
    )
    return jax.shard_map(
        functools.partial(local, sizes),
        mesh=mesh,
        in_specs=placed,
        out_specs=(
            P(("dp", "col"), "row", None, None),
            P(("dp", "col"), "row", None, None),
            P(("row", "col")),
            P(("row", "col")),
            P(None, ("row", "col")),
            P(None, ("row", "col")),
            P(None, ("row", "col")),
            P(("row", "col"), None),
            P(("row", "col"), None),
            P("row", "col"),
            P("row", "col"),
            P("col", "row"),
        ),
        check_vma=False,
    )
```

```python
import functools

import jax
import jax.numpy as jnp
import numpy as np
from jax import lax
from jax.experimental import pallas as pl
from jax.experimental.pallas import tpu as pltpu
from jax.sharding import PartitionSpec as P

HEADS = 6
DKV = 64
BUCKETS = 32
MAX_DIST = 128
EPSILON = 1e-06
HIGHEST = lax.Precision.HIGHEST
F32 = jnp.float32
BF16 = jnp.bfloat16
VMEM_LIMIT = 56 * 1024 * 1024


def bucket_table(length):
    offsets = np.arange(-(length - 1), length)
    half_count = BUCKETS // 2
    exact_count = half_count // 2
    upper_half = (offsets > 0).astype(np.int64) * half_count
    distance = np.abs(offsets)
    safe_distance = np.maximum(distance, 1)
    spread = (
        np.log(safe_distance / exact_count)
        / np.log(MAX_DIST / exact_count)
        * (half_count - exact_count)
    )
    far_bucket = np.minimum(
        exact_count + np.floor(np.maximum(spread, 0.0)).astype(np.int64), half_count - 1
    )
    return (upper_half + np.where(distance < exact_count, distance, far_bucket)).astype(np.int32)


def bucket_onehot(length):
    onehot = np.zeros((BUCKETS, 2 * length), np.float32)
    offsets = np.arange(-(length - 1), length)
    onehot[bucket_table(length), (-offsets) % (2 * length)] = 1.0
    return onehot


def dot(a, b, dims, precision=None):
    return lax.dot_general(a, b, (dims, ((), ())), precision=precision, preferred_element_type=F32)


NN = ((1,), (0,))
NT = ((1,), (1,))
TN = ((0,), (0,))


def vmem_spec():
    return pl.BlockSpec(memory_space=pltpu.VMEM)


def any_spec():
    return pl.BlockSpec(memory_space=pl.ANY)


def wide(column, width):
    return jnp.concatenate([column] * (width // column.shape[1]), axis=1)


def attention_forward_kernel(
    where_ref, x_ref, gain_one_ref, gain_two_ref, bias_ref, onehot_ref, *rest, n_row, shard
):
    units = rest[:8]
    normed_two_ref, outs, held = rest[8], rest[9:15], rest[15:21]
    weights_ref, residual_ref, normed_one_ref, qkv_ref, context_ref, probs_ref = held
    sems, out_sems = rest[21:]
    length, core, x_bit, y_bit, z_index = (where_ref[k] for k in range(5))
    inner = HEADS * DKV
    seq = x_ref.shape[1]
    stores = [pltpu.make_async_copy(held[k], outs[k], out_sems.at[k]) for k in range(6)]
    copies = []
    for unit in range(8):
        far, one, two = unit >> 2, (unit >> 1) & 1, unit & 1
        own_core = core ^ far
        x_shift = jnp.where(own_core == 0, one, two)
        y_shift = jnp.where(own_core == 0, two, one)
        matrix = (x_bit ^ x_shift) * 2 + own_core
        side = y_bit ^ y_shift
        for k in range(n_row):
            z_from = lax.rem(z_index - k + n_row, n_row)
            start = pl.multiple_of(matrix * inner + (z_from * 2 + side) * shard, 16)
            copy = pltpu.make_async_copy(
                units[unit].at[pl.ds(k * shard, shard)],
                weights_ref.at[pl.ds(start, shard)],
                sems.at[unit, k],
            )
            copy.start()
            copies.append(copy)
    x = x_ref[...].astype(F32)
    inverse = lax.rsqrt(jnp.mean(x * x, axis=0, keepdims=True) + EPSILON)
    normed = (x * inverse * wide(gain_one_ref[...], seq)).astype(BF16)
    normed_one_ref[...] = normed
    per_offset = dot(bias_ref[...], onehot_ref[...], NN, HIGHEST)
    key_valid = lax.broadcasted_iota(jnp.int32, (seq, seq), 0) < length
    for copy in copies:
        copy.wait()
    stores[0].start()
    stores[2].start()
    for m in range(3):
        qkv_ref[m] = dot(weights_ref[m * inner : (m + 1) * inner, :], normed, NN).astype(BF16)
    stores[3].start()
    for h in range(HEADS):
        rows = slice(h * DKV, (h + 1) * DKV)
        row = jnp.broadcast_to(per_offset[h : h + 1, :], (seq, 2 * seq))
        bias = pltpu.roll(row, 0, 1, stride=1, stride_axis=0)[:, :seq]
        scores = dot(qkv_ref[1, rows, :], qkv_ref[0, rows, :], TN) + bias
        scores = jnp.where(key_valid, scores, -1e30)
        weights = jnp.exp(scores - jnp.max(scores, axis=0, keepdims=True))
        probs = weights / jnp.sum(weights, axis=0, keepdims=True)
        probs_ref[h] = probs
        context_ref[rows, :] = dot(qkv_ref[2, rows, :], probs.astype(BF16), NN).astype(BF16)
    stores[5].start()
    stores[4].start()
    residual = x + dot(weights_ref[3 * inner :, :], context_ref[...], TN)
    residual_ref[...] = residual
    stores[1].start()
    inverse_two = lax.rsqrt(jnp.mean(residual * residual, axis=0, keepdims=True) + EPSILON)
    normed_two_ref[...] = (residual * inverse_two * wide(gain_two_ref[...], seq)).astype(BF16)
    for store in stores:
        store.wait()


def attention_forward(where, x, gain_one, gain_two, bias, onehot, units, n_row):
    width, seq = x.shape
    inner = HEADS * DKV
    held = (
        ((4 * inner, width), BF16),
        ((width, seq), F32),
        ((width, seq), BF16),
        ((3, inner, seq), BF16),
        ((inner, seq), BF16),
        ((HEADS, seq, seq), F32),
    )
    normed_two, weights, residual, normed_one, qkv, context, probs = pl.pallas_call(
        functools.partial(attention_forward_kernel, n_row=n_row, shard=inner // (2 * n_row)),
        out_shape=[jax.ShapeDtypeStruct((width, seq), BF16)]
        + [jax.ShapeDtypeStruct(shape, dtype) for shape, dtype in held],
        in_specs=[pl.BlockSpec(memory_space=pltpu.SMEM)] + [vmem_spec()] * 5 + [any_spec()] * 8,
        out_specs=[vmem_spec()] + [any_spec()] * 6,
        scratch_shapes=[pltpu.VMEM(shape, dtype) for shape, dtype in held]
        + [pltpu.SemaphoreType.DMA((8, n_row)), pltpu.SemaphoreType.DMA((6,))],
        compiler_params=pltpu.CompilerParams(vmem_limit_bytes=VMEM_LIMIT),
        cost_estimate=pl.CostEstimate(flops=8_000_000_000, bytes_accessed=16_000_000, transcendentals=400_000),
        name="attention_forward",
    )(where, x, gain_one, gain_two, bias, onehot, *units)
    return weights, residual, normed_one, normed_two, qkv, context, probs


def attention_backward_kernel(
    where_ref,
    x_ref,
    gain_one_ref,
    gain_two_ref,
    onehot_ref,
    out_grad_ref,
    part_a_ref,
    part_b_ref,
    part_c_ref,
    weights_ref,
    residual_ref,
    normed_one_ref,
    qkv_ref,
    context_ref,
    probs_ref,
    near_ref,
    far_ref,
    tokens_grad_ref,
    small_ref,
    grads_ref,
    *,
    n_row,
    shard,
):
    _, core, x_bit, y_bit, z_index = (where_ref[k] for k in range(5))
    inner = HEADS * DKV
    seq = x_ref.shape[1]
    width = x_ref.shape[0]
    ones = jnp.ones((8, seq), F32)

    def store_weight_grad(matrix, grad):
        grad = grad.astype(BF16)
        target_core = matrix & 1
        x_shift = (matrix >> 1) ^ x_bit
        for side in range(2):
            y_shift = side ^ y_bit
            if target_core == 0:
                unit = x_shift * 2 + y_shift
            else:
                unit = y_shift * 2 + x_shift
            for z in range(n_row):
                slot = unit * n_row + lax.rem(z - z_index + n_row, n_row)
                start = (z * 2 + side) * shard
                block = grad[start : start + shard, :]

                @pl.when(core == target_core)
                def _():
                    near_ref[slot] = block

                @pl.when(core != target_core)
                def _():
                    far_ref[slot] = block

    residual = residual_ref[...]
    grad_normed = (
        part_a_ref[...].astype(F32) + part_b_ref[...].astype(F32) + part_c_ref[...].astype(F32)
    )
    inverse_two = lax.rsqrt(jnp.mean(residual * residual, axis=0, keepdims=True) + EPSILON)
    gained = grad_normed * wide(gain_two_ref[...], seq)
    ffn_gain_grad = dot(ones, grad_normed * residual * inverse_two, NT, HIGHEST)
    grad_residual = (
        out_grad_ref[...].astype(F32)
        + inverse_two * gained
        - residual
        * (inverse_two * inverse_two * inverse_two * jnp.mean(gained * residual, axis=0, keepdims=True))
    )
    grad_attended = grad_residual.astype(BF16)
    store_weight_grad(3, dot(context_ref[...], grad_attended, NT))
    grad_context = dot(weights_ref[3 * inner :, :], grad_attended, NN).astype(BF16)
    flip = (
        lax.broadcasted_iota(jnp.int32, (seq, seq), 0)
        + lax.broadcasted_iota(jnp.int32, (seq, seq), 1)
        == seq - 1
    ).astype(BF16)
    zero_half = jnp.zeros((seq, seq), F32)
    diagonals = []
    for h in range(HEADS):
        rows = slice(h * DKV, (h + 1) * DKV)
        probs = probs_ref[h]
        grad_head = grad_context[rows, :]
        grads_ref[2, rows, :] = dot(grad_head, probs.astype(BF16), NT).astype(BF16)
        grad_probs = dot(qkv_ref[2, rows, :], grad_head, TN)
        grad_scores = (
            probs * (grad_probs - jnp.sum(probs * grad_probs, axis=0, keepdims=True))
        ).astype(BF16)
        grads_ref[0, rows, :] = dot(qkv_ref[1, rows, :], grad_scores, NN).astype(BF16)
        grads_ref[1, rows, :] = dot(qkv_ref[0, rows, :], grad_scores, NT).astype(BF16)
        flipped = jnp.concatenate((dot(flip, grad_scores, NN), zero_half), axis=1)
        rolled = pltpu.roll(flipped, seq + 1, 1, stride=1, stride_axis=0)
        diagonals.append(jnp.sum(rolled, axis=0, keepdims=True))
    diagonals.append(jnp.zeros((8 - HEADS, 2 * seq), F32))
    table = dot(jnp.concatenate(diagonals, axis=0), onehot_ref[...], NT, HIGHEST)
    normed_one = normed_one_ref[...]
    grad_normed_one = None
    for m in range(3):
        store_weight_grad(m, dot(grads_ref[m], normed_one, NT))
        part = dot(weights_ref[m * inner : (m + 1) * inner, :], grads_ref[m], TN)
        grad_normed_one = part if grad_normed_one is None else grad_normed_one + part
    x = x_ref[...].astype(F32)
    inverse_one = lax.rsqrt(jnp.mean(x * x, axis=0, keepdims=True) + EPSILON)
    gained_one = grad_normed_one * wide(gain_one_ref[...], seq)
    attn_gain_grad = dot(ones, grad_normed_one * x * inverse_one, NT, HIGHEST)
    tokens_grad_ref[...] = (
        grad_residual
        + inverse_one * gained_one
        - x * (inverse_one * inverse_one * inverse_one * jnp.mean(gained_one * x, axis=0, keepdims=True))
    ).astype(BF16)
    small_ref[0:8, :] = jnp.where(
        lax.broadcasted_iota(jnp.int32, (8, width), 0) == 0, attn_gain_grad, ffn_gain_grad
    )
    small_ref[8:16, :] = jnp.concatenate((table, jnp.zeros((8, width - BUCKETS), F32)), axis=1)


def attention_backward(where, x, gain_one, gain_two, onehot, out_grad, parts, saved, n_row):
    width, seq = x.shape
    inner = HEADS * DKV
    shard = inner // (2 * n_row)
    return pl.pallas_call(
        functools.partial(attention_backward_kernel, n_row=n_row, shard=shard),
        out_shape=(
            jax.ShapeDtypeStruct((4 * n_row, shard, width), BF16),
            jax.ShapeDtypeStruct((4 * n_row, shard, width), BF16),
            jax.ShapeDtypeStruct((width, seq), BF16),
            jax.ShapeDtypeStruct((16, width), F32),
        ),
        in_specs=[pl.BlockSpec(memory_space=pltpu.SMEM)] + [vmem_spec()] * 14,
        out_specs=(vmem_spec(),) * 4,
        scratch_shapes=[pltpu.VMEM((3, inner, seq), BF16)],
        compiler_params=pltpu.CompilerParams(vmem_limit_bytes=VMEM_LIMIT),
        cost_estimate=pl.CostEstimate(flops=12_000_000_000, bytes_accessed=20_000_000, transcendentals=1000),
        name="attention_backward",
    )(where, x, gain_one, gain_two, onehot, out_grad, *parts, *saved)


GELU_SCALE = float(np.sqrt(2.0 / np.pi))


def feed_forward_kernel(*refs, count, hidden):
    normed_refs, grad_refs = refs[:count], refs[count : 2 * count]
    weights_ref, gated_ref, hidden_ref = refs[2 * count : 2 * count + 3]
    back_refs = refs[2 * count + 3 : 3 * count + 3]
    weights, turned, normed, grads, gated, grads_in, back, weight_sem, in_sems, out_sems, back_sems = refs[
        3 * count + 3 :
    ]
    rows = normed_refs[0].shape[1]
    pairs = count // 2

    def fetch(pair):
        slot = pair % 2
        copies = []
        for k, (sources, target) in enumerate(((normed_refs, normed), (grad_refs, grads))):
            for i in range(2):
                copy = pltpu.make_async_copy(
                    sources[2 * pair + i],
                    target.at[slot, :, pl.ds(i * rows, rows)],
                    in_sems.at[k, 2 * pair + i],
                )
                copy.start()
                copies.append(copy)
        return copies

    load = pltpu.make_async_copy(weights_ref, weights, weight_sem)
    load.start()
    load.wait()
    coming = fetch(0)
    turned[...] = weights[...].T
    stores = []
    for pair in range(pairs):
        slot = pair % 2
        for copy in coming:
            copy.wait()
        if pair + 1 < pairs:
            coming = fetch(pair + 1)
        both = dot(turned[: 2 * hidden], normed[slot], NN)
        gate, up = both[:hidden], both[hidden:]
        grad_gated = dot(turned[2 * hidden : 3 * hidden], grads[slot], NN)
        square = gate * gate
        tanh = jnp.tanh(GELU_SCALE * gate * (1.0 + 0.044715 * square))
        half = 0.5 * (1.0 + tanh)
        gelu = gate * half
        slope = half + (0.5 * GELU_SCALE) * gate * (1.0 - tanh * tanh) * (1.0 + 3 * 0.044715 * square)
        gated[pair] = (gelu * up).astype(BF16)
        grads_in[pair, :hidden] = (grad_gated * up * slope).astype(BF16)
        grads_in[pair, hidden:] = (grad_gated * gelu).astype(BF16)
        back[pair] = dot(weights[:, : 2 * hidden], grads_in[pair], NN).astype(BF16)
        tokens = pl.ds(pair * 2 * rows, 2 * rows)
        made = [
            pltpu.make_async_copy(gated.at[pair], gated_ref.at[:, tokens], out_sems.at[0, pair]),
            pltpu.make_async_copy(grads_in.at[pair], hidden_ref.at[:, tokens], out_sems.at[1, pair]),
        ]
        for i in range(2):
            made.append(
                pltpu.make_async_copy(
                    back.at[pair, :, pl.ds(i * rows, rows)],
                    back_refs[2 * pair + i],
                    back_sems.at[2 * pair + i],
                )
            )
        for copy in made:
            copy.start()
        stores += made
    for copy in stores:
        copy.wait()


def feed_forward(normed, grads, weights, hidden):
    count = len(normed)
    width, rows = normed[0].shape
    tokens, pairs, lanes = count * rows, count // 2, weights.shape[1]
    outs = pl.pallas_call(
        functools.partial(feed_forward_kernel, count=count, hidden=hidden),
        out_shape=[
            jax.ShapeDtypeStruct((hidden, tokens), BF16),
            jax.ShapeDtypeStruct((2 * hidden, tokens), BF16),
        ]
        + [jax.ShapeDtypeStruct((width, rows), BF16)] * count,
        in_specs=[any_spec()] * (2 * count + 1),
        out_specs=[any_spec()] * (count + 2),
        scratch_shapes=[
            pltpu.VMEM((width, lanes), BF16),
            pltpu.VMEM((lanes, width), BF16),
            pltpu.VMEM((2, width, 2 * rows), BF16),
            pltpu.VMEM((2, width, 2 * rows), BF16),
            pltpu.VMEM((pairs, hidden, 2 * rows), BF16),
            pltpu.VMEM((pairs, 2 * hidden, 2 * rows), BF16),
            pltpu.VMEM((pairs, width, 2 * rows), BF16),
            pltpu.SemaphoreType.DMA(()),
            pltpu.SemaphoreType.DMA((2, count)),
            pltpu.SemaphoreType.DMA((2, pairs)),
            pltpu.SemaphoreType.DMA((count,)),
        ],
        compiler_params=pltpu.CompilerParams(vmem_limit_bytes=VMEM_LIMIT),
        cost_estimate=pl.CostEstimate(
            flops=16 * tokens * width * hidden,
            bytes_accessed=2 * (3 * width * hidden + tokens * (3 * width + 3 * hidden)),
            transcendentals=tokens * hidden,
        ),
        name="feed_forward",
    )(*normed, *grads, weights)
    return outs[0], outs[1], outs[2:]


def weight_grads_kernel(*refs, count):
    normed, grads = refs[:count], refs[count : 2 * count]
    gated_ref, hidden_ref, weights_ref, out_ref = refs[2 * count : 2 * count + 4]
    branch = refs[2 * count + 4 : 3 * count + 4]
    normed_all, grads_all, gated_all, hidden_all, weights, sums, sent = refs[3 * count + 4 : 3 * count + 11]
    in_sems, whole_sems, sum_sems, sent_sems = refs[3 * count + 11 :]
    rows = normed[0].shape[1]
    hidden = gated_ref.shape[0]
    tail = out_ref.shape[1] - 2 * hidden

    def start(source, target, sem):
        copy = pltpu.make_async_copy(source, target, sem)
        copy.start()
        return copy

    def load(k, sources, target):
        return [
            start(sources[b], target.at[:, pl.ds(b * rows, rows)], in_sems.at[k, b])
            for b in range(count)
        ]

    def wait(copies):
        for copy in copies:
            copy.wait()

    wait(
        [
            start(gated_ref, gated_all, whole_sems.at[1]),
            start(weights_ref.at[:, pl.ds(2 * hidden, tail)], weights, whole_sems.at[2]),
        ]
    )
    first = [start(hidden_ref, hidden_all, whole_sems.at[0])] + load(0, normed, normed_all)
    for pair in range(count // 2):
        at = slice(2 * pair * rows, 2 * (pair + 1) * rows)
        sent[pair] = dot(weights[:, :hidden], gated_all[:, at], NN).astype(BF16)
    wait(first)
    later = load(1, grads, grads_all)
    stores = [
        start(sent.at[b // 2, :, pl.ds(b % 2 * rows, rows)], branch[b], sent_sems.at[b])
        for b in range(count)
    ]
    sums[:, : 2 * hidden] = dot(normed_all[...], hidden_all[...], NT).astype(BF16)
    stores.append(
        start(sums.at[:, pl.ds(0, 2 * hidden)], out_ref.at[:, pl.ds(0, 2 * hidden)], sum_sems.at[0])
    )
    wait(later)
    sums[:, 2 * hidden : 3 * hidden] = dot(grads_all[...], gated_all[...], NT).astype(BF16)
    sums[:, 3 * hidden :] = jnp.zeros((sums.shape[0], tail - hidden), BF16)
    stores.append(
        start(sums.at[:, pl.ds(2 * hidden, tail)], out_ref.at[:, pl.ds(2 * hidden, tail)], sum_sems.at[1])
    )
    wait(stores)


def weight_grads(normed, grads, gated, hidden_grads, weights):
    count = len(grads)
    width, rows = grads[0].shape
    hidden, tokens = gated.shape
    lanes = weights.shape[1]
    outs = pl.pallas_call(
        functools.partial(weight_grads_kernel, count=count),
        out_shape=[jax.ShapeDtypeStruct((width, lanes), BF16)]
        + [jax.ShapeDtypeStruct((width, rows), BF16)] * count,
        in_specs=[any_spec()] * (2 * count + 3),
        out_specs=[any_spec()] * (count + 1),
        scratch_shapes=[
            pltpu.VMEM((width, tokens), BF16),
            pltpu.VMEM((width, tokens), BF16),
            pltpu.VMEM((hidden, tokens), BF16),
            pltpu.VMEM((2 * hidden, tokens), BF16),
            pltpu.VMEM((width, lanes - 2 * hidden), BF16),
            pltpu.VMEM((width, lanes), BF16),
            pltpu.VMEM((count // 2, width, 2 * rows), BF16),
            pltpu.SemaphoreType.DMA((2, count)),
            pltpu.SemaphoreType.DMA((3,)),
            pltpu.SemaphoreType.DMA((2,)),
            pltpu.SemaphoreType.DMA((count,)),
        ],
        compiler_params=pltpu.CompilerParams(vmem_limit_bytes=VMEM_LIMIT),
        cost_estimate=pl.CostEstimate(
            flops=14 * tokens * width * hidden,
            bytes_accessed=2 * (6 * width * hidden + 3 * tokens * (width + hidden)),
            transcendentals=0,
        ),
        name="weight_grads",
    )(*normed, *grads, gated, hidden_grads, weights)
    return outs[0], outs[1:]


def join_pair_kernel(where_ref, near_ref, far_ref, *refs, other):
    outs, joined, sems = refs[-5:-2], refs[-2], refs[-1]
    own_first = where_ref[1] == 0
    half = where_ref[2] if not other else 1 - where_ref[2]
    cols = outs[0].shape[1] // 4
    at = pl.ds(pl.multiple_of(half * (2 * cols), 128), 2 * cols)
    stores = []
    for m in range(3):
        lanes = slice(m * cols, (m + 1) * cols)
        near, far = near_ref[:, lanes].astype(F32), far_ref[:, lanes].astype(F32)
        joined[m] = jnp.concatenate(
            (jnp.where(own_first, near, far), jnp.where(own_first, far, near)), axis=1
        )
        store = pltpu.make_async_copy(joined.at[m], outs[m].at[:, at], sems.at[m])
        store.start()
        stores.append(store)
    for store in stores:
        store.wait()


def join_pair(where, near, far, cols, held=None):
    rows = near.shape[0]
    held = () if held is None else tuple(held)
    return pl.pallas_call(
        functools.partial(join_pair_kernel, other=len(held) > 0),
        out_shape=[jax.ShapeDtypeStruct((rows, 4 * cols), F32)] * 3,
        in_specs=[pl.BlockSpec(memory_space=pltpu.SMEM)] + [vmem_spec()] * 2 + [any_spec()] * len(held),
        out_specs=[any_spec()] * 3,
        scratch_shapes=[pltpu.VMEM((3, rows, 2 * cols), F32), pltpu.SemaphoreType.DMA((3,))],
        input_output_aliases={3 + m: m for m in range(len(held))},
        compiler_params=pltpu.CompilerParams(vmem_limit_bytes=VMEM_LIMIT),
        cost_estimate=pl.CostEstimate(flops=0, bytes_accessed=6 * rows * cols * 6, transcendentals=0),
        name="join_pair",
    )(where, near, far, *held)


def local(
    sizes,
    tokens,
    lengths,
    attn_gain,
    ffn_gain,
    w_query,
    w_key,
    w_value,
    w_attn_out,
    rel_bias,
    w_gate,
    w_up,
    w_down,
    out_grad,
):
    n_dp, n_row, n_col = sizes
    lo = n_col // 2
    one_group = n_dp == 4 and n_col == 2
    seq, width = tokens.shape[2], tokens.shape[3]
    inner = HEADS * DKV
    dp, row, col = lax.axis_index("dp"), lax.axis_index("row"), lax.axis_index("col")
    core, x_bit, y_bit, quarter = dp % 2, (dp // 2) % 2, col // lo, dp % 4

    first, second = [], []
    for d in range(n_dp):
        for c in range(n_col):
            here, over_x, over_y = d * n_col + c, (d ^ 2) * n_col + c, d * n_col + (c + lo) % n_col
            first.append((here, over_x if d % 2 == 0 else over_y))
            second.append((here, over_y if d % 2 == 0 else over_x))
    swap = [(d, d ^ 1) for d in range(n_dp)]

    def send_first(a):
        return lax.ppermute(a, ("dp", "col"), first)

    def send_second(a):
        return lax.ppermute(a, ("dp", "col"), second)

    def send_core(a):
        return lax.ppermute(a, "dp", swap)

    def send_row(a, k):
        return lax.ppermute(a, "row", [(i, (i + k) % n_row) for i in range(n_row)])

    def after(a, *others):
        return lax.optimization_barrier((a, *others))[0]

    def add(a, b):
        return (a.astype(F32) + b.astype(F32)).astype(BF16)

    def whole_cols(a, axis):
        return lax.all_gather(a, "col", axis=axis, tiled=True) if lo > 1 else a

    x = jnp.transpose(tokens.reshape(seq, width))
    grad = jnp.transpose(out_grad.reshape(seq, width))
    onehot = jnp.asarray(bucket_onehot(seq))
    where = jnp.stack((lengths.reshape(()), core, x_bit, y_bit, row)).astype(jnp.int32)
    gain_one = jnp.broadcast_to(attn_gain.reshape(width, 1), (width, 128))
    gain_two = jnp.broadcast_to(ffn_gain.reshape(width, 1), (width, 128))
    bias = jnp.pad(jnp.transpose(rel_bias), ((0, 8 - HEADS), (0, 0)))

    shard = inner // (2 * n_row)
    proj = jnp.where(quarter == 0, w_query, jnp.where(quarter == 1, w_key, w_value))
    own = jnp.where(quarter == 3, w_attn_out, jnp.transpose(proj))
    if lo > 1:
        own = lax.dynamic_slice_in_dim(whole_cols(own, 0), y_bit * shard, shard, 0)
    others = [send_row(own, k) for k in range(1, n_row)]
    unit = jnp.concatenate([own] + others, axis=0)
    grad_two = send_first(grad)
    unit = after(unit, grad_two)
    unit_two, unit_one = send_first(unit), send_second(unit)
    unit_three = send_second(after(unit_two, gain_one, gain_two))
    grad_one = send_second(after(grad, unit_three))
    near_units = [unit, unit_one, unit_two, unit_three]
    units = near_units + [send_core(u) for u in near_units]
    grad_three = send_second(after(grad_two, unit_three))
    near_grads = [grad, grad_one, grad_two, grad_three]
    grads = near_grads + [send_core(g) for g in near_grads]

    hidden = w_gate.shape[1] * lo // 4
    start = quarter * hidden + (y_bit * 4 * hidden if lo > 1 else 0)
    ffn_own = jnp.concatenate(
        (
            lax.dynamic_slice_in_dim(whole_cols(w_gate, 1), start, hidden, 1),
            lax.dynamic_slice_in_dim(whole_cols(w_up, 1), start, hidden, 1),
            jnp.transpose(lax.dynamic_slice_in_dim(whole_cols(w_down, 0), start, hidden, 0)),
            jnp.zeros((w_gate.shape[0], -3 * hidden % 128), BF16),
        ),
        axis=1,
    )
    ffn_weights = lax.all_gather(after(ffn_own, unit), "row", axis=0, tiled=True)

    weights, residual, normed_one, normed_two, qkv, context, probs = attention_forward(
        where, x, gain_one, gain_two, bias, onehot, units, n_row
    )
    normed_two = after(normed_two, grad_one)
    two, one = send_first(normed_two), send_second(normed_two)
    three = send_second(after(two, one))
    near_normed = [normed_two, one, two, three]
    normed = near_normed + [send_core(a) for a in near_normed]

    gated, hidden_grads, back = feed_forward(normed, grads, ffn_weights, hidden)

    near = {p: add(back[p], send_core(back[4 + p])) for p in (3, 1, 2, 0)}
    from_three, from_one = send_second(near[3]), send_second(near[1])
    ffn_grads, branch = weight_grads(
        normed, grads, gated, hidden_grads, after(ffn_weights, near[3], near[1])
    )
    near[2] = add(after(near[2], branch[0], from_one), from_three)
    from_two = send_first(near[2])
    back_parts = near[0], from_one, from_two
    ffn_grads = lax.psum_scatter(ffn_grads, "row", scatter_dimension=0, tiled=True)

    near = {p: add(branch[p], send_core(branch[4 + p])) for p in (3, 1, 2, 0)}
    branch_one = send_second(after(near[1], *back_parts))
    branch_three = send_second(after(near[3], near[2], near[0], *back_parts))

    near_grads, far_grads, tokens_grad, small = attention_backward(
        where,
        x,
        gain_one,
        gain_two,
        onehot,
        grad,
        back_parts,
        (weights, residual, normed_one, qkv, context, probs),
        n_row,
    )
    summed = add(near_grads, send_core(after(far_grads, branch_one, branch_three)))
    quad = [summed[p * n_row : (p + 1) * n_row] for p in range(4)]
    from_one = send_second(quad[1])
    from_three = send_second(quad[3])
    branch_two = send_first(add(near[2], branch_three))
    from_two = send_first(add(after(quad[2], branch_two), from_three))
    mine = (quad[0].astype(F32) + from_one.astype(F32) + from_two.astype(F32)).astype(BF16)
    ffn_grads = after(ffn_grads, mine)
    mine = after(mine, ffn_grads)
    layer_out = (
        residual + near[0].astype(F32) + branch_one.astype(F32) + branch_two.astype(F32)
    ).astype(BF16)
    if one_group:
        small = small + send_core(small)
        small = small + send_first(small)
        small = small + send_second(small)
        extra = small.astype(BF16)
    else:
        small = lax.psum(small, ("dp", "row", "col"))
        extra = jnp.zeros(small.shape, BF16)
    got = [
        send_row(jnp.concatenate((mine[k], extra), axis=0), k).astype(F32) for k in range(1, n_row)
    ]
    attn_grad = mine[0].astype(F32) + sum(a[:shard] for a in got)
    attn_grad = after(attn_grad.astype(BF16), layer_out)
    small = small + sum(a[shard:] for a in got)
    def quarters(a):
        two = lax.ppermute(a, "dp", [(d, d ^ 2) for d in range(n_dp)])
        return [a, send_core(a), two, send_core(two)]

    def gather_quarters(a):
        placed = lax.dynamic_update_index_in_dim(jnp.zeros((4, *a.shape), a.dtype), a, quarter, 0)
        return lax.psum(placed, "dp")

    def own_cols(a):
        placed = jnp.zeros((n_col, *a.shape[1:]), a.dtype)
        placed = lax.dynamic_update_slice_in_dim(placed, a, y_bit * lo, 0)
        return lax.psum_scatter(placed, "col", scatter_dimension=0, tiled=False)

    if one_group:
        two = lax.ppermute(ffn_grads, "dp", [(d, d ^ 2) for d in range(n_dp)])
        half = join_pair(where, ffn_grads, send_core(ffn_grads), hidden)
        two = after(two, *half)
        gate_grad, up_grad, down_grads = join_pair(where, two, send_core(two), hidden, half)
        parts = quarters(attn_grad)
        attn_grads = []
        for m in range(4):
            picked = parts[3]
            for r in range(3):
                picked = jnp.where(quarter == m ^ r, parts[r], picked)
            attn_grads.append(picked.astype(F32))
    else:
        ffn_grads = gather_quarters(ffn_grads)[:, :, : 3 * hidden].reshape(4, width // n_row, 3, hidden)
        ffn_grads = jnp.transpose(ffn_grads, (2, 1, 0, 3)).reshape(3, width // n_row, lo, 4 * hidden // lo)
        ffn_grads = own_cols(jnp.transpose(ffn_grads, (2, 0, 1, 3))).astype(F32)
        gate_grad, up_grad, down_grads = ffn_grads[0], ffn_grads[1], ffn_grads[2]
        attn_grads = gather_quarters(attn_grad).reshape(4, lo, shard // lo, width)
        attn_grads = own_cols(jnp.transpose(attn_grads, (1, 0, 2, 3)))
    attn_grads = [attn_grads[m].astype(F32) for m in range(4)]

    place = row * n_col + col
    gain_cols, table_rows = width // (n_row * n_col), BUCKETS // (n_row * n_col)
    gain_grads = lax.dynamic_slice_in_dim(small[:2], place * gain_cols, gain_cols, 1)
    table_grad = jnp.transpose(small[8 : 8 + HEADS, :BUCKETS])
    table_grad = lax.dynamic_slice_in_dim(table_grad, place * table_rows, table_rows, 0)
    return (
        jnp.transpose(layer_out).reshape(tokens.shape),
        jnp.transpose(tokens_grad).reshape(tokens.shape),
        gain_grads[0],
        gain_grads[1],
        jnp.transpose(attn_grads[0]),
        jnp.transpose(attn_grads[1]),
        jnp.transpose(attn_grads[2]),
        attn_grads[3],
        table_grad,
        gate_grad,
        up_grad,
        jnp.transpose(down_grads),
    )


def solution(mesh):
    sizes = tuple(mesh.shape[name] for name in ("dp", "row", "col"))
    placed = (
        P(("dp", "col"), "row", None, None),
        P(("dp", "col"), "row"),
        P(),
        P(),
        P(None, ("row", "col")),
        P(None, ("row", "col")),
        P(None, ("row", "col")),
        P(("row", "col"), None),
        P(),
        P("row", "col"),
        P("row", "col"),
        P("col", "row"),
        P(("dp", "col"), "row", None, None),
    )
    return jax.shard_map(
        functools.partial(local, sizes),
        mesh=mesh,
        in_specs=placed,
        out_specs=(
            P(("dp", "col"), "row", None, None),
            P(("dp", "col"), "row", None, None),
            P(("row", "col")),
            P(("row", "col")),
            P(None, ("row", "col")),
            P(None, ("row", "col")),
            P(None, ("row", "col")),
            P(("row", "col"), None),
            P(("row", "col"), None),
            P("row", "col"),
            P("row", "col"),
            P("col", "row"),
        ),
        check_vma=False,
    )
```

```python
import functools

import jax
import jax.numpy as jnp
import numpy as np
from jax import lax
from jax.experimental import pallas as pl
from jax.experimental.pallas import tpu as pltpu
from jax.sharding import PartitionSpec as P

HEADS = 6
DKV = 64
BUCKETS = 32
MAX_DIST = 128
EPSILON = 1e-06
HIGHEST = lax.Precision.HIGHEST
F32 = jnp.float32
BF16 = jnp.bfloat16
VMEM_LIMIT = 56 * 1024 * 1024


def bucket_table(length):
    offsets = np.arange(-(length - 1), length)
    half_count = BUCKETS // 2
    exact_count = half_count // 2
    upper_half = (offsets > 0).astype(np.int64) * half_count
    distance = np.abs(offsets)
    safe_distance = np.maximum(distance, 1)
    spread = (
        np.log(safe_distance / exact_count)
        / np.log(MAX_DIST / exact_count)
        * (half_count - exact_count)
    )
    far_bucket = np.minimum(
        exact_count + np.floor(np.maximum(spread, 0.0)).astype(np.int64), half_count - 1
    )
    return (upper_half + np.where(distance < exact_count, distance, far_bucket)).astype(np.int32)


def bucket_onehot(length):
    onehot = np.zeros((BUCKETS, 2 * length), np.float32)
    offsets = np.arange(-(length - 1), length)
    onehot[bucket_table(length), (-offsets) % (2 * length)] = 1.0
    return onehot


def dot(a, b, dims, precision=None):
    return lax.dot_general(a, b, (dims, ((), ())), precision=precision, preferred_element_type=F32)


NN = ((1,), (0,))
NT = ((1,), (1,))
TN = ((0,), (0,))


def vmem_spec():
    return pl.BlockSpec(memory_space=pltpu.VMEM)


def any_spec():
    return pl.BlockSpec(memory_space=pl.ANY)


def wide(column, width):
    return jnp.concatenate([column] * (width // column.shape[1]), axis=1)


def attention_forward_kernel(
    where_ref, x_ref, gain_one_ref, gain_two_ref, bias_ref, onehot_ref, *rest, n_row, shard
):
    units = rest[:8]
    normed_two_ref, outs, held = rest[8], rest[9:15], rest[15:21]
    weights_ref, residual_ref, normed_one_ref, qkv_ref, context_ref, probs_ref = held
    sems, out_sems = rest[21:]
    length, core, x_bit, y_bit, z_index = (where_ref[k] for k in range(5))
    inner = HEADS * DKV
    seq = x_ref.shape[1]
    stores = [pltpu.make_async_copy(held[k], outs[k], out_sems.at[k]) for k in range(6)]
    copies = []
    for unit in range(8):
        far, one, two = unit >> 2, (unit >> 1) & 1, unit & 1
        own_core = core ^ far
        x_shift = jnp.where(own_core == 0, one, two)
        y_shift = jnp.where(own_core == 0, two, one)
        matrix = (x_bit ^ x_shift) * 2 + own_core
        side = y_bit ^ y_shift
        for k in range(n_row):
            z_from = lax.rem(z_index - k + n_row, n_row)
            start = pl.multiple_of(matrix * inner + (z_from * 2 + side) * shard, 16)
            copy = pltpu.make_async_copy(
                units[unit].at[pl.ds(k * shard, shard)],
                weights_ref.at[pl.ds(start, shard)],
                sems.at[unit, k],
            )
            copy.start()
            copies.append(copy)
    x = x_ref[...].astype(F32)
    inverse = lax.rsqrt(jnp.mean(x * x, axis=0, keepdims=True) + EPSILON)
    normed = (x * inverse * wide(gain_one_ref[...], seq)).astype(BF16)
    normed_one_ref[...] = normed
    per_offset = dot(bias_ref[...], onehot_ref[...], NN, HIGHEST)
    key_valid = lax.broadcasted_iota(jnp.int32, (seq, seq), 0) < length
    for copy in copies:
        copy.wait()
    stores[0].start()
    stores[2].start()
    for m in range(3):
        qkv_ref[m] = dot(weights_ref[m * inner : (m + 1) * inner, :], normed, NN).astype(BF16)
    stores[3].start()
    for h in range(HEADS):
        rows = slice(h * DKV, (h + 1) * DKV)
        row = jnp.broadcast_to(per_offset[h : h + 1, :], (seq, 2 * seq))
        bias = pltpu.roll(row, 0, 1, stride=1, stride_axis=0)[:, :seq]
        scores = dot(qkv_ref[1, rows, :], qkv_ref[0, rows, :], TN) + bias
        scores = jnp.where(key_valid, scores, -1e30)
        weights = jnp.exp(scores - jnp.max(scores, axis=0, keepdims=True))
        probs = weights / jnp.sum(weights, axis=0, keepdims=True)
        probs_ref[h] = probs
        context_ref[rows, :] = dot(qkv_ref[2, rows, :], probs.astype(BF16), NN).astype(BF16)
    stores[5].start()
    stores[4].start()
    residual = x + dot(weights_ref[3 * inner :, :], context_ref[...], TN)
    residual_ref[...] = residual
    stores[1].start()
    inverse_two = lax.rsqrt(jnp.mean(residual * residual, axis=0, keepdims=True) + EPSILON)
    normed_two_ref[...] = (residual * inverse_two * wide(gain_two_ref[...], seq)).astype(BF16)
    for store in stores:
        store.wait()


def attention_forward(where, x, gain_one, gain_two, bias, onehot, units, n_row):
    width, seq = x.shape
    inner = HEADS * DKV
    held = (
        ((4 * inner, width), BF16),
        ((width, seq), F32),
        ((width, seq), BF16),
        ((3, inner, seq), BF16),
        ((inner, seq), BF16),
        ((HEADS, seq, seq), F32),
    )
    normed_two, weights, residual, normed_one, qkv, context, probs = pl.pallas_call(
        functools.partial(attention_forward_kernel, n_row=n_row, shard=inner // (2 * n_row)),
        out_shape=[jax.ShapeDtypeStruct((width, seq), BF16)]
        + [jax.ShapeDtypeStruct(shape, dtype) for shape, dtype in held],
        in_specs=[pl.BlockSpec(memory_space=pltpu.SMEM)] + [vmem_spec()] * 5 + [any_spec()] * 8,
        out_specs=[vmem_spec()] + [any_spec()] * 6,
        scratch_shapes=[pltpu.VMEM(shape, dtype) for shape, dtype in held]
        + [pltpu.SemaphoreType.DMA((8, n_row)), pltpu.SemaphoreType.DMA((6,))],
        compiler_params=pltpu.CompilerParams(vmem_limit_bytes=VMEM_LIMIT),
        cost_estimate=pl.CostEstimate(flops=8_000_000_000, bytes_accessed=16_000_000, transcendentals=400_000),
        name="attention_forward",
    )(where, x, gain_one, gain_two, bias, onehot, *units)
    return weights, residual, normed_one, normed_two, qkv, context, probs


def attention_backward_kernel(
    where_ref,
    x_ref,
    gain_one_ref,
    gain_two_ref,
    onehot_ref,
    out_grad_ref,
    part_a_ref,
    part_b_ref,
    part_c_ref,
    weights_ref,
    residual_ref,
    normed_one_ref,
    qkv_ref,
    context_ref,
    probs_ref,
    near_ref,
    far_ref,
    tokens_grad_ref,
    small_ref,
    grads_ref,
    *,
    n_row,
    shard,
):
    _, core, x_bit, y_bit, z_index = (where_ref[k] for k in range(5))
    inner = HEADS * DKV
    seq = x_ref.shape[1]
    width = x_ref.shape[0]
    ones = jnp.ones((8, seq), F32)

    def store_weight_grad(matrix, grad):
        grad = grad.astype(BF16)
        target_core = matrix & 1
        x_shift = (matrix >> 1) ^ x_bit
        for side in range(2):
            y_shift = side ^ y_bit
            if target_core == 0:
                unit = x_shift * 2 + y_shift
            else:
                unit = y_shift * 2 + x_shift
            for z in range(n_row):
                slot = unit * n_row + lax.rem(z - z_index + n_row, n_row)
                start = (z * 2 + side) * shard
                block = grad[start : start + shard, :]

                @pl.when(core == target_core)
                def _():
                    near_ref[slot] = block

                @pl.when(core != target_core)
                def _():
                    far_ref[slot] = block

    residual = residual_ref[...]
    grad_normed = (
        part_a_ref[...].astype(F32) + part_b_ref[...].astype(F32) + part_c_ref[...].astype(F32)
    )
    inverse_two = lax.rsqrt(jnp.mean(residual * residual, axis=0, keepdims=True) + EPSILON)
    gained = grad_normed * wide(gain_two_ref[...], seq)
    ffn_gain_grad = dot(ones, grad_normed * residual * inverse_two, NT, HIGHEST)
    grad_residual = (
        out_grad_ref[...].astype(F32)
        + inverse_two * gained
        - residual
        * (inverse_two * inverse_two * inverse_two * jnp.mean(gained * residual, axis=0, keepdims=True))
    )
    grad_attended = grad_residual.astype(BF16)
    store_weight_grad(3, dot(context_ref[...], grad_attended, NT))
    grad_context = dot(weights_ref[3 * inner :, :], grad_attended, NN).astype(BF16)
    flip = (
        lax.broadcasted_iota(jnp.int32, (seq, seq), 0)
        + lax.broadcasted_iota(jnp.int32, (seq, seq), 1)
        == seq - 1
    ).astype(BF16)
    zero_half = jnp.zeros((seq, seq), F32)
    diagonals = []
    for h in range(HEADS):
        rows = slice(h * DKV, (h + 1) * DKV)
        probs = probs_ref[h]
        grad_head = grad_context[rows, :]
        grads_ref[2, rows, :] = dot(grad_head, probs.astype(BF16), NT).astype(BF16)
        grad_probs = dot(qkv_ref[2, rows, :], grad_head, TN)
        grad_scores = (
            probs * (grad_probs - jnp.sum(probs * grad_probs, axis=0, keepdims=True))
        ).astype(BF16)
        grads_ref[0, rows, :] = dot(qkv_ref[1, rows, :], grad_scores, NN).astype(BF16)
        grads_ref[1, rows, :] = dot(qkv_ref[0, rows, :], grad_scores, NT).astype(BF16)
        flipped = jnp.concatenate((dot(flip, grad_scores, NN), zero_half), axis=1)
        rolled = pltpu.roll(flipped, seq + 1, 1, stride=1, stride_axis=0)
        diagonals.append(jnp.sum(rolled, axis=0, keepdims=True))
    diagonals.append(jnp.zeros((8 - HEADS, 2 * seq), F32))
    table = dot(jnp.concatenate(diagonals, axis=0), onehot_ref[...], NT, HIGHEST)
    normed_one = normed_one_ref[...]
    grad_normed_one = None
    for m in range(3):
        store_weight_grad(m, dot(grads_ref[m], normed_one, NT))
        part = dot(weights_ref[m * inner : (m + 1) * inner, :], grads_ref[m], TN)
        grad_normed_one = part if grad_normed_one is None else grad_normed_one + part
    x = x_ref[...].astype(F32)
    inverse_one = lax.rsqrt(jnp.mean(x * x, axis=0, keepdims=True) + EPSILON)
    gained_one = grad_normed_one * wide(gain_one_ref[...], seq)
    attn_gain_grad = dot(ones, grad_normed_one * x * inverse_one, NT, HIGHEST)
    tokens_grad_ref[...] = (
        grad_residual
        + inverse_one * gained_one
        - x * (inverse_one * inverse_one * inverse_one * jnp.mean(gained_one * x, axis=0, keepdims=True))
    ).astype(BF16)
    small_ref[0:8, :] = jnp.where(
        lax.broadcasted_iota(jnp.int32, (8, width), 0) == 0, attn_gain_grad, ffn_gain_grad
    )
    small_ref[8:16, :] = jnp.concatenate((table, jnp.zeros((8, width - BUCKETS), F32)), axis=1)


def attention_backward(where, x, gain_one, gain_two, onehot, out_grad, parts, saved, n_row):
    width, seq = x.shape
    inner = HEADS * DKV
    shard = inner // (2 * n_row)
    return pl.pallas_call(
        functools.partial(attention_backward_kernel, n_row=n_row, shard=shard),
        out_shape=(
            jax.ShapeDtypeStruct((4 * n_row, shard, width), BF16),
            jax.ShapeDtypeStruct((4 * n_row, shard, width), BF16),
            jax.ShapeDtypeStruct((width, seq), BF16),
            jax.ShapeDtypeStruct((16, width), F32),
        ),
        in_specs=[pl.BlockSpec(memory_space=pltpu.SMEM)] + [vmem_spec()] * 14,
        out_specs=(vmem_spec(),) * 4,
        scratch_shapes=[pltpu.VMEM((3, inner, seq), BF16)],
        compiler_params=pltpu.CompilerParams(vmem_limit_bytes=VMEM_LIMIT),
        cost_estimate=pl.CostEstimate(flops=12_000_000_000, bytes_accessed=20_000_000, transcendentals=1000),
        name="attention_backward",
    )(where, x, gain_one, gain_two, onehot, out_grad, *parts, *saved)


def split_rows(rows):
    top = (rows + 31) // 32 * 16
    return top, rows - top


def packed_rows(rows, cols):
    return cols // 128 * rows + split_rows(rows)[0]


def pack(a):
    rows, cols = a.shape
    top, bottom = split_rows(rows)
    rest = a[:, cols - 64 :]
    right = jnp.pad(rest[top:], ((0, top - bottom), (0, 0)))
    tiles = [a[:, t * 128 : (t + 1) * 128] for t in range(cols // 128)]
    return jnp.concatenate(tiles + [jnp.concatenate((rest[:top], right), axis=1)], axis=0)


def unpack(a, rows):
    top, bottom = split_rows(rows)
    count = (a.shape[0] - top) // rows
    last = a[count * rows :]
    rest = jnp.concatenate((last[:, :64], last[:bottom, 64:]), axis=0)
    return jnp.concatenate([a[t * rows : (t + 1) * rows] for t in range(count)] + [rest], axis=1)


GELU_SCALE = float(np.sqrt(2.0 / np.pi))


def unpack_copies(packed, target, rest, sems, rows, first, count):
    top = split_rows(rows)[0]
    chunk = rest.shape[0]
    height = packed.shape[0] // chunk
    copies = []
    for z in range(chunk):
        for t in range(first, count):
            copies.append(
                pltpu.make_async_copy(
                    packed.at[pl.ds(z * height + t * rows, rows)],
                    target.at[pl.ds(z * rows, rows), pl.ds((t - first) * 128, 128)],
                    sems.at[z, t],
                )
            )
        copies.append(
            pltpu.make_async_copy(
                packed.at[pl.ds(z * height + count * rows, top)], rest.at[z], sems.at[z, count]
            )
        )
    return copies


def place_rest(target, rest, rows, lane):
    top, bottom = split_rows(rows)
    for z in range(rest.shape[0]):
        start = z * rows
        target[start : start + top, lane : lane + 64] = rest[z, :, :64]
        target[start + top : start + rows, lane : lane + 64] = rest[z, :bottom, 64:]


def feed_forward_kernel(*refs, count, hidden, n_row):
    normed_refs, grad_refs = refs[:count], refs[count : 2 * count]
    weights_ref, gated_ref, hidden_ref = refs[2 * count : 2 * count + 3]
    back_refs = refs[2 * count + 3 : 3 * count + 3]
    weights, turned, normed, grads, gated, grads_in, back, rest, weight_sems, in_sems, out_sems, back_sems = refs[
        3 * count + 3 :
    ]
    chunk = weights.shape[0] // n_row
    tiles = 3 * hidden // 128
    rows = normed_refs[0].shape[1]
    pairs = count // 2

    def fetch(pair):
        slot = pair % 2
        copies = []
        for k, (sources, target) in enumerate(((normed_refs, normed), (grad_refs, grads))):
            for i in range(2):
                copy = pltpu.make_async_copy(
                    sources[2 * pair + i],
                    target.at[slot, :, pl.ds(i * rows, rows)],
                    in_sems.at[k, 2 * pair + i],
                )
                copy.start()
                copies.append(copy)
        return copies

    load = unpack_copies(weights_ref, weights, rest, weight_sems, chunk, 0, tiles)
    for copy in load:
        copy.start()
    for copy in load:
        copy.wait()
    coming = fetch(0)
    place_rest(weights, rest, chunk, tiles * 128)
    turned[...] = weights[...].T
    stores = []
    for pair in range(pairs):
        slot = pair % 2
        for copy in coming:
            copy.wait()
        if pair + 1 < pairs:
            coming = fetch(pair + 1)
        both = dot(turned[: 2 * hidden], normed[slot], NN)
        gate, up = both[:hidden], both[hidden:]
        grad_gated = dot(turned[2 * hidden : 3 * hidden], grads[slot], NN)
        square = gate * gate
        tanh = jnp.tanh(GELU_SCALE * gate * (1.0 + 0.044715 * square))
        half = 0.5 * (1.0 + tanh)
        gelu = gate * half
        slope = half + (0.5 * GELU_SCALE) * gate * (1.0 - tanh * tanh) * (1.0 + 3 * 0.044715 * square)
        gated[pair] = (gelu * up).astype(BF16)
        grads_in[pair, :hidden] = (grad_gated * up * slope).astype(BF16)
        grads_in[pair, hidden:] = (grad_gated * gelu).astype(BF16)
        back[pair] = dot(weights[:, : 2 * hidden], grads_in[pair], NN).astype(BF16)
        tokens = pl.ds(pair * 2 * rows, 2 * rows)
        made = [
            pltpu.make_async_copy(gated.at[pair], gated_ref.at[:, tokens], out_sems.at[0, pair]),
            pltpu.make_async_copy(grads_in.at[pair], hidden_ref.at[:, tokens], out_sems.at[1, pair]),
        ]
        for i in range(2):
            made.append(
                pltpu.make_async_copy(
                    back.at[pair, :, pl.ds(i * rows, rows)],
                    back_refs[2 * pair + i],
                    back_sems.at[2 * pair + i],
                )
            )
        for copy in made:
            copy.start()
        stores += made
    for copy in stores:
        copy.wait()


def feed_forward(normed, grads, weights, hidden, n_row):
    count = len(normed)
    width, rows = normed[0].shape
    tokens, pairs, lanes = count * rows, count // 2, 3 * hidden
    tiles = lanes // 128
    outs = pl.pallas_call(
        functools.partial(feed_forward_kernel, count=count, hidden=hidden, n_row=n_row),
        out_shape=[
            jax.ShapeDtypeStruct((hidden, tokens), BF16),
            jax.ShapeDtypeStruct((2 * hidden, tokens), BF16),
        ]
        + [jax.ShapeDtypeStruct((width, rows), BF16)] * count,
        in_specs=[any_spec()] * (2 * count + 1),
        out_specs=[any_spec()] * (count + 2),
        scratch_shapes=[
            pltpu.VMEM((width, lanes), BF16),
            pltpu.VMEM((lanes, width), BF16),
            pltpu.VMEM((2, width, 2 * rows), BF16),
            pltpu.VMEM((2, width, 2 * rows), BF16),
            pltpu.VMEM((pairs, hidden, 2 * rows), BF16),
            pltpu.VMEM((pairs, 2 * hidden, 2 * rows), BF16),
            pltpu.VMEM((pairs, width, 2 * rows), BF16),
            pltpu.VMEM((n_row, split_rows(width // n_row)[0], 128), BF16),
            pltpu.SemaphoreType.DMA((n_row, tiles + 1)),
            pltpu.SemaphoreType.DMA((2, count)),
            pltpu.SemaphoreType.DMA((2, pairs)),
            pltpu.SemaphoreType.DMA((count,)),
        ],
        compiler_params=pltpu.CompilerParams(vmem_limit_bytes=VMEM_LIMIT),
        cost_estimate=pl.CostEstimate(
            flops=16 * tokens * width * hidden,
            bytes_accessed=2 * (3 * width * hidden + tokens * (3 * width + 3 * hidden)),
            transcendentals=tokens * hidden,
        ),
        name="feed_forward",
    )(*normed, *grads, weights)
    return outs[0], outs[1], outs[2:]


def weight_grads_kernel(*refs, count, n_row):
    normed, grads = refs[:count], refs[count : 2 * count]
    gated_ref, hidden_ref, weights_ref, out_ref = refs[2 * count : 2 * count + 4]
    branch = refs[2 * count + 4 : 3 * count + 4]
    normed_all, grads_all, gated_all, hidden_all, weights, sums, sent, rest, packed = refs[
        3 * count + 4 : 3 * count + 13
    ]
    in_sems, whole_sems, weight_sems, sum_sems, sent_sems = refs[3 * count + 13 :]
    rows = normed[0].shape[1]
    hidden = gated_ref.shape[0]
    chunk = sums.shape[0] // n_row
    tiles, first = 3 * hidden // 128, 2 * hidden // 128
    top, bottom = split_rows(chunk)
    height = out_ref.shape[0] // n_row

    def start(source, target, sem):
        copy = pltpu.make_async_copy(source, target, sem)
        copy.start()
        return copy

    def load(k, sources, target):
        return [
            start(sources[b], target.at[:, pl.ds(b * rows, rows)], in_sems.at[k, b])
            for b in range(count)
        ]

    def wait(copies):
        for copy in copies:
            copy.wait()

    def store_tiles(low, high):
        return [
            start(
                sums.at[pl.ds(z * chunk, chunk), pl.ds(t * 128, 128)],
                out_ref.at[pl.ds(z * height + t * chunk, chunk)],
                sum_sems.at[z, t],
            )
            for z in range(n_row)
            for t in range(low, high)
        ]

    loads = unpack_copies(weights_ref, weights, rest, weight_sems, chunk, first, tiles)
    for copy in loads:
        copy.start()
    wait(loads + [start(gated_ref, gated_all, whole_sems.at[1])])
    place_rest(weights, rest, chunk, (tiles - first) * 128)
    early = [start(hidden_ref, hidden_all, whole_sems.at[0])] + load(0, normed, normed_all)
    for pair in range(count // 2):
        at = slice(2 * pair * rows, 2 * (pair + 1) * rows)
        sent[pair] = dot(weights[:, :hidden], gated_all[:, at], NN).astype(BF16)
    wait(early)
    later = load(1, grads, grads_all)
    stores = [
        start(sent.at[b // 2, :, pl.ds(b % 2 * rows, rows)], branch[b], sent_sems.at[b])
        for b in range(count)
    ]
    sums[:, : 2 * hidden] = dot(normed_all[...], hidden_all[...], NT).astype(BF16)
    stores += store_tiles(0, first)
    wait(later)
    sums[:, 2 * hidden : 3 * hidden] = dot(grads_all[...], gated_all[...], NT).astype(BF16)
    lane = tiles * 128
    for z in range(n_row):
        start_row = z * chunk
        packed[z, :, :64] = sums[start_row : start_row + top, lane : lane + 64]
        packed[z, :bottom, 64:] = sums[start_row + top : start_row + chunk, lane : lane + 64]
        packed[z, bottom:, 64:] = jnp.zeros((top - bottom, 64), BF16)
        stores.append(
            start(packed.at[z], out_ref.at[pl.ds(z * height + tiles * chunk, top)], sum_sems.at[z, tiles])
        )
    stores += store_tiles(first, tiles)
    wait(stores)


def weight_grads(normed, grads, gated, hidden_grads, weights, n_row):
    count = len(grads)
    width, rows = grads[0].shape
    hidden, tokens = gated.shape
    tiles = 3 * hidden // 128
    top = split_rows(width // n_row)[0]
    outs = pl.pallas_call(
        functools.partial(weight_grads_kernel, count=count, n_row=n_row),
        out_shape=[jax.ShapeDtypeStruct(weights.shape, BF16)]
        + [jax.ShapeDtypeStruct((width, rows), BF16)] * count,
        in_specs=[any_spec()] * (2 * count + 3),
        out_specs=[any_spec()] * (count + 1),
        scratch_shapes=[
            pltpu.VMEM((width, tokens), BF16),
            pltpu.VMEM((width, tokens), BF16),
            pltpu.VMEM((hidden, tokens), BF16),
            pltpu.VMEM((2 * hidden, tokens), BF16),
            pltpu.VMEM((width, hidden), BF16),
            pltpu.VMEM((width, 3 * hidden), BF16),
            pltpu.VMEM((count // 2, width, 2 * rows), BF16),
            pltpu.VMEM((n_row, top, 128), BF16),
            pltpu.VMEM((n_row, top, 128), BF16),
            pltpu.SemaphoreType.DMA((2, count)),
            pltpu.SemaphoreType.DMA((2,)),
            pltpu.SemaphoreType.DMA((n_row, tiles + 1)),
            pltpu.SemaphoreType.DMA((n_row, tiles + 1)),
            pltpu.SemaphoreType.DMA((count,)),
        ],
        compiler_params=pltpu.CompilerParams(vmem_limit_bytes=VMEM_LIMIT),
        cost_estimate=pl.CostEstimate(
            flops=14 * tokens * width * hidden,
            bytes_accessed=2 * (6 * width * hidden + 3 * tokens * (width + hidden)),
            transcendentals=0,
        ),
        name="weight_grads",
    )(*normed, *grads, gated, hidden_grads, weights)
    return outs[0], outs[1:]


def join_pair_kernel(where_ref, near_ref, far_ref, *refs, other):
    outs, (joined, wide_near, wide_far, sems) = refs[-7:-4], refs[-4:]
    own_first = where_ref[1] == 0
    half = where_ref[2] if not other else 1 - where_ref[2]
    cols = outs[0].shape[1] // 4
    rows = outs[0].shape[0]
    top, bottom = split_rows(rows)
    tiles = 3 * cols // 128
    for source, target in ((near_ref, wide_near), (far_ref, wide_far)):
        for t in range(tiles):
            target[:, t * 128 : (t + 1) * 128] = source[t * rows : (t + 1) * rows, :]
        target[:top, tiles * 128 :] = source[tiles * rows :, :64]
        target[top:, tiles * 128 :] = source[tiles * rows : tiles * rows + bottom, 64:]
    at = pl.ds(pl.multiple_of(half * (2 * cols), 128), 2 * cols)
    stores = []
    for m in range(3):
        lanes = slice(m * cols, (m + 1) * cols)
        near, far = wide_near[:, lanes].astype(F32), wide_far[:, lanes].astype(F32)
        joined[m] = jnp.concatenate(
            (jnp.where(own_first, near, far), jnp.where(own_first, far, near)), axis=1
        )
        store = pltpu.make_async_copy(joined.at[m], outs[m].at[:, at], sems.at[m])
        store.start()
        stores.append(store)
    for store in stores:
        store.wait()


def join_pair(where, near, far, cols, rows, held=None):
    held = () if held is None else tuple(held)
    return pl.pallas_call(
        functools.partial(join_pair_kernel, other=len(held) > 0),
        out_shape=[jax.ShapeDtypeStruct((rows, 4 * cols), F32)] * 3,
        in_specs=[pl.BlockSpec(memory_space=pltpu.SMEM)] + [vmem_spec()] * 2 + [any_spec()] * len(held),
        out_specs=[any_spec()] * 3,
        scratch_shapes=[
            pltpu.VMEM((3, rows, 2 * cols), F32),
            pltpu.VMEM((rows, 3 * cols), BF16),
            pltpu.VMEM((rows, 3 * cols), BF16),
            pltpu.SemaphoreType.DMA((3,)),
        ],
        input_output_aliases={3 + m: m for m in range(len(held))},
        compiler_params=pltpu.CompilerParams(vmem_limit_bytes=VMEM_LIMIT),
        cost_estimate=pl.CostEstimate(flops=0, bytes_accessed=6 * rows * cols * 6, transcendentals=0),
        name="join_pair",
    )(where, near, far, *held)


def local(
    sizes,
    tokens,
    lengths,
    attn_gain,
    ffn_gain,
    w_query,
    w_key,
    w_value,
    w_attn_out,
    rel_bias,
    w_gate,
    w_up,
    w_down,
    out_grad,
):
    n_dp, n_row, n_col = sizes
    lo = n_col // 2
    one_group = n_dp == 4 and n_col == 2
    seq, width = tokens.shape[2], tokens.shape[3]
    inner = HEADS * DKV
    dp, row, col = lax.axis_index("dp"), lax.axis_index("row"), lax.axis_index("col")
    core, x_bit, y_bit, quarter = dp % 2, (dp // 2) % 2, col // lo, dp % 4

    first, second = [], []
    for d in range(n_dp):
        for c in range(n_col):
            here, over_x, over_y = d * n_col + c, (d ^ 2) * n_col + c, d * n_col + (c + lo) % n_col
            first.append((here, over_x if d % 2 == 0 else over_y))
            second.append((here, over_y if d % 2 == 0 else over_x))
    swap = [(d, d ^ 1) for d in range(n_dp)]

    def send_first(a):
        return lax.ppermute(a, ("dp", "col"), first)

    def send_second(a):
        return lax.ppermute(a, ("dp", "col"), second)

    def send_core(a):
        return lax.ppermute(a, "dp", swap)

    def send_row(a, k):
        return lax.ppermute(a, "row", [(i, (i + k) % n_row) for i in range(n_row)])

    def after(a, *others):
        return lax.optimization_barrier((a, *others))[0]

    def add(a, b):
        return (a.astype(F32) + b.astype(F32)).astype(BF16)

    def whole_cols(a, axis):
        return lax.all_gather(a, "col", axis=axis, tiled=True) if lo > 1 else a

    x = jnp.transpose(tokens.reshape(seq, width))
    grad = jnp.transpose(out_grad.reshape(seq, width))
    onehot = jnp.asarray(bucket_onehot(seq))
    where = jnp.stack((lengths.reshape(()), core, x_bit, y_bit, row)).astype(jnp.int32)
    gain_one = jnp.broadcast_to(attn_gain.reshape(width, 1), (width, 128))
    gain_two = jnp.broadcast_to(ffn_gain.reshape(width, 1), (width, 128))
    bias = jnp.pad(jnp.transpose(rel_bias), ((0, 8 - HEADS), (0, 0)))

    shard = inner // (2 * n_row)
    proj = jnp.where(quarter == 0, w_query, jnp.where(quarter == 1, w_key, w_value))
    own = jnp.where(quarter == 3, w_attn_out, jnp.transpose(proj))
    if lo > 1:
        own = lax.dynamic_slice_in_dim(whole_cols(own, 0), y_bit * shard, shard, 0)
    others = [send_row(own, k) for k in range(1, n_row)]
    unit = jnp.concatenate([own] + others, axis=0)
    grad_two = send_first(grad)
    unit = after(unit, grad_two)
    unit_two, unit_one = send_first(unit), send_second(unit)
    unit_three = send_second(after(unit_two, gain_one, gain_two))
    grad_one = send_second(after(grad, unit_three))
    near_units = [unit, unit_one, unit_two, unit_three]
    units = near_units + [send_core(u) for u in near_units]
    grad_three = send_second(after(grad_two, unit_three))
    near_grads = [grad, grad_one, grad_two, grad_three]
    grads = near_grads + [send_core(g) for g in near_grads]

    hidden = w_gate.shape[1] * lo // 4
    start = quarter * hidden + (y_bit * 4 * hidden if lo > 1 else 0)
    ffn_own = jnp.concatenate(
        (
            lax.dynamic_slice_in_dim(whole_cols(w_gate, 1), start, hidden, 1),
            lax.dynamic_slice_in_dim(whole_cols(w_up, 1), start, hidden, 1),
            jnp.transpose(lax.dynamic_slice_in_dim(whole_cols(w_down, 0), start, hidden, 0)),
        ),
        axis=1,
    )
    ffn_own = pack(ffn_own)
    ffn_weights = lax.all_gather(after(ffn_own, unit), "row", axis=0, tiled=True)

    weights, residual, normed_one, normed_two, qkv, context, probs = attention_forward(
        where, x, gain_one, gain_two, bias, onehot, units, n_row
    )
    normed_two = after(normed_two, grad_one)
    two, one = send_first(normed_two), send_second(normed_two)
    three = send_second(after(two, one))
    near_normed = [normed_two, one, two, three]
    normed = near_normed + [send_core(a) for a in near_normed]

    gated, hidden_grads, back = feed_forward(normed, grads, ffn_weights, hidden, n_row)

    near = {p: add(back[p], send_core(back[4 + p])) for p in (3, 1, 2, 0)}
    from_three, from_one = send_second(near[3]), send_second(near[1])
    ffn_grads, branch = weight_grads(
        normed, grads, gated, hidden_grads, after(ffn_weights, near[3], near[1]), n_row
    )
    near[2] = add(after(near[2], branch[0], from_one), from_three)
    from_two = send_first(near[2])
    back_parts = near[0], from_one, from_two
    ffn_grads = lax.psum_scatter(ffn_grads, "row", scatter_dimension=0, tiled=True)

    near = {p: add(branch[p], send_core(branch[4 + p])) for p in (3, 1, 2, 0)}
    branch_one = send_second(after(near[1], *back_parts))
    branch_three = send_second(after(near[3], near[2], near[0], *back_parts))

    near_grads, far_grads, tokens_grad, small = attention_backward(
        where,
        x,
        gain_one,
        gain_two,
        onehot,
        grad,
        back_parts,
        (weights, residual, normed_one, qkv, context, probs),
        n_row,
    )
    summed = add(near_grads, send_core(after(far_grads, branch_one, branch_three)))
    quad = [summed[p * n_row : (p + 1) * n_row] for p in range(4)]
    from_one = send_second(quad[1])
    from_three = send_second(quad[3])
    branch_two = send_first(add(near[2], branch_three))
    from_two = send_first(add(after(quad[2], branch_two), from_three))
    mine = (quad[0].astype(F32) + from_one.astype(F32) + from_two.astype(F32)).astype(BF16)
    ffn_grads = after(ffn_grads, mine)
    mine = after(mine, ffn_grads)
    layer_out = (
        residual + near[0].astype(F32) + branch_one.astype(F32) + branch_two.astype(F32)
    ).astype(BF16)
    if one_group:
        small = small + send_core(small)
        small = small + send_first(small)
        small = small + send_second(small)
        extra = small.astype(BF16)
    else:
        small = lax.psum(small, ("dp", "row", "col"))
        extra = jnp.zeros(small.shape, BF16)
    got = [
        send_row(jnp.concatenate((mine[k], extra), axis=0), k).astype(F32) for k in range(1, n_row)
    ]
    attn_grad = mine[0].astype(F32) + sum(a[:shard] for a in got)
    attn_grad = after(attn_grad.astype(BF16), layer_out)
    small = small + sum(a[shard:] for a in got)
    def quarters(a):
        two = lax.ppermute(a, "dp", [(d, d ^ 2) for d in range(n_dp)])
        return [a, send_core(a), two, send_core(two)]

    def gather_quarters(a):
        placed = lax.dynamic_update_index_in_dim(jnp.zeros((4, *a.shape), a.dtype), a, quarter, 0)
        return lax.psum(placed, "dp")

    def own_cols(a):
        placed = jnp.zeros((n_col, *a.shape[1:]), a.dtype)
        placed = lax.dynamic_update_slice_in_dim(placed, a, y_bit * lo, 0)
        return lax.psum_scatter(placed, "col", scatter_dimension=0, tiled=False)

    if one_group:
        two = lax.ppermute(ffn_grads, "dp", [(d, d ^ 2) for d in range(n_dp)])
        half = join_pair(where, ffn_grads, send_core(ffn_grads), hidden, width // n_row)
        two = after(two, *half)
        gate_grad, up_grad, down_grads = join_pair(where, two, send_core(two), hidden, width // n_row, half)
        parts = quarters(attn_grad)
        attn_grads = []
        for m in range(4):
            picked = parts[3]
            for r in range(3):
                picked = jnp.where(quarter == m ^ r, parts[r], picked)
            attn_grads.append(picked.astype(F32))
    else:
        ffn_grads = gather_quarters(ffn_grads)
        ffn_grads = jnp.stack([unpack(ffn_grads[q], width // n_row) for q in range(4)])
        ffn_grads = ffn_grads.reshape(4, width // n_row, 3, hidden)
        ffn_grads = jnp.transpose(ffn_grads, (2, 1, 0, 3)).reshape(3, width // n_row, lo, 4 * hidden // lo)
        ffn_grads = own_cols(jnp.transpose(ffn_grads, (2, 0, 1, 3))).astype(F32)
        gate_grad, up_grad, down_grads = ffn_grads[0], ffn_grads[1], ffn_grads[2]
        attn_grads = gather_quarters(attn_grad).reshape(4, lo, shard // lo, width)
        attn_grads = own_cols(jnp.transpose(attn_grads, (1, 0, 2, 3)))
    attn_grads = [attn_grads[m].astype(F32) for m in range(4)]

    place = row * n_col + col
    gain_cols, table_rows = width // (n_row * n_col), BUCKETS // (n_row * n_col)
    gain_grads = lax.dynamic_slice_in_dim(small[:2], place * gain_cols, gain_cols, 1)
    table_grad = jnp.transpose(small[8 : 8 + HEADS, :BUCKETS])
    table_grad = lax.dynamic_slice_in_dim(table_grad, place * table_rows, table_rows, 0)
    return (
        jnp.transpose(layer_out).reshape(tokens.shape),
        jnp.transpose(tokens_grad).reshape(tokens.shape),
        gain_grads[0],
        gain_grads[1],
        jnp.transpose(attn_grads[0]),
        jnp.transpose(attn_grads[1]),
        jnp.transpose(attn_grads[2]),
        attn_grads[3],
        table_grad,
        gate_grad,
        up_grad,
        jnp.transpose(down_grads),
    )


def solution(mesh):
    sizes = tuple(mesh.shape[name] for name in ("dp", "row", "col"))
    placed = (
        P(("dp", "col"), "row", None, None),
        P(("dp", "col"), "row"),
        P(),
        P(),
        P(None, ("row", "col")),
        P(None, ("row", "col")),
        P(None, ("row", "col")),
        P(("row", "col"), None),
        P(),
        P("row", "col"),
        P("row", "col"),
        P("col", "row"),
        P(("dp", "col"), "row", None, None),
    )
    return jax.shard_map(
        functools.partial(local, sizes),
        mesh=mesh,
        in_specs=placed,
        out_specs=(
            P(("dp", "col"), "row", None, None),
            P(("dp", "col"), "row", None, None),
            P(("row", "col")),
            P(("row", "col")),
            P(None, ("row", "col")),
            P(None, ("row", "col")),
            P(None, ("row", "col")),
            P(("row", "col"), None),
            P(("row", "col"), None),
            P("row", "col"),
            P("row", "col"),
            P("col", "row"),
        ),
        check_vma=False,
    )
```

```python
import functools

import jax
import jax.numpy as jnp
import numpy as np
from jax import lax
from jax.experimental import pallas as pl
from jax.experimental.pallas import tpu as pltpu
from jax.sharding import PartitionSpec as P

HEADS = 6
DKV = 64
BUCKETS = 32
MAX_DIST = 128
EPSILON = 1e-06
HIGHEST = lax.Precision.HIGHEST
F32 = jnp.float32
BF16 = jnp.bfloat16
VMEM_LIMIT = 56 * 1024 * 1024


def bucket_table(length):
    offsets = np.arange(-(length - 1), length)
    half_count = BUCKETS // 2
    exact_count = half_count // 2
    upper_half = (offsets > 0).astype(np.int64) * half_count
    distance = np.abs(offsets)
    safe_distance = np.maximum(distance, 1)
    spread = (
        np.log(safe_distance / exact_count)
        / np.log(MAX_DIST / exact_count)
        * (half_count - exact_count)
    )
    far_bucket = np.minimum(
        exact_count + np.floor(np.maximum(spread, 0.0)).astype(np.int64), half_count - 1
    )
    return (upper_half + np.where(distance < exact_count, distance, far_bucket)).astype(np.int32)


def bucket_onehot(length):
    onehot = np.zeros((BUCKETS, 2 * length), np.float32)
    offsets = np.arange(-(length - 1), length)
    onehot[bucket_table(length), (-offsets) % (2 * length)] = 1.0
    return onehot


def dot(a, b, dims, precision=None):
    return lax.dot_general(a, b, (dims, ((), ())), precision=precision, preferred_element_type=F32)


NN = ((1,), (0,))
NT = ((1,), (1,))
TN = ((0,), (0,))


def vmem_spec():
    return pl.BlockSpec(memory_space=pltpu.VMEM)


def any_spec():
    return pl.BlockSpec(memory_space=pl.ANY)


def wide(column, width):
    return jnp.concatenate([column] * (width // column.shape[1]), axis=1)


def attention_forward_kernel(
    where_ref, x_ref, gain_one_ref, gain_two_ref, bias_ref, onehot_ref, *rest, n_row, shard
):
    units = rest[:8]
    normed_two_ref, outs, held = rest[8], rest[9:15], rest[15:21]
    weights_ref, residual_ref, normed_one_ref, qkv_ref, context_ref, probs_ref = held
    sems, out_sems = rest[21:]
    length, core, x_bit, y_bit, z_index = (where_ref[k] for k in range(5))
    inner = HEADS * DKV
    seq = x_ref.shape[1]
    stores = [pltpu.make_async_copy(held[k], outs[k], out_sems.at[k]) for k in range(6)]
    copies = []
    for unit in range(8):
        far, one, two = unit >> 2, (unit >> 1) & 1, unit & 1
        own_core = core ^ far
        x_shift = jnp.where(own_core == 0, one, two)
        y_shift = jnp.where(own_core == 0, two, one)
        matrix = (x_bit ^ x_shift) * 2 + own_core
        side = y_bit ^ y_shift
        for k in range(n_row):
            z_from = lax.rem(z_index - k + n_row, n_row)
            start = pl.multiple_of(matrix * inner + (z_from * 2 + side) * shard, 16)
            copy = pltpu.make_async_copy(
                units[unit].at[pl.ds(k * shard, shard)],
                weights_ref.at[pl.ds(start, shard)],
                sems.at[unit, k],
            )
            copy.start()
            copies.append(copy)
    x = x_ref[...].astype(F32)
    inverse = lax.rsqrt(jnp.mean(x * x, axis=0, keepdims=True) + EPSILON)
    normed = (x * inverse * wide(gain_one_ref[...], seq)).astype(BF16)
    normed_one_ref[...] = normed
    per_offset = dot(bias_ref[...], onehot_ref[...], NN, HIGHEST)
    key_valid = lax.broadcasted_iota(jnp.int32, (seq, seq), 0) < length
    for copy in copies:
        copy.wait()
    stores[0].start()
    stores[2].start()
    for m in range(3):
        qkv_ref[m] = dot(weights_ref[m * inner : (m + 1) * inner, :], normed, NN).astype(BF16)
    stores[3].start()
    for h in range(HEADS):
        rows = slice(h * DKV, (h + 1) * DKV)
        row = jnp.broadcast_to(per_offset[h : h + 1, :], (seq, 2 * seq))
        bias = pltpu.roll(row, 0, 1, stride=1, stride_axis=0)[:, :seq]
        scores = dot(qkv_ref[1, rows, :], qkv_ref[0, rows, :], TN) + bias
        scores = jnp.where(key_valid, scores, -1e30)
        weights = jnp.exp(scores - jnp.max(scores, axis=0, keepdims=True))
        probs = weights / jnp.sum(weights, axis=0, keepdims=True)
        probs_ref[h] = probs
        context_ref[rows, :] = dot(qkv_ref[2, rows, :], probs.astype(BF16), NN).astype(BF16)
    stores[5].start()
    stores[4].start()
    residual = x + dot(weights_ref[3 * inner :, :], context_ref[...], TN)
    residual_ref[...] = residual
    stores[1].start()
    inverse_two = lax.rsqrt(jnp.mean(residual * residual, axis=0, keepdims=True) + EPSILON)
    normed_two_ref[...] = (residual * inverse_two * wide(gain_two_ref[...], seq)).astype(BF16)
    for store in stores:
        store.wait()


def attention_forward(where, x, gain_one, gain_two, bias, onehot, units, n_row):
    width, seq = x.shape
    inner = HEADS * DKV
    held = (
        ((4 * inner, width), BF16),
        ((width, seq), F32),
        ((width, seq), BF16),
        ((3, inner, seq), BF16),
        ((inner, seq), BF16),
        ((HEADS, seq, seq), F32),
    )
    normed_two, weights, residual, normed_one, qkv, context, probs = pl.pallas_call(
        functools.partial(attention_forward_kernel, n_row=n_row, shard=inner // (2 * n_row)),
        out_shape=[jax.ShapeDtypeStruct((width, seq), BF16)]
        + [jax.ShapeDtypeStruct(shape, dtype) for shape, dtype in held],
        in_specs=[pl.BlockSpec(memory_space=pltpu.SMEM)] + [vmem_spec()] * 5 + [any_spec()] * 8,
        out_specs=[vmem_spec()] + [any_spec()] * 6,
        scratch_shapes=[pltpu.VMEM(shape, dtype) for shape, dtype in held]
        + [pltpu.SemaphoreType.DMA((8, n_row)), pltpu.SemaphoreType.DMA((6,))],
        compiler_params=pltpu.CompilerParams(vmem_limit_bytes=VMEM_LIMIT),
        cost_estimate=pl.CostEstimate(flops=8_000_000_000, bytes_accessed=16_000_000, transcendentals=400_000),
        name="attention_forward",
    )(where, x, gain_one, gain_two, bias, onehot, *units)
    return weights, residual, normed_one, normed_two, qkv, context, probs


def attention_backward_kernel(
    where_ref,
    x_ref,
    gain_one_ref,
    gain_two_ref,
    onehot_ref,
    out_grad_ref,
    part_a_ref,
    part_b_ref,
    part_c_ref,
    weights_ref,
    residual_ref,
    normed_one_ref,
    qkv_ref,
    context_ref,
    probs_ref,
    near_ref,
    far_ref,
    tokens_grad_ref,
    small_ref,
    grads_ref,
    *,
    n_row,
    shard,
):
    _, core, x_bit, y_bit, z_index = (where_ref[k] for k in range(5))
    inner = HEADS * DKV
    seq = x_ref.shape[1]
    width = x_ref.shape[0]
    ones = jnp.ones((8, seq), F32)

    def store_weight_grad(matrix, grad):
        grad = grad.astype(BF16)
        target_core = matrix & 1
        x_shift = (matrix >> 1) ^ x_bit
        for side in range(2):
            y_shift = side ^ y_bit
            if target_core == 0:
                unit = x_shift * 2 + y_shift
            else:
                unit = y_shift * 2 + x_shift
            for z in range(n_row):
                slot = unit * n_row + lax.rem(z - z_index + n_row, n_row)
                start = (z * 2 + side) * shard
                block = grad[start : start + shard, :]

                @pl.when(core == target_core)
                def _():
                    near_ref[slot] = block

                @pl.when(core != target_core)
                def _():
                    far_ref[slot] = block

    residual = residual_ref[...]
    grad_normed = (
        part_a_ref[...].astype(F32) + part_b_ref[...].astype(F32) + part_c_ref[...].astype(F32)
    )
    inverse_two = lax.rsqrt(jnp.mean(residual * residual, axis=0, keepdims=True) + EPSILON)
    gained = grad_normed * wide(gain_two_ref[...], seq)
    ffn_gain_grad = dot(ones, grad_normed * residual * inverse_two, NT, HIGHEST)
    grad_residual = (
        out_grad_ref[...].astype(F32)
        + inverse_two * gained
        - residual
        * (inverse_two * inverse_two * inverse_two * jnp.mean(gained * residual, axis=0, keepdims=True))
    )
    grad_attended = grad_residual.astype(BF16)
    store_weight_grad(3, dot(context_ref[...], grad_attended, NT))
    grad_context = dot(weights_ref[3 * inner :, :], grad_attended, NN).astype(BF16)
    flip = (
        lax.broadcasted_iota(jnp.int32, (seq, seq), 0)
        + lax.broadcasted_iota(jnp.int32, (seq, seq), 1)
        == seq - 1
    ).astype(BF16)
    zero_half = jnp.zeros((seq, seq), F32)
    diagonals = []
    for h in range(HEADS):
        rows = slice(h * DKV, (h + 1) * DKV)
        probs = probs_ref[h]
        grad_head = grad_context[rows, :]
        grads_ref[2, rows, :] = dot(grad_head, probs.astype(BF16), NT).astype(BF16)
        grad_probs = dot(qkv_ref[2, rows, :], grad_head, TN)
        grad_scores = (
            probs * (grad_probs - jnp.sum(probs * grad_probs, axis=0, keepdims=True))
        ).astype(BF16)
        grads_ref[0, rows, :] = dot(qkv_ref[1, rows, :], grad_scores, NN).astype(BF16)
        grads_ref[1, rows, :] = dot(qkv_ref[0, rows, :], grad_scores, NT).astype(BF16)
        flipped = jnp.concatenate((dot(flip, grad_scores, NN), zero_half), axis=1)
        rolled = pltpu.roll(flipped, seq + 1, 1, stride=1, stride_axis=0)
        diagonals.append(jnp.sum(rolled, axis=0, keepdims=True))
    diagonals.append(jnp.zeros((8 - HEADS, 2 * seq), F32))
    table = dot(jnp.concatenate(diagonals, axis=0), onehot_ref[...], NT, HIGHEST)
    normed_one = normed_one_ref[...]
    grad_normed_one = None
    for m in range(3):
        store_weight_grad(m, dot(grads_ref[m], normed_one, NT))
        part = dot(weights_ref[m * inner : (m + 1) * inner, :], grads_ref[m], TN)
        grad_normed_one = part if grad_normed_one is None else grad_normed_one + part
    x = x_ref[...].astype(F32)
    inverse_one = lax.rsqrt(jnp.mean(x * x, axis=0, keepdims=True) + EPSILON)
    gained_one = grad_normed_one * wide(gain_one_ref[...], seq)
    attn_gain_grad = dot(ones, grad_normed_one * x * inverse_one, NT, HIGHEST)
    tokens_grad_ref[...] = (
        grad_residual
        + inverse_one * gained_one
        - x * (inverse_one * inverse_one * inverse_one * jnp.mean(gained_one * x, axis=0, keepdims=True))
    ).astype(BF16)
    small_ref[0:8, :] = jnp.where(
        lax.broadcasted_iota(jnp.int32, (8, width), 0) == 0, attn_gain_grad, ffn_gain_grad
    )
    small_ref[8:16, :] = jnp.concatenate((table, jnp.zeros((8, width - BUCKETS), F32)), axis=1)


def attention_backward(where, x, gain_one, gain_two, onehot, out_grad, parts, saved, n_row):
    width, seq = x.shape
    inner = HEADS * DKV
    shard = inner // (2 * n_row)
    return pl.pallas_call(
        functools.partial(attention_backward_kernel, n_row=n_row, shard=shard),
        out_shape=(
            jax.ShapeDtypeStruct((4 * n_row, shard, width), BF16),
            jax.ShapeDtypeStruct((4 * n_row, shard, width), BF16),
            jax.ShapeDtypeStruct((width, seq), BF16),
            jax.ShapeDtypeStruct((16, width), F32),
        ),
        in_specs=[pl.BlockSpec(memory_space=pltpu.SMEM)] + [vmem_spec()] * 14,
        out_specs=(vmem_spec(),) * 4,
        scratch_shapes=[pltpu.VMEM((3, inner, seq), BF16)],
        compiler_params=pltpu.CompilerParams(vmem_limit_bytes=VMEM_LIMIT),
        cost_estimate=pl.CostEstimate(flops=12_000_000_000, bytes_accessed=20_000_000, transcendentals=1000),
        name="attention_backward",
    )(where, x, gain_one, gain_two, onehot, out_grad, *parts, *saved)


def split_rows(rows):
    top = (rows + 31) // 32 * 16
    return top, rows - top


def packed_rows(rows, cols):
    return cols // 128 * rows + split_rows(rows)[0]


def pack_quarter_kernel(where_ref, gate_ref, up_ref, down_ref, out_ref, full):
    quarter = where_ref[2] * 2 + where_ref[1]
    rows, cols = full.shape
    hidden, tiles = cols // 3, cols // 128
    top, bottom = split_rows(rows)
    for q in range(4):

        @pl.when(quarter == q)
        def _():
            for m, ref in enumerate((gate_ref, up_ref, down_ref)):
                full[:, m * hidden : (m + 1) * hidden] = ref[:, q * hidden : (q + 1) * hidden]

    for t in range(tiles):
        out_ref[t * rows : (t + 1) * rows, :] = full[:, t * 128 : (t + 1) * 128]
    out_ref[tiles * rows :, :64] = full[:top, tiles * 128 :]
    out_ref[tiles * rows : tiles * rows + bottom, 64:] = full[top:, tiles * 128 :]
    out_ref[tiles * rows + bottom :, 64:] = jnp.zeros((top - bottom, 64), BF16)


def pack_quarter(where, gate, up, down):
    rows, cols = gate.shape
    lanes = 3 * cols // 4
    return pl.pallas_call(
        pack_quarter_kernel,
        out_shape=jax.ShapeDtypeStruct((packed_rows(rows, lanes), 128), BF16),
        in_specs=[pl.BlockSpec(memory_space=pltpu.SMEM)] + [vmem_spec()] * 3,
        out_specs=vmem_spec(),
        scratch_shapes=[pltpu.VMEM((rows, lanes), BF16)],
        compiler_params=pltpu.CompilerParams(vmem_limit_bytes=VMEM_LIMIT),
        cost_estimate=pl.CostEstimate(flops=0, bytes_accessed=2 * rows * (3 * cols + lanes), transcendentals=0),
        name="pack_quarter",
    )(where, gate, up, down)


def unpack(a, rows):
    top, bottom = split_rows(rows)
    count = (a.shape[0] - top) // rows
    last = a[count * rows :]
    rest = jnp.concatenate((last[:, :64], last[:bottom, 64:]), axis=0)
    return jnp.concatenate([a[t * rows : (t + 1) * rows] for t in range(count)] + [rest], axis=1)


GELU_SCALE = float(np.sqrt(2.0 / np.pi))


def unpack_copies(packed, target, rest, sems, rows, first, count):
    top = split_rows(rows)[0]
    chunk = rest.shape[0]
    height = packed.shape[0] // chunk
    copies = []
    for z in range(chunk):
        for t in range(first, count):
            copies.append(
                pltpu.make_async_copy(
                    packed.at[pl.ds(z * height + t * rows, rows)],
                    target.at[pl.ds(z * rows, rows), pl.ds((t - first) * 128, 128)],
                    sems.at[z, t],
                )
            )
        copies.append(
            pltpu.make_async_copy(
                packed.at[pl.ds(z * height + count * rows, top)], rest.at[z], sems.at[z, count]
            )
        )
    return copies


def place_rest(target, rest, rows, lane):
    top, bottom = split_rows(rows)
    for z in range(rest.shape[0]):
        start = z * rows
        target[start : start + top, lane : lane + 64] = rest[z, :, :64]
        target[start + top : start + rows, lane : lane + 64] = rest[z, :bottom, 64:]


def feed_forward_kernel(*refs, count, hidden, n_row):
    normed_refs, grad_refs = refs[:count], refs[count : 2 * count]
    weights_ref, gated_ref, hidden_ref = refs[2 * count : 2 * count + 3]
    back_refs = refs[2 * count + 3 : 3 * count + 3]
    weights, turned, normed, grads, gated, grads_in, back, rest, weight_sems, in_sems, out_sems, back_sems = refs[
        3 * count + 3 :
    ]
    chunk = weights.shape[0] // n_row
    tiles = 3 * hidden // 128
    rows = normed_refs[0].shape[1]
    pairs = count // 2

    def fetch(pair):
        slot = pair % 2
        copies = []
        for k, (sources, target) in enumerate(((normed_refs, normed), (grad_refs, grads))):
            for i in range(2):
                copy = pltpu.make_async_copy(
                    sources[2 * pair + i],
                    target.at[slot, :, pl.ds(i * rows, rows)],
                    in_sems.at[k, 2 * pair + i],
                )
                copy.start()
                copies.append(copy)
        return copies

    load = unpack_copies(weights_ref, weights, rest, weight_sems, chunk, 0, tiles)
    for copy in load:
        copy.start()
    for copy in load:
        copy.wait()
    coming = fetch(0)
    place_rest(weights, rest, chunk, tiles * 128)
    turned[...] = weights[...].T
    stores = []
    for pair in range(pairs):
        slot = pair % 2
        for copy in coming:
            copy.wait()
        if pair + 1 < pairs:
            coming = fetch(pair + 1)
        both = dot(turned[: 2 * hidden], normed[slot], NN)
        gate, up = both[:hidden], both[hidden:]
        grad_gated = dot(turned[2 * hidden : 3 * hidden], grads[slot], NN)
        square = gate * gate
        tanh = jnp.tanh(GELU_SCALE * gate * (1.0 + 0.044715 * square))
        half = 0.5 * (1.0 + tanh)
        gelu = gate * half
        slope = half + (0.5 * GELU_SCALE) * gate * (1.0 - tanh * tanh) * (1.0 + 3 * 0.044715 * square)
        gated[pair] = (gelu * up).astype(BF16)
        grads_in[pair, :hidden] = (grad_gated * up * slope).astype(BF16)
        grads_in[pair, hidden:] = (grad_gated * gelu).astype(BF16)
        back[pair] = dot(weights[:, : 2 * hidden], grads_in[pair], NN).astype(BF16)
        tokens = pl.ds(pair * 2 * rows, 2 * rows)
        made = [
            pltpu.make_async_copy(gated.at[pair], gated_ref.at[:, tokens], out_sems.at[0, pair]),
            pltpu.make_async_copy(grads_in.at[pair], hidden_ref.at[:, tokens], out_sems.at[1, pair]),
        ]
        for i in range(2):
            made.append(
                pltpu.make_async_copy(
                    back.at[pair, :, pl.ds(i * rows, rows)],
                    back_refs[2 * pair + i],
                    back_sems.at[2 * pair + i],
                )
            )
        for copy in made:
            copy.start()
        stores += made
    for copy in stores:
        copy.wait()


def feed_forward(normed, grads, weights, hidden, n_row):
    count = len(normed)
    width, rows = normed[0].shape
    tokens, pairs, lanes = count * rows, count // 2, 3 * hidden
    tiles = lanes // 128
    outs = pl.pallas_call(
        functools.partial(feed_forward_kernel, count=count, hidden=hidden, n_row=n_row),
        out_shape=[
            jax.ShapeDtypeStruct((hidden, tokens), BF16),
            jax.ShapeDtypeStruct((2 * hidden, tokens), BF16),
        ]
        + [jax.ShapeDtypeStruct((width, rows), BF16)] * count,
        in_specs=[any_spec()] * (2 * count + 1),
        out_specs=[any_spec()] * (count + 2),
        scratch_shapes=[
            pltpu.VMEM((width, lanes), BF16),
            pltpu.VMEM((lanes, width), BF16),
            pltpu.VMEM((2, width, 2 * rows), BF16),
            pltpu.VMEM((2, width, 2 * rows), BF16),
            pltpu.VMEM((pairs, hidden, 2 * rows), BF16),
            pltpu.VMEM((pairs, 2 * hidden, 2 * rows), BF16),
            pltpu.VMEM((pairs, width, 2 * rows), BF16),
            pltpu.VMEM((n_row, split_rows(width // n_row)[0], 128), BF16),
            pltpu.SemaphoreType.DMA((n_row, tiles + 1)),
            pltpu.SemaphoreType.DMA((2, count)),
            pltpu.SemaphoreType.DMA((2, pairs)),
            pltpu.SemaphoreType.DMA((count,)),
        ],
        compiler_params=pltpu.CompilerParams(vmem_limit_bytes=VMEM_LIMIT),
        cost_estimate=pl.CostEstimate(
            flops=16 * tokens * width * hidden,
            bytes_accessed=2 * (3 * width * hidden + tokens * (3 * width + 3 * hidden)),
            transcendentals=tokens * hidden,
        ),
        name="feed_forward",
    )(*normed, *grads, weights)
    return outs[0], outs[1], outs[2:]


def weight_grads_kernel(*refs, count, n_row):
    normed, grads = refs[:count], refs[count : 2 * count]
    gated_ref, hidden_ref, weights_ref, out_ref = refs[2 * count : 2 * count + 4]
    branch = refs[2 * count + 4 : 3 * count + 4]
    normed_all, grads_all, gated_all, hidden_all, weights, sums, sent, rest, packed = refs[
        3 * count + 4 : 3 * count + 13
    ]
    in_sems, whole_sems, weight_sems, sum_sems, sent_sems = refs[3 * count + 13 :]
    rows = normed[0].shape[1]
    hidden = gated_ref.shape[0]
    chunk = sums.shape[0] // n_row
    tiles, first = 3 * hidden // 128, 2 * hidden // 128
    top, bottom = split_rows(chunk)
    height = out_ref.shape[0] // n_row

    def start(source, target, sem):
        copy = pltpu.make_async_copy(source, target, sem)
        copy.start()
        return copy

    def load(k, sources, target):
        return [
            start(sources[b], target.at[:, pl.ds(b * rows, rows)], in_sems.at[k, b])
            for b in range(count)
        ]

    def wait(copies):
        for copy in copies:
            copy.wait()

    def store_tiles(low, high):
        return [
            start(
                sums.at[pl.ds(z * chunk, chunk), pl.ds(t * 128, 128)],
                out_ref.at[pl.ds(z * height + t * chunk, chunk)],
                sum_sems.at[z, t],
            )
            for z in range(n_row)
            for t in range(low, high)
        ]

    loads = unpack_copies(weights_ref, weights, rest, weight_sems, chunk, first, tiles)
    for copy in loads:
        copy.start()
    wait(loads + [start(gated_ref, gated_all, whole_sems.at[1])])
    place_rest(weights, rest, chunk, (tiles - first) * 128)
    early = [start(hidden_ref, hidden_all, whole_sems.at[0])] + load(0, normed, normed_all)
    for pair in range(count // 2):
        at = slice(2 * pair * rows, 2 * (pair + 1) * rows)
        sent[pair] = dot(weights[:, :hidden], gated_all[:, at], NN).astype(BF16)
    wait(early)
    later = load(1, grads, grads_all)
    stores = [
        start(sent.at[b // 2, :, pl.ds(b % 2 * rows, rows)], branch[b], sent_sems.at[b])
        for b in range(count)
    ]
    sums[:, : 2 * hidden] = dot(normed_all[...], hidden_all[...], NT).astype(BF16)
    stores += store_tiles(0, first)
    wait(later)
    sums[:, 2 * hidden : 3 * hidden] = dot(grads_all[...], gated_all[...], NT).astype(BF16)
    lane = tiles * 128
    for z in range(n_row):
        start_row = z * chunk
        packed[z, :, :64] = sums[start_row : start_row + top, lane : lane + 64]
        packed[z, :bottom, 64:] = sums[start_row + top : start_row + chunk, lane : lane + 64]
        packed[z, bottom:, 64:] = jnp.zeros((top - bottom, 64), BF16)
        stores.append(
            start(packed.at[z], out_ref.at[pl.ds(z * height + tiles * chunk, top)], sum_sems.at[z, tiles])
        )
    stores += store_tiles(first, tiles)
    wait(stores)


def weight_grads(normed, grads, gated, hidden_grads, weights, n_row):
    count = len(grads)
    width, rows = grads[0].shape
    hidden, tokens = gated.shape
    tiles = 3 * hidden // 128
    top = split_rows(width // n_row)[0]
    outs = pl.pallas_call(
        functools.partial(weight_grads_kernel, count=count, n_row=n_row),
        out_shape=[jax.ShapeDtypeStruct(weights.shape, BF16)]
        + [jax.ShapeDtypeStruct((width, rows), BF16)] * count,
        in_specs=[any_spec()] * (2 * count + 3),
        out_specs=[any_spec()] * (count + 1),
        scratch_shapes=[
            pltpu.VMEM((width, tokens), BF16),
            pltpu.VMEM((width, tokens), BF16),
            pltpu.VMEM((hidden, tokens), BF16),
            pltpu.VMEM((2 * hidden, tokens), BF16),
            pltpu.VMEM((width, hidden), BF16),
            pltpu.VMEM((width, 3 * hidden), BF16),
            pltpu.VMEM((count // 2, width, 2 * rows), BF16),
            pltpu.VMEM((n_row, top, 128), BF16),
            pltpu.VMEM((n_row, top, 128), BF16),
            pltpu.SemaphoreType.DMA((2, count)),
            pltpu.SemaphoreType.DMA((2,)),
            pltpu.SemaphoreType.DMA((n_row, tiles + 1)),
            pltpu.SemaphoreType.DMA((n_row, tiles + 1)),
            pltpu.SemaphoreType.DMA((count,)),
        ],
        compiler_params=pltpu.CompilerParams(vmem_limit_bytes=VMEM_LIMIT),
        cost_estimate=pl.CostEstimate(
            flops=14 * tokens * width * hidden,
            bytes_accessed=2 * (6 * width * hidden + 3 * tokens * (width + hidden)),
            transcendentals=0,
        ),
        name="weight_grads",
    )(*normed, *grads, gated, hidden_grads, weights)
    return outs[0], outs[1:]


def join_pair_kernel(where_ref, near_ref, far_ref, *refs, other):
    outs, (joined, wide_near, wide_far, sems) = refs[-7:-4], refs[-4:]
    own_first = where_ref[1] == 0
    half = where_ref[2] if not other else 1 - where_ref[2]
    cols = outs[0].shape[1] // 4
    rows = outs[0].shape[0]
    top, bottom = split_rows(rows)
    tiles = 3 * cols // 128
    for source, target in ((near_ref, wide_near), (far_ref, wide_far)):
        for t in range(tiles):
            target[:, t * 128 : (t + 1) * 128] = source[t * rows : (t + 1) * rows, :]
        target[:top, tiles * 128 :] = source[tiles * rows :, :64]
        target[top:, tiles * 128 :] = source[tiles * rows : tiles * rows + bottom, 64:]
    at = pl.ds(pl.multiple_of(half * (2 * cols), 128), 2 * cols)
    stores = []
    for m in range(3):
        lanes = slice(m * cols, (m + 1) * cols)
        near, far = wide_near[:, lanes].astype(F32), wide_far[:, lanes].astype(F32)
        joined[m] = jnp.concatenate(
            (jnp.where(own_first, near, far), jnp.where(own_first, far, near)), axis=1
        )
        store = pltpu.make_async_copy(joined.at[m], outs[m].at[:, at], sems.at[m])
        store.start()
        stores.append(store)
    for store in stores:
        store.wait()


def join_pair(where, near, far, cols, rows, held=None):
    held = () if held is None else tuple(held)
    return pl.pallas_call(
        functools.partial(join_pair_kernel, other=len(held) > 0),
        out_shape=[jax.ShapeDtypeStruct((rows, 4 * cols), F32)] * 3,
        in_specs=[pl.BlockSpec(memory_space=pltpu.SMEM)] + [vmem_spec()] * 2 + [any_spec()] * len(held),
        out_specs=[any_spec()] * 3,
        scratch_shapes=[
            pltpu.VMEM((3, rows, 2 * cols), F32),
            pltpu.VMEM((rows, 3 * cols), BF16),
            pltpu.VMEM((rows, 3 * cols), BF16),
            pltpu.SemaphoreType.DMA((3,)),
        ],
        input_output_aliases={3 + m: m for m in range(len(held))},
        compiler_params=pltpu.CompilerParams(vmem_limit_bytes=VMEM_LIMIT),
        cost_estimate=pl.CostEstimate(flops=0, bytes_accessed=6 * rows * cols * 6, transcendentals=0),
        name="join_pair",
    )(where, near, far, *held)


def local(
    sizes,
    tokens,
    lengths,
    attn_gain,
    ffn_gain,
    w_query,
    w_key,
    w_value,
    w_attn_out,
    rel_bias,
    w_gate,
    w_up,
    w_down,
    out_grad,
):
    n_dp, n_row, n_col = sizes
    lo = n_col // 2
    one_group = n_dp == 4 and n_col == 2
    seq, width = tokens.shape[2], tokens.shape[3]
    inner = HEADS * DKV
    dp, row, col = lax.axis_index("dp"), lax.axis_index("row"), lax.axis_index("col")
    core, x_bit, y_bit, quarter = dp % 2, (dp // 2) % 2, col // lo, dp % 4

    first, second = [], []
    for d in range(n_dp):
        for c in range(n_col):
            here, over_x, over_y = d * n_col + c, (d ^ 2) * n_col + c, d * n_col + (c + lo) % n_col
            first.append((here, over_x if d % 2 == 0 else over_y))
            second.append((here, over_y if d % 2 == 0 else over_x))
    swap = [(d, d ^ 1) for d in range(n_dp)]

    def send_first(a):
        return lax.ppermute(a, ("dp", "col"), first)

    def send_second(a):
        return lax.ppermute(a, ("dp", "col"), second)

    def send_core(a):
        return lax.ppermute(a, "dp", swap)

    def send_row(a, k):
        return lax.ppermute(a, "row", [(i, (i + k) % n_row) for i in range(n_row)])

    def after(a, *others):
        return lax.optimization_barrier((a, *others))[0]

    def add(a, b):
        return (a.astype(F32) + b.astype(F32)).astype(BF16)

    def whole_cols(a, axis):
        return lax.all_gather(a, "col", axis=axis, tiled=True) if lo > 1 else a

    x = jnp.transpose(tokens.reshape(seq, width))
    grad = jnp.transpose(out_grad.reshape(seq, width))
    onehot = jnp.asarray(bucket_onehot(seq))
    where = jnp.stack((lengths.reshape(()), core, x_bit, y_bit, row)).astype(jnp.int32)
    gain_one = jnp.broadcast_to(attn_gain.reshape(width, 1), (width, 128))
    gain_two = jnp.broadcast_to(ffn_gain.reshape(width, 1), (width, 128))
    bias = jnp.pad(jnp.transpose(rel_bias), ((0, 8 - HEADS), (0, 0)))

    shard = inner // (2 * n_row)
    proj = jnp.where(quarter == 0, w_query, jnp.where(quarter == 1, w_key, w_value))
    own = jnp.where(quarter == 3, w_attn_out, jnp.transpose(proj))
    if lo > 1:
        own = lax.dynamic_slice_in_dim(whole_cols(own, 0), y_bit * shard, shard, 0)
    others = [send_row(own, k) for k in range(1, n_row)]
    unit = jnp.concatenate([own] + others, axis=0)
    grad_two = send_first(grad)
    unit = after(unit, grad_two)
    unit_two, unit_one = send_first(unit), send_second(unit)
    unit_three = send_second(unit_two)
    grad_one = send_second(after(grad, unit_three))
    near_units = [unit, unit_one, unit_two, unit_three]
    units = near_units + [send_core(u) for u in near_units]
    grad_three = send_second(after(grad_two, unit_three))
    near_grads = [grad, grad_one, grad_two, grad_three]
    grads = near_grads + [send_core(g) for g in near_grads]

    hidden = w_gate.shape[1] * lo // 4
    ffn_shards = [whole_cols(w_gate, 1), whole_cols(w_up, 1), jnp.transpose(whole_cols(w_down, 0))]
    if lo > 1:
        half_start = y_bit * 4 * hidden
        ffn_shards = [lax.dynamic_slice_in_dim(a, half_start, 4 * hidden, 1) for a in ffn_shards]
    ffn_own = pack_quarter(after(where, gain_one, gain_two), *ffn_shards)
    ffn_weights = lax.all_gather(after(ffn_own, unit), "row", axis=0, tiled=True)

    weights, residual, normed_one, normed_two, qkv, context, probs = attention_forward(
        where, x, gain_one, gain_two, bias, onehot, units, n_row
    )
    normed_two = after(normed_two, grad_one)
    two, one = send_first(normed_two), send_second(normed_two)
    three = send_second(after(two, one))
    near_normed = [normed_two, one, two, three]
    normed = near_normed + [send_core(a) for a in near_normed]

    gated, hidden_grads, back = feed_forward(normed, grads, ffn_weights, hidden, n_row)

    near = {p: add(back[p], send_core(back[4 + p])) for p in (3, 1, 2, 0)}
    from_three, from_one = send_second(near[3]), send_second(near[1])
    ffn_grads, branch = weight_grads(
        normed, grads, gated, hidden_grads, after(ffn_weights, near[3], near[1]), n_row
    )
    near[2] = add(after(near[2], branch[0], from_one), from_three)
    from_two = send_first(near[2])
    back_parts = near[0], from_one, from_two
    ffn_grads = lax.psum_scatter(ffn_grads, "row", scatter_dimension=0, tiled=True)

    near = {p: add(branch[p], send_core(branch[4 + p])) for p in (3, 1, 2, 0)}
    branch_one = send_second(after(near[1], *back_parts))
    branch_three = send_second(after(near[3], near[2], near[0], *back_parts))

    near_grads, far_grads, tokens_grad, small = attention_backward(
        where,
        x,
        gain_one,
        gain_two,
        onehot,
        grad,
        back_parts,
        (weights, residual, normed_one, qkv, context, probs),
        n_row,
    )
    summed = add(near_grads, send_core(after(far_grads, branch_one, branch_three)))
    quad = [summed[p * n_row : (p + 1) * n_row] for p in range(4)]
    from_one = send_second(quad[1])
    from_three = send_second(quad[3])
    branch_two = send_first(add(near[2], branch_three))
    from_two = send_first(add(after(quad[2], branch_two), from_three))
    mine = (quad[0].astype(F32) + from_one.astype(F32) + from_two.astype(F32)).astype(BF16)
    ffn_grads = after(ffn_grads, mine)
    mine = after(mine, ffn_grads)
    layer_out = (
        residual + near[0].astype(F32) + branch_one.astype(F32) + branch_two.astype(F32)
    ).astype(BF16)
    if one_group:
        small = small + send_core(small)
        small = small + send_first(small)
        small = small + send_second(small)
        extra = small.astype(BF16)
    else:
        small = lax.psum(small, ("dp", "row", "col"))
        extra = jnp.zeros(small.shape, BF16)
    got = [
        send_row(jnp.concatenate((mine[k], extra), axis=0), k).astype(F32) for k in range(1, n_row)
    ]
    attn_grad = mine[0].astype(F32) + sum(a[:shard] for a in got)
    attn_grad = after(attn_grad.astype(BF16), layer_out)
    small = small + sum(a[shard:] for a in got)
    def quarters(a):
        two = lax.ppermute(a, "dp", [(d, d ^ 2) for d in range(n_dp)])
        return [a, send_core(a), two, send_core(two)]

    def gather_quarters(a):
        placed = lax.dynamic_update_index_in_dim(jnp.zeros((4, *a.shape), a.dtype), a, quarter, 0)
        return lax.psum(placed, "dp")

    def own_cols(a):
        placed = jnp.zeros((n_col, *a.shape[1:]), a.dtype)
        placed = lax.dynamic_update_slice_in_dim(placed, a, y_bit * lo, 0)
        return lax.psum_scatter(placed, "col", scatter_dimension=0, tiled=False)

    if one_group:
        two = lax.ppermute(ffn_grads, "dp", [(d, d ^ 2) for d in range(n_dp)])
        half = join_pair(where, ffn_grads, send_core(ffn_grads), hidden, width // n_row)
        two = after(two, *half)
        gate_grad, up_grad, down_grads = join_pair(where, two, send_core(two), hidden, width // n_row, half)
        parts = quarters(attn_grad)
        attn_grads = []
        for m in range(4):
            picked = parts[3]
            for r in range(3):
                picked = jnp.where(quarter == m ^ r, parts[r], picked)
            attn_grads.append(picked.astype(F32))
    else:
        ffn_grads = gather_quarters(ffn_grads)
        ffn_grads = jnp.stack([unpack(ffn_grads[q], width // n_row) for q in range(4)])
        ffn_grads = ffn_grads.reshape(4, width // n_row, 3, hidden)
        ffn_grads = jnp.transpose(ffn_grads, (2, 1, 0, 3)).reshape(3, width // n_row, lo, 4 * hidden // lo)
        ffn_grads = own_cols(jnp.transpose(ffn_grads, (2, 0, 1, 3))).astype(F32)
        gate_grad, up_grad, down_grads = ffn_grads[0], ffn_grads[1], ffn_grads[2]
        attn_grads = gather_quarters(attn_grad).reshape(4, lo, shard // lo, width)
        attn_grads = own_cols(jnp.transpose(attn_grads, (1, 0, 2, 3)))
    attn_grads = [attn_grads[m].astype(F32) for m in range(4)]

    place = row * n_col + col
    gain_cols, table_rows = width // (n_row * n_col), BUCKETS // (n_row * n_col)
    gain_grads = lax.dynamic_slice_in_dim(small[:2], place * gain_cols, gain_cols, 1)
    table_grad = jnp.transpose(small[8 : 8 + HEADS, :BUCKETS])
    table_grad = lax.dynamic_slice_in_dim(table_grad, place * table_rows, table_rows, 0)
    return (
        jnp.transpose(layer_out).reshape(tokens.shape),
        jnp.transpose(tokens_grad).reshape(tokens.shape),
        gain_grads[0],
        gain_grads[1],
        jnp.transpose(attn_grads[0]),
        jnp.transpose(attn_grads[1]),
        jnp.transpose(attn_grads[2]),
        attn_grads[3],
        table_grad,
        gate_grad,
        up_grad,
        jnp.transpose(down_grads),
    )


def solution(mesh):
    sizes = tuple(mesh.shape[name] for name in ("dp", "row", "col"))
    placed = (
        P(("dp", "col"), "row", None, None),
        P(("dp", "col"), "row"),
        P(),
        P(),
        P(None, ("row", "col")),
        P(None, ("row", "col")),
        P(None, ("row", "col")),
        P(("row", "col"), None),
        P(),
        P("row", "col"),
        P("row", "col"),
        P("col", "row"),
        P(("dp", "col"), "row", None, None),
    )
    return jax.shard_map(
        functools.partial(local, sizes),
        mesh=mesh,
        in_specs=placed,
        out_specs=(
            P(("dp", "col"), "row", None, None),
            P(("dp", "col"), "row", None, None),
            P(("row", "col")),
            P(("row", "col")),
            P(None, ("row", "col")),
            P(None, ("row", "col")),
            P(None, ("row", "col")),
            P(("row", "col"), None),
            P(("row", "col"), None),
            P("row", "col"),
            P("row", "col"),
            P("col", "row"),
        ),
        check_vma=False,
    )
```
